256 devices in a mesh: lat: 32 (over y_hi, z, core), seg: 8 (over y_lo, x).
Axes of the slice: x: 4, y: 4 (y_hi: 2, y_lo: 2; y = y_hi * 2 + y_lo), z: 8, core: 2. Of those that a mesh axis runs over, the one named last changes fastest.
Arguments:
- atmosphere: float32 [384, 96, 768], P('lat', 'seg'), may hold values from -6 to 6
- cloud_state: float32 [32, 96, 49152], P('lat', None, 'seg'), may hold values from -6 to 6
- channel_lat: int32 [32], P('lat'), may hold values from 0 to 383, as said below
- cell_column: int32 [32, 49152], P('lat', 'seg'), may hold values from 0 to 95, as said below
- channel_wind: float32 [32, 96], P('lat'), may hold values from -0.45 to 0.45
- diffusivity: float32 [96], replicated, may hold values from 0.03 to 0.25
- mixing: float32 [96, 96], replicated, may hold values from -0.625 to 0.625
Outputs:
- next_atmosphere: float32 [384, 96, 768], P('lat', 'seg')
- next_clouds: float32 [32, 96, 49152], P('lat', None, 'seg')
The draws below stay inside these ranges and needn't reach their ends.
Inputs may be any that keep to these rules, and one draw needn't show every extreme that they name: channel_lat[c] lies in the latitude rows c * 12 to (c + 1) * 12 - 1. `cell_column`: within each segment of 6144 cells of a channel, column numbers never fall and every column holds between half of 64 and three halves of 64 cells; both bounds are reached in every segment.
All inputs are finite; a program needn't handle non-finite values.
Results may differ from the reference program's by a relative error of at most 0.0003.
Values sent between devices are 32-bit elements; how exact they have to be, the bound alone decides.
No kernel may reach another device: no remote copies, remote signals or barrier semaphores. Data moves between devices by JAX's collectives and lax.ppermute only.
A program may use at most 64 MiB of HBM per device.

```python
import math
import jax
import jax.numpy as jnp
from jax import lax

NLON = 768
M = 256
NT = 256
CPC = 64
LAT_DEV = 12
STEPS = 2
SUBSTEPS = 3
K = 96
NLAT = 384
CHANNELS = 32
COLS_SEG = 96
CELLS_SEG = 6144
CELLS = 49152
N_SEG = 8


def draw_channel_lat(key, part):
    offsets = jax.random.randint(key, (CHANNELS,), 0, LAT_DEV)
    offsets = offsets.at[0].set(0)
    offsets = offsets.at[CHANNELS - 1].set(LAT_DEV - 1)
    return (jnp.arange(CHANNELS, dtype=jnp.int32) * LAT_DEV + offsets).astype(jnp.int32)


def draw_cell_column(key, part):
    segments = CELLS // CELLS_SEG
    blocks = CHANNELS * segments
    pair_count = COLS_SEG // 2
    shift_key, order_key = jax.random.split(key)
    shifts = jax.random.randint(shift_key, (blocks, pair_count), -1, 2) * (CPC // 2)
    shifts = shifts.at[:, 0].set(CPC // 2)
    by_slot = jnp.concatenate((CPC + shifts, CPC - shifts), axis=1)
    orders = jax.vmap(lambda subkey: jax.random.permutation(subkey, COLS_SEG))(jax.random.split(order_key, blocks))
    counts = jnp.zeros((blocks, COLS_SEG), jnp.int32).at[jnp.arange(blocks)[:, None], orders].set(by_slot)
    bounds = jnp.cumsum(counts, axis=1)
    cells = jnp.arange(CELLS_SEG, dtype=jnp.int32)
    column = jax.vmap(lambda limits: jnp.searchsorted(limits, cells, side='right'))(bounds)
    return column.reshape(CHANNELS, segments * CELLS_SEG).astype(jnp.int32)


def block_levels(rng, shape, cuts, smallest, largest):
    loudness = 1.0
    for dim, shards_of in cuts:
        draws = jax.random.uniform(jax.random.fold_in(jax.random.fold_in(rng, 6), dim), (shards_of,), jnp.float32, smallest / len(cuts), largest / len(cuts))
        loudness = loudness * jnp.repeat(jnp.exp(draws), shape[dim] // shards_of).reshape((-1,) + (1,) * (len(shape) - 1 - dim))
    return loudness


def normal_values(own_key, extent, deviation, most, pieces=(), held_as=jnp.bfloat16):
    values = deviation * jax.random.normal(own_key, extent, jnp.float32)
    if pieces:
        values = values * block_levels(own_key, extent, pieces, -0.22, 0.18)
    return jnp.clip(values, -most, most).astype(held_as)


def setup_inputs(seed: int = 0) -> dict:
    arg_keys = jax.random.split(jax.random.key(seed), 8)
    return {
        "atmosphere": normal_values(arg_keys[0], (NLAT, K, NLON), 1.0, 6.0, ((0, 32), (1, 8)), jnp.float32),
        "cloud_state": normal_values(arg_keys[1], (CHANNELS, K, CELLS), 1.0, 6.0, ((0, 32), (2, 8)), jnp.float32),
        "channel_lat": draw_channel_lat(jax.random.fold_in(arg_keys[7], 71), 0),
        "cell_column": draw_cell_column(jax.random.fold_in(arg_keys[7], 71), 0),
        "channel_wind": jnp.clip(jax.random.uniform(arg_keys[4], (CHANNELS, K), jnp.float32, -0.45, 0.45) * block_levels(arg_keys[4], (CHANNELS, K), ((0, 32),), -0.4, 0.0), -0.45, 0.45),
        "diffusivity": jnp.clip(jnp.exp(jax.random.uniform(arg_keys[5], (K,), jnp.float32, math.log(0.03), math.log(0.25))), 0.03, 0.25),
        "mixing": normal_values(arg_keys[6], (K, K), K ** -0.5, 0.625, (), jnp.float32),
    }


RELAXATION = 0.5
MIXING_RATE = 0.3
DAMPING = 0.2
COUPLING = 2.0
HIGHEST = lax.Precision.HIGHEST


def fourier_tables(wavenumbers, longitudes):
    positions = jnp.arange(longitudes, dtype=jnp.int32)
    phase_turns = (positions[:, None] * wavenumbers[None, :]) % longitudes
    angles = phase_turns.astype(jnp.float32) * (2.0 * math.pi / longitudes)
    waves_pair = jnp.stack((jnp.cos(angles), jnp.sin(angles)), axis=2)
    weights = jnp.where(wavenumbers == 0, 1.0, 2.0).astype(jnp.float32)
    return waves_pair / longitudes, waves_pair * weights[None, :, None]


def meridian_tables(latitudes, degrees, lat_total):
    phase_turns = (degrees[:, None] * (2 * latitudes[None, :] + 1)) % (4 * lat_total)
    angles = phase_turns.astype(jnp.float32) * (math.pi / (2.0 * lat_total))
    basis = jnp.cos(angles)
    weights = jnp.where(degrees == 0, 1.0, 2.0).astype(jnp.float32) / lat_total
    return basis * weights[:, None], jnp.transpose(basis)


def implicit_solve(spectrum, wavenumbers):
    degree_total = spectrum.shape[0]
    degrees = jnp.arange(degree_total, dtype=jnp.int32)
    wave_values = wavenumbers.astype(jnp.float32)
    degree_values = degrees.astype(jnp.float32)
    size_ratio = (wave_values[None, :] * wave_values[None, :] + degree_values[:, None] * degree_values[:, None]) / (degree_total * degree_total)
    damping_factor = (1.0 + size_ratio * size_ratio)[:, :, None, None]
    coupling_factor = (COUPLING * size_ratio)[:, :, None, None]
    determinant = damping_factor * damping_factor + coupling_factor * coupling_factor
    retained = ((wavenumbers[None, :] + degrees[:, None]) < degree_total).astype(jnp.float32)[:, :, None, None, None]
    shape_full = spectrum.shape
    components = spectrum.reshape(shape_full[0], shape_full[1], shape_full[2], shape_full[3] // 3, 3)
    vorticity = components[..., 0] / damping_factor
    divergence = (damping_factor * components[..., 1] + coupling_factor * components[..., 2]) / determinant
    geopotential = (damping_factor * components[..., 2] - coupling_factor * components[..., 1]) / determinant
    return (jnp.stack((vorticity, divergence, geopotential), axis=4) * retained).reshape(shape_full)


def advance(padded, forcing, diffusivity, channel_wind, mixing):
    center = padded[:, :, 1:-1]
    right_cell = padded[:, :, 2:]
    left_cell = padded[:, :, :-2]
    mixed_levels = jnp.einsum("kl,clx->ckx", mixing, center, precision=HIGHEST)
    return (center + diffusivity[None, :, None] * (right_cell - 2.0 * center + left_cell)
            - 0.5 * channel_wind[:, :, None] * (right_cell - left_cell)
            + MIXING_RATE * mixed_levels + forcing - DAMPING * jnp.tanh(center))


def channel_step(clouds, column, wind_row, profile, diffusivity, mixing):
    local_cells = column.reshape(N_SEG, CELLS_SEG)
    onehot = (local_cells[:, :, None] == jnp.arange(COLS_SEG, dtype=jnp.int32)[None, None, :]).astype(jnp.float32)
    counts = jnp.sum(onehot, axis=1)

    def column_mean(values):
        column_sums = jnp.einsum("ksx,sxn->ksn", values.reshape(K, N_SEG, CELLS_SEG), onehot, precision=HIGHEST)
        return (column_sums / counts[None]).reshape(K, NLON)

    start_mean = column_mean(clouds)
    pulled = RELAXATION * (profile - start_mean)
    forcing = jnp.einsum("ksn,sxn->ksx", pulled.reshape(K, N_SEG, COLS_SEG), onehot, precision=HIGHEST).reshape(1, K, CELLS)
    cloud_now = clouds[None]
    for substep in range(SUBSTEPS):
        padded = jnp.concatenate((cloud_now[:, :, -1:], cloud_now, cloud_now[:, :, :1]), axis=2)
        cloud_now = advance(padded, forcing, diffusivity, wind_row[None], mixing)
    return cloud_now[0], column_mean(cloud_now[0]) - start_mean


def reference(atmosphere, cloud_state, channel_lat, cell_column, channel_wind, diffusivity, mixing):
    wavenumbers = jnp.arange(M, dtype=jnp.int32)
    forward, inverse = fourier_tables(wavenumbers, NLON)
    to_spec, from_spec = meridian_tables(jnp.arange(NLAT, dtype=jnp.int32), jnp.arange(NT, dtype=jnp.int32), NLAT)
    for model_step in range(STEPS):
        profiles = jnp.take(atmosphere, channel_lat, axis=0)
        cloud_state, tendency = lax.map(
            lambda packed: channel_step(packed[0], packed[1], packed[2], packed[3], diffusivity, mixing),
            (cloud_state, cell_column, channel_wind, profiles))
        atmosphere = atmosphere.at[channel_lat].add(tendency)
        coeffs = jnp.einsum("jkx,xmc->jmck", atmosphere, forward, precision=HIGHEST)
        spectrum = jnp.einsum("nj,jmck->nmck", to_spec, coeffs, precision=HIGHEST)
        spectrum = implicit_solve(spectrum, wavenumbers)
        back_rows = jnp.einsum("jn,nmck->jmck", from_spec, spectrum, precision=HIGHEST)
        atmosphere = jnp.einsum("jmck,xmc->jkx", back_rows, inverse, precision=HIGHEST)
    return atmosphere, cloud_state
```

```python
import numpy as np

import jax
import jax.numpy as jnp
from jax import lax
from jax.experimental import pallas as pl
from jax.experimental.pallas import tpu as pltpu
from jax.sharding import PartitionSpec as P

NLON = 768
M = 256
NT = 256
NLAT = 384
LAT_DEV = 12
K = 96
KD = 12
COLS = 96
CELLS = 6144
LATS = 32
SEGS = 8
TILE = 256
EXT = CELLS + 512
RELAXATION = 0.5
MIXING_RATE = 0.3
DAMPING = 0.2
COUPLING = 2.0
F32 = jnp.float32
BF16 = jnp.bfloat16
HIGHEST = lax.Precision.HIGHEST
HIGH = lax.Precision.HIGH

CHIP_GROUPS = [[16 * q + i for i in range(16)] for q in range(16)]
ROW_GROUPS = [[2 * q + b for q in range(16)] for b in range(2)]
CORE_SWAP = [(i, i ^ 1) for i in range(LATS)]


def tables():
    m = np.arange(M)
    x = np.arange(NLON)
    angles = 2.0 * np.pi * ((m[:, None] * x[None, :]) % NLON) / NLON
    waves = np.stack([np.cos(angles), np.sin(angles)])
    sigma = np.where(m == 0, 1.0, 2.0)
    inverse = (waves * sigma[None, :, None]).reshape(2 * M, NLON)
    forward = (waves / NLON).reshape(2 * M, NLON).T
    forward_seg = np.zeros((SEGS, 128, 2 * M))
    forward_seg[:, :COLS] = forward.reshape(SEGS, COLS, 2 * M)
    inverse_seg = np.zeros((2 * M, SEGS, 128))
    for s in range(SEGS):
        inverse_seg[:, s, : COLS + 1] = inverse[:, (COLS * s + np.arange(COLS + 1)) % NLON]
        inverse_seg[:, s, COLS + 1] = inverse[:, (COLS * s - 1) % NLON]
    n = np.arange(NT)
    j = np.arange(NLAT)
    basis = np.cos(np.pi * ((n[:, None] * (2 * j[None, :] + 1)) % (4 * NLAT)) / (2 * NLAT))
    weights = np.where(n == 0, 1.0, 2.0) / NLAT
    size = (m[None, :] ** 2 + n[:, None] ** 2) / (NT * NT)
    damping = 1.0 + size * size
    coupling = COUPLING * size
    det = damping**2 + coupling**2
    keep = (m[None, :] + n[:, None] < NT).astype(np.float64)
    update = np.stack([keep / damping, keep * damping / det, keep * coupling / det])
    row_weights = np.transpose(update * weights[None, :, None], (1, 0, 2)).reshape(NT, 3 * M)
    f = np.float32
    return dict(
        forward=forward.astype(f),
        inverse=inverse.astype(f),
        forward_seg=forward_seg.reshape(SEGS * 128, 2 * M).astype(f),
        inverse_seg=inverse_seg.reshape(2 * M, SEGS * 128).astype(f),
        to_spec=(basis * weights[:, None]).astype(f),
        from_spec=np.ascontiguousarray(basis.T).astype(f),
        update=update.astype(f),
        row_weights=row_weights.astype(f),
    )


def permutations():
    natural = np.zeros((K, SEGS * 24), np.float32)
    grouped = np.zeros((K, SEGS * 24), np.float32)
    for s in range(SEGS):
        for i in range(KD):
            natural[KD * s + i, 24 * s + i] = 1.0
            grouped[KD * s + i, 24 * s + (i % 3) * 4 + i // 3] = 1.0
    return natural, grouped


def lanes_of(shape):
    return lax.broadcasted_iota(jnp.int32, shape, len(shape) - 1)


def split(x):
    high = x.astype(BF16)
    low = (x - high.astype(F32)).astype(BF16)
    return high, low


def mixing_block(mixing):
    high, low = split(MIXING_RATE * mixing)
    return jnp.concatenate(
        [jnp.concatenate([high, high], axis=1), jnp.concatenate([low, low], axis=1)], axis=0
    )


def substep_tile(window, mix, diffusivity, wind):
    width = window.shape[1]
    center = window[:, 128 : width - 128]
    right = pltpu.roll(window, width - 1, 1)[:, 128 : width - 128]
    left = pltpu.roll(window, 1, 1)[:, 128 : width - 128]
    high, low = split(center)
    mixed = jnp.dot(mix, jnp.concatenate([high, low], axis=0), preferred_element_type=F32)
    return (
        center
        + diffusivity * (right - 2.0 * center + left)
        - 0.5 * wind * (right - left)
        + (mixed[:K] + mixed[K:])
        - DAMPING * jnp.tanh(center)
    )


def column_hits(col):
    ids = lax.broadcasted_iota(jnp.int32, (128, col.shape[1]), 0)
    return jnp.where(ids == col, 1.0, 0.0).astype(BF16)


def edge_rows(first, last, mean_first, mean_last):
    lane = lanes_of((K, 128))
    edge = jnp.where(
        lane < 3,
        first,
        jnp.where(
            lane < 6, pltpu.roll(last, 6, 1), jnp.where(lane == 6, mean_first, mean_last)
        ),
    )
    padded = jnp.concatenate([edge, jnp.zeros((32, 128), F32)], axis=0)
    return padded.T[:8]


def prepare_kernel(off_ref, row_ref, first_ref, last_ref, colf_ref, coll_ref, send_ref):
    del off_ref
    row = row_ref[0]
    lane = lanes_of((KD, 128))
    hit_first = jnp.where(colf_ref[...] == 0, 1.0, 0.0)
    hit_last = jnp.where(coll_ref[...] == COLS - 1, 1.0, 0.0)
    first, last = first_ref[...], last_ref[...]
    mean_first = jnp.sum(first * hit_first, axis=1, keepdims=True) / jnp.sum(
        hit_first, axis=1, keepdims=True
    )
    mean_last = jnp.sum(last * hit_last, axis=1, keepdims=True) / jnp.sum(
        hit_last, axis=1, keepdims=True
    )
    edge = edge_rows(first, last, mean_first, mean_last)
    for s in range(SEGS):
        own = pltpu.roll(row, (NLON - COLS * s) % NLON, 1)[:, :128]
        before = pltpu.roll(row, (COLS + 1 - (COLS * s - 1)) % NLON, 1)[:, :128]
        chunk = jnp.where(lane <= COLS, own, jnp.where(lane == COLS + 1, before, 0.0))
        send_ref[s, 0:KD, :] = chunk
        send_ref[s, KD:16, :] = jnp.zeros((16 - KD, 128), F32)
        send_ref[s, 16:24, :] = edge


def prepare(offset, atmosphere, clouds, col):
    last = CELLS // 128 - 1
    return pl.pallas_call(
        prepare_kernel,
        grid_spec=pltpu.PrefetchScalarGridSpec(
            num_scalar_prefetch=1,
            grid=(1,),
            in_specs=[
                pl.BlockSpec((1, KD, NLON), lambda i, off: (off[0], 0, 0)),
                pl.BlockSpec((K, 128), lambda i, off: (0, 0)),
                pl.BlockSpec((K, 128), lambda i, off: (0, last)),
                pl.BlockSpec((1, 128), lambda i, off: (0, 0)),
                pl.BlockSpec((1, 128), lambda i, off: (0, last)),
            ],
            out_specs=pl.BlockSpec((SEGS, 24, 128), lambda i, off: (0, 0, 0)),
        ),
        out_shape=jax.ShapeDtypeStruct((SEGS, 24, 128), F32),
        name="prepare",
    )(offset, atmosphere, clouds, clouds, col, col)


def inner_kernel(with_mean, *refs):
    if with_mean:
        c_ref, col_ref, diff_ref, wind_ref, mixing_ref, base_ref, mean_ref, inv_ref, ext, sem = refs
    else:
        c_ref, diff_ref, wind_ref, mixing_ref, base_ref, ext, sem = refs
    copy = pltpu.make_async_copy(c_ref, ext.at[:, 128 : 128 + CELLS], sem)
    copy.start()
    ext[:, 0:128] = jnp.zeros((K, 128), F32)
    ext[:, 128 + CELLS :] = jnp.zeros((K, 128), F32)
    mix = mixing_block(mixing_ref[...])
    diffusivity, wind = diff_ref[...], wind_ref[...]
    copy.wait()

    def step(t, total):
        start = pl.multiple_of(t * TILE, TILE)
        window = ext[:, pl.ds(start, TILE + 256)]
        base_ref[:, pl.ds(start, TILE)] = substep_tile(window, mix, diffusivity, wind)
        if not with_mean:
            return total
        hits = column_hits(col_ref[:, pl.ds(start, TILE)])
        high, low = split(window[:, 128 : 128 + TILE])
        rows = jnp.concatenate([high, low, jnp.ones((16, TILE), BF16)], axis=0)
        return total + lax.dot_general(
            rows, hits, (((1,), (1,)), ((), ())), preferred_element_type=F32
        )

    if with_mean:
        total = lax.fori_loop(0, CELLS // TILE, step, jnp.zeros((2 * K + 16, 128), F32))
        counts = total[2 * K : 2 * K + 8]
        inv = jnp.where(counts > 0.0, 1.0 / jnp.maximum(counts, 1.0), 0.0)
        inv_ref[...] = inv
        mean_ref[...] = (total[:K] + total[K : 2 * K]) * inv[0:1]
    else:
        lax.fori_loop(0, CELLS // TILE, step, 0)


VMEM_SPEC = pl.BlockSpec(memory_space=pltpu.VMEM)
ANY_SPEC = pl.BlockSpec(memory_space=pl.ANY)


def inner(clouds, col, diffusivity, wind, mixing, with_mean):
    args = [clouds] + ([col] if with_mean else []) + [diffusivity, wind, mixing]
    shapes = [jax.ShapeDtypeStruct((K, CELLS), F32)]
    if with_mean:
        shapes += [jax.ShapeDtypeStruct((K, 128), F32), jax.ShapeDtypeStruct((8, 128), F32)]
    out = pl.pallas_call(
        lambda *refs: inner_kernel(with_mean, *refs),
        in_specs=[ANY_SPEC] + [VMEM_SPEC] * (len(args) - 1),
        out_specs=[VMEM_SPEC] * len(shapes),
        out_shape=shapes,
        scratch_shapes=[pltpu.VMEM((K, CELLS + 256), F32), pltpu.SemaphoreType.DMA],
        compiler_params=pltpu.CompilerParams(vmem_limit_bytes=40 << 20),
        name="inner",
    )(*args)
    return out if with_mean else out[0]


def outer_kernel(
    seg_ref, base_ref, first_ref, last_ref, prof_ref, halo_ref, perm_ref, back_ref, mean_ref, inv_ref,
    col_ref, diff_ref, wind_ref, mixing_ref, out_ref, end_ref, send_ref, ext1, ext2, force, cols, sem,
):
    copy = pltpu.make_async_copy(base_ref, ext1.at[:, 256 : 256 + CELLS], sem)
    copy.start()
    seg = seg_ref[0]
    lane = lanes_of((K, 128))
    zeros = jnp.zeros((K, 128), F32)
    mix = mixing_block(mixing_ref[...])
    diffusivity, wind = diff_ref[...], wind_ref[...]

    from_left = halo_ref[lax.rem(seg + SEGS - 1, SEGS), 16:24, :]
    from_right = halo_ref[lax.rem(seg + 1, SEGS), 16:24, :]
    edges = jnp.concatenate([from_left, from_right, jnp.zeros((112, 128), F32)], axis=0).T[:K]
    left_tile = jnp.where(lane >= 125, pltpu.roll(edges, 122, 1), 0.0)
    right_tile = jnp.where(lane < 3, pltpu.roll(edges, 120, 1), 0.0)
    mean = mean_ref[...]
    mean_all = jnp.where(
        lane < COLS,
        mean,
        jnp.where(
            lane == COLS,
            pltpu.roll(edges, COLS - 14, 1),
            jnp.where(lane == COLS + 1, pltpu.roll(edges, COLS + 1 - 7, 1), 0.0),
        ),
    )
    profile = jnp.dot(
        perm_ref[...],
        prof_ref[...].reshape(SEGS * 24, 128),
        precision=HIGHEST,
        preferred_element_type=F32,
    )
    pulled = jnp.where(lane < COLS + 2, RELAXATION * (profile - mean_all), 0.0)
    pulled = jnp.concatenate(split(pulled), axis=1)

    cols[:, 0:256] = jnp.full((1, 256), COLS + 1, jnp.int32)
    cols[:, 256 + CELLS :] = jnp.full((1, 256), COLS, jnp.int32)
    cols[:, 256 : 256 + CELLS] = col_ref[...]
    ext1[:, 0:128] = zeros
    ext1[:, EXT - 128 :] = zeros
    copy.wait()
    left_window = jnp.concatenate([zeros, left_tile, first_ref[...]], axis=1)
    ext1[:, 128:384] = substep_tile(left_window, mix, diffusivity, wind)
    right_window = jnp.concatenate([last_ref[...], right_tile, zeros], axis=1)
    ext1[:, EXT - 384 : EXT - 128] = substep_tile(right_window, mix, diffusivity, wind)

    def force_step(t, _):
        start = pl.multiple_of(128 + t * TILE, 128)
        hits = column_hits(cols[:, pl.ds(start, TILE)])
        forced = jnp.dot(
            pulled, jnp.concatenate([hits, hits], axis=0), preferred_element_type=F32
        )
        force[:, pl.ds(start, TILE)] = forced
        ext1[:, pl.ds(start, TILE)] += forced
        return 0

    lax.fori_loop(0, CELLS // TILE + 1, force_step, 0)

    def second_step(t, _):
        start = pl.multiple_of(t * TILE, TILE)
        here = pl.multiple_of(start + 128, 128)
        window = ext1[:, pl.ds(start, TILE + 256)]
        ext2[:, pl.ds(here, TILE)] = (
            substep_tile(window, mix, diffusivity, wind) + force[:, pl.ds(here, TILE)]
        )
        return 0

    lax.fori_loop(0, CELLS // TILE + 1, second_step, 0)

    def third_step(t, total):
        start = pl.multiple_of(t * TILE, TILE)
        here = pl.multiple_of(start + 256, 128)
        window = ext2[:, pl.ds(pl.multiple_of(start + 128, 128), TILE + 256)]
        value = substep_tile(window, mix, diffusivity, wind) + force[:, pl.ds(here, TILE)]
        out_ref[:, pl.ds(start, TILE)] = value
        hits = column_hits(cols[:, pl.ds(here, TILE)])
        rows = jnp.concatenate(split(value), axis=0)
        return total + lax.dot_general(
            rows, hits, (((1,), (1,)), ((), ())), preferred_element_type=F32
        )

    total = lax.fori_loop(0, CELLS // TILE, third_step, jnp.zeros((2 * K, 128), F32))
    end = (total[:K] + total[K:]) * inv_ref[0:1]
    end_ref[...] = end
    tendency = jnp.where(lane < COLS, end - mean, 0.0)
    sent = jnp.dot(back_ref[...], tendency, precision=HIGHEST, preferred_element_type=F32)
    edge = edge_rows(
        out_ref[:, 0:128], out_ref[:, CELLS - 128 :], end[:, 0:1], end[:, COLS - 1 : COLS]
    )
    for s in range(SEGS):
        send_ref[s, 0:16, :] = sent[24 * s : 24 * s + 16]
        send_ref[s, 16:24, :] = edge


def outer(seg, base, clouds, profile, halo, perm, back, mean, inv, col, diffusivity, wind, mixing):
    ends = CELLS // 256 - 1
    full = lambda shape: pl.BlockSpec(shape, lambda i, seg: (0,) * len(shape))
    return pl.pallas_call(
        outer_kernel,
        grid_spec=pltpu.PrefetchScalarGridSpec(
            num_scalar_prefetch=1,
            grid=(1,),
            in_specs=[
                ANY_SPEC,
                pl.BlockSpec((K, 256), lambda i, seg: (0, 0)),
                pl.BlockSpec((K, 256), lambda i, seg: (0, ends)),
                full((SEGS, 24, 128)),
                full((SEGS, 24, 128)),
                full((K, SEGS * 24)),
                full((SEGS * 24, K)),
                full((K, 128)),
                full((8, 128)),
                full((1, CELLS)),
                full((K, 1)),
                full((K, 1)),
                full((K, K)),
            ],
            out_specs=[full((K, CELLS)), full((K, 128)), full((SEGS, 24, 128))],
            scratch_shapes=[
                pltpu.VMEM((K, EXT), F32),
                pltpu.VMEM((K, EXT), F32),
                pltpu.VMEM((K, EXT), F32),
                pltpu.VMEM((1, EXT), jnp.int32),
                pltpu.SemaphoreType.DMA,
            ],
        ),
        out_shape=[
            jax.ShapeDtypeStruct((K, CELLS), F32),
            jax.ShapeDtypeStruct((K, 128), F32),
            jax.ShapeDtypeStruct((SEGS, 24, 128), F32),
        ],
        compiler_params=pltpu.CompilerParams(vmem_limit_bytes=48 << 20),
        name="outer",
    )(seg, base, clouds, clouds, profile, halo, perm, back, mean, inv, col, diffusivity, wind, mixing)


def dft_rows(received, table):
    lead = received.shape[:-3]
    rows = jnp.moveaxis(received[..., :KD, :], -3, -2).reshape(lead + (KD, SEGS * 128))
    coeffs = jnp.dot(rows, table, precision=HIGH).reshape(lead + (3, 4, 2, M))
    return jnp.moveaxis(coeffs, -2, -3).reshape(lead + (3, 8, M))


def weigh(factors, rows, axis):
    vort, div, geo = rows[:, :, 0], rows[:, :, 1], rows[:, :, 2]
    f = factors[:, :, :, None, :]
    return jnp.stack(
        (
            jnp.sum(f[0] * vort, axis=axis),
            jnp.sum(f[1] * div + f[2] * geo, axis=axis),
            jnp.sum(f[1] * geo - f[2] * div, axis=axis),
        ),
        axis=1,
    )


def spectral_twice(rows, tab, lat):
    sent = rows.reshape(LAT_DEV, 3, 8, LATS, 8).transpose(3, 0, 1, 2, 4)
    sent = sent.reshape(LATS, LAT_DEV * 3 * 64)
    got = lax.all_to_all(sent, "lat", 0, 0, tiled=True).reshape(NLAT, 3 * 64)
    spec = jnp.dot(tab["to_spec"], got, precision=HIGH).reshape(NT, 3, 8, 8)
    factors = lax.dynamic_slice_in_dim(tab["update"], lat * 8, 8, axis=2)[:, :, None, :]
    vort, div, geo = spec[:, 0], spec[:, 1], spec[:, 2]
    for _ in range(2):
        vort = factors[0] * vort
        div, geo = factors[1] * div + factors[2] * geo, factors[1] * geo - factors[2] * div
    spec = jnp.stack((vort, div, geo), axis=1).reshape(NT, 3 * 64)
    back = jnp.dot(tab["from_spec"], spec, precision=HIGH).reshape(LATS, LAT_DEV * 3 * 64)
    got = lax.all_to_all(back, "lat", 0, 0, tiled=True)
    return got.reshape(LATS, LAT_DEV, 3, 8, 8).transpose(1, 2, 3, 0, 4).reshape(LAT_DEV, 3, 8, M)


def shards(atmosphere, cloud_state, channel_lat, cell_column, channel_wind, diffusivity, mixing):
    tab = {name: jnp.asarray(value) for name, value in tables().items()}
    natural, grouped = permutations()
    lat = lax.axis_index("lat")
    seg = lax.axis_index("seg").astype(jnp.int32).reshape(1)
    core = lat % 2
    chip = lat // 2
    offset = channel_lat - (lat * LAT_DEV).astype(jnp.int32)
    clouds = cloud_state[0]
    col = cell_column
    wind = channel_wind.reshape(K, 1)
    diff = diffusivity.reshape(K, 1)

    position = lax.all_to_all(
        jnp.broadcast_to(channel_lat[None, :], (LATS, 128)), "lat", 0, 0, tiled=True
    )[:, 0]

    first_send = prepare(offset, atmosphere, clouds, col)
    first_got = lax.all_to_all(first_send, "seg", 0, 0, tiled=True)
    base, mean, inv = inner(clouds, col, diff, wind, mixing, True)

    basis = tab["from_spec"]
    picks = (position[:, None] == jnp.arange(NLAT, dtype=jnp.int32)[None, :]).astype(F32)
    channel_basis = jnp.dot(picks, basis, precision=HIGHEST).reshape(16, 2, NT)
    mine = lax.dynamic_index_in_dim(channel_basis, core, 1, keepdims=False)
    others = lax.dynamic_index_in_dim(channel_basis, 1 - core, 1, keepdims=False)
    here = lax.dynamic_slice_in_dim(basis, lat * LAT_DEV, LAT_DEV, axis=0)
    pair = lax.dynamic_index_in_dim(channel_basis, chip, 0, keepdims=False)
    products = jnp.concatenate(
        (
            (mine[:, None] * here[None]).reshape(-1, NT),
            (others[:, None] * here[None]).reshape(-1, NT),
            (mine[:, None] * pair[None]).reshape(-1, NT),
        ),
        axis=0,
    )
    weights = jnp.dot(products, tab["row_weights"], precision=HIGH).reshape(-1, 3, M)
    weights = weights.transpose(1, 0, 2)
    to_mine = weights[:, :192].reshape(3, 16, LAT_DEV, M)
    to_others = weights[:, 192:384].reshape(3, 16, LAT_DEV, M)
    to_pair = weights[:, 384:].reshape(3, 16, 2, M)

    ordered = atmosphere.reshape(LAT_DEV, 4, 3, NLON).transpose(0, 2, 1, 3).reshape(-1, NLON)
    rows = jnp.dot(ordered, tab["forward"], precision=HIGH).reshape(LAT_DEV, 3, 4, 2, M)
    rows = rows.transpose(0, 1, 3, 2, 4).reshape(LAT_DEV, 3, 8, M)
    base_mine = weigh(to_mine, rows[None], 1)
    base_others = weigh(to_others, rows[None], 1)
    base_sum = base_mine + lax.ppermute(base_others, "lat", CORE_SWAP)

    clouds, mean_1, send = outer(
        seg, base, clouds, first_got, first_got, jnp.asarray(natural), jnp.asarray(grouped.T.copy()),
        mean, inv, col, diff, wind, mixing,
    )
    got = lax.all_to_all(
        jnp.concatenate((send, send), axis=0), ("lat", "seg"), 0, 0,
        axis_index_groups=CHIP_GROUPS, tiled=True,
    ).reshape(2, SEGS, 24, 128)
    base = inner(clouds, col, diff, wind, mixing, False)
    pair_rows = dft_rows(got, tab["forward_seg"])
    parts = base_sum + weigh(to_pair, pair_rows[None], 1)
    parts = lax.all_to_all(parts, "lat", 0, 0, axis_index_groups=ROW_GROUPS, tiled=True)
    profile_rows = jnp.sum(parts, axis=0).reshape(3, 2, 4, M).transpose(0, 2, 1, 3).reshape(KD, 2 * M)
    profile = jnp.dot(profile_rows, tab["inverse_seg"], precision=HIGH).reshape(KD, SEGS, 128)
    profile = jnp.pad(profile.transpose(1, 0, 2), ((0, 0), (0, 24 - KD), (0, 0)))
    profile = lax.all_to_all(profile, "seg", 0, 0, tiled=True)

    own_row = lax.dynamic_index_in_dim(pair_rows, core, 0)
    at_channel = jnp.arange(LAT_DEV, dtype=jnp.int32) == offset[0]
    forced_rows = rows + jnp.where(at_channel[:, None, None, None], own_row, 0.0)
    settled = spectral_twice(forced_rows, tab, lat)

    halo = lax.dynamic_index_in_dim(got, core, 0, keepdims=False)
    clouds, _, send = outer(
        seg, base, clouds, profile, halo, jnp.asarray(grouped), jnp.asarray(grouped.T.copy()),
        mean_1, inv, col, diff, wind, mixing,
    )
    got = lax.all_to_all(send, "seg", 0, 0, tiled=True)
    last_rows = dft_rows(got, tab["forward_seg"])
    from_mine = lax.all_to_all(
        jnp.broadcast_to(last_rows[None], (16, 3, 8, M)), "lat", 0, 0,
        axis_index_groups=ROW_GROUPS, tiled=True,
    )
    from_others = lax.ppermute(from_mine, "lat", CORE_SWAP)
    final = settled + weigh(to_mine, from_mine[:, None], 0) + weigh(to_others, from_others[:, None], 0)
    final = final.reshape(LAT_DEV, 3, 2, 4, M).transpose(0, 3, 1, 2, 4).reshape(LAT_DEV * KD, 2 * M)
    grid = jnp.dot(final, tab["inverse"], precision=HIGH).reshape(LAT_DEV, KD, NLON)
    return grid, clouds[None]


def solution(mesh):
    placed = (
        P("lat", "seg", None),
        P("lat", None, "seg"),
        P("lat"),
        P("lat", "seg"),
        P("lat", None),
        P(),
        P(),
    )
    return jax.shard_map(
        shards,
        mesh=mesh,
        in_specs=placed,
        out_specs=(P("lat", "seg", None), P("lat", None, "seg")),
        check_vma=False,
    )
```

```python
import ml_dtypes
import numpy as np

import jax
import jax.numpy as jnp
from jax import lax
from jax.experimental import pallas as pl
from jax.experimental.pallas import tpu as pltpu
from jax.sharding import PartitionSpec as P

NLON = 768
M = 256
NT = 256
NLAT = 384
LAT_DEV = 12
K = 96
KD = 12
COLS = 96
CELLS = 6144
LATS = 32
SEGS = 8
TILE = 256
EXT = CELLS + 512
RELAXATION = 0.5
MIXING_RATE = 0.3
DAMPING = 0.2
COUPLING = 2.0
F32 = jnp.float32
BF16 = jnp.bfloat16
HIGHEST = lax.Precision.HIGHEST
HIGH = lax.Precision.HIGH

CHIP_GROUPS = [[16 * q + i for i in range(16)] for q in range(16)]
ROW_GROUPS = [[2 * q + b for q in range(16)] for b in range(2)]
CORE_SWAP = [(i, i ^ 1) for i in range(LATS)]


def tables():
    m = np.arange(M)
    x = np.arange(NLON)
    angles = 2.0 * np.pi * ((m[:, None] * x[None, :]) % NLON) / NLON
    waves = np.stack([np.cos(angles), np.sin(angles)])
    sigma = np.where(m == 0, 1.0, 2.0)
    inverse = (waves * sigma[None, :, None]).reshape(2 * M, NLON)
    forward = (waves / NLON).reshape(2 * M, NLON).T
    forward_seg = np.zeros((SEGS, 128, 2 * M))
    forward_seg[:, :COLS] = forward.reshape(SEGS, COLS, 2 * M)
    inverse_seg = np.zeros((2 * M, SEGS, 128))
    for s in range(SEGS):
        inverse_seg[:, s, : COLS + 1] = inverse[:, (COLS * s + np.arange(COLS + 1)) % NLON]
        inverse_seg[:, s, COLS + 1] = inverse[:, (COLS * s - 1) % NLON]
    n = np.arange(NT)
    j = np.arange(NLAT)
    basis = np.cos(np.pi * ((n[:, None] * (2 * j[None, :] + 1)) % (4 * NLAT)) / (2 * NLAT))
    weights = np.where(n == 0, 1.0, 2.0) / NLAT
    size = (m[None, :] ** 2 + n[:, None] ** 2) / (NT * NT)
    damping = 1.0 + size * size
    coupling = COUPLING * size
    det = damping**2 + coupling**2
    keep = (m[None, :] + n[:, None] < NT).astype(np.float64)
    update = np.stack([keep / damping, keep * damping / det, keep * coupling / det])
    twice = np.stack(
        [
            keep / damping**2,
            keep * (damping**2 - coupling**2) / det**2,
            keep * 2.0 * damping * coupling / det**2,
        ]
    )
    row_weights = np.transpose(update * weights[None, :, None], (1, 0, 2)).reshape(NT, 3 * M)
    parity = basis.reshape(NT, 16, 2, LAT_DEV)
    spread = np.zeros((2, NT, 16, 16))
    spread[:, :, :, :LAT_DEV] = np.transpose(parity, (2, 0, 1, 3))
    spread = spread.reshape(2, NT, 256)
    f = np.float32
    return dict(
        forward=pair_of(forward),
        inverse=pair_of(inverse),
        forward_seg=pair_of(forward_seg.reshape(SEGS * 128, 2 * M)),
        inverse_seg=pair_of(inverse_seg.reshape(2 * M, SEGS * 128)),
        to_spec=pair_of(spread * weights[None, :, None]),
        from_spec=pair_of(np.transpose(spread, (0, 2, 1))),
        basis=np.ascontiguousarray(basis.T).astype(f),
        twice=np.ascontiguousarray(np.transpose(twice.reshape(3, NT, 2, 128), (2, 0, 1, 3))).astype(f),
        row_weights=row_weights.astype(f),
    )


def pair_of(x):
    x = x.astype(np.float32)
    high = x.astype(ml_dtypes.bfloat16)
    low = (x - high.astype(np.float32)).astype(ml_dtypes.bfloat16)
    return np.stack((high, low))


def permutations():
    natural = np.zeros((K, SEGS * 16), np.float32)
    grouped = np.zeros((K, SEGS * 16), np.float32)
    for s in range(SEGS):
        for i in range(KD):
            natural[KD * s + i, 16 * s + i] = 1.0
            grouped[KD * s + i, 16 * s + (i % 3) * 4 + i // 3] = 1.0
    return natural, grouped


def lanes_of(shape):
    return lax.broadcasted_iota(jnp.int32, shape, len(shape) - 1)


def split(x):
    high = x.astype(BF16)
    low = (x - high.astype(F32)).astype(BF16)
    return high, low


def mixing_block(mixing):
    high, low = split(MIXING_RATE * mixing)
    return jnp.concatenate(
        [jnp.concatenate([high, high], axis=1), jnp.concatenate([low, low], axis=1)], axis=0
    )


def substep_tile(window, mix, diffusivity, wind):
    width = window.shape[1]
    center = window[:, 128 : width - 128]
    right = pltpu.roll(window, width - 1, 1)[:, 128 : width - 128]
    left = pltpu.roll(window, 1, 1)[:, 128 : width - 128]
    high, low = split(center)
    mixed = jnp.dot(mix, jnp.concatenate([high, low], axis=0), preferred_element_type=F32)
    return (
        center
        + diffusivity * (right - 2.0 * center + left)
        - 0.5 * wind * (right - left)
        + (mixed[:K] + mixed[K:])
        - DAMPING * jnp.tanh(center)
    )


def column_hits(col):
    ids = lax.broadcasted_iota(jnp.int32, (128, col.shape[1]), 0)
    return jnp.where(ids == col, 1.0, 0.0).astype(BF16)


def edge_rows(first, last, mean_first, mean_last):
    lane = lanes_of((K, 128))
    edge = jnp.where(
        lane < 3,
        first,
        jnp.where(
            lane < 6, pltpu.roll(last, 6, 1), jnp.where(lane == 6, mean_first, mean_last)
        ),
    )
    padded = jnp.concatenate([edge, jnp.zeros((32, 128), F32)], axis=0)
    return padded.T[:8]


def prepare_kernel(off_ref, row_ref, first_ref, last_ref, colf_ref, coll_ref, send_ref):
    del off_ref
    row = row_ref[0]
    lane = lanes_of((KD, 128))
    hit_first = jnp.where(colf_ref[...] == 0, 1.0, 0.0)
    hit_last = jnp.where(coll_ref[...] == COLS - 1, 1.0, 0.0)
    first, last = first_ref[...], last_ref[...]
    mean_first = jnp.sum(first * hit_first, axis=1, keepdims=True) / jnp.sum(
        hit_first, axis=1, keepdims=True
    )
    mean_last = jnp.sum(last * hit_last, axis=1, keepdims=True) / jnp.sum(
        hit_last, axis=1, keepdims=True
    )
    edge = edge_rows(first, last, mean_first, mean_last)
    for s in range(SEGS):
        own = pltpu.roll(row, (NLON - COLS * s) % NLON, 1)[:, :128]
        before = pltpu.roll(row, (COLS + 1 - (COLS * s - 1)) % NLON, 1)[:, :128]
        chunk = jnp.where(lane <= COLS, own, jnp.where(lane == COLS + 1, before, 0.0))
        send_ref[s, 0:KD, :] = chunk
        send_ref[s, KD:16, :] = jnp.zeros((16 - KD, 128), F32)
        send_ref[s, 16:24, :] = edge


def prepare(offset, atmosphere, clouds, col):
    last = CELLS // 128 - 1
    return pl.pallas_call(
        prepare_kernel,
        grid_spec=pltpu.PrefetchScalarGridSpec(
            num_scalar_prefetch=1,
            grid=(1,),
            in_specs=[
                pl.BlockSpec((1, KD, NLON), lambda i, off: (off[0], 0, 0)),
                pl.BlockSpec((K, 128), lambda i, off: (0, 0)),
                pl.BlockSpec((K, 128), lambda i, off: (0, last)),
                pl.BlockSpec((1, 128), lambda i, off: (0, 0)),
                pl.BlockSpec((1, 128), lambda i, off: (0, last)),
            ],
            out_specs=pl.BlockSpec((SEGS, 24, 128), lambda i, off: (0, 0, 0)),
        ),
        out_shape=jax.ShapeDtypeStruct((SEGS, 24, 128), F32),
        name="prepare",
    )(offset, atmosphere, clouds, clouds, col, col)


def inner_kernel(with_mean, *refs):
    if with_mean:
        c_ref, col_ref, diff_ref, wind_ref, mixing_ref, base_ref, mean_ref, inv_ref, ext, sem = refs
    else:
        c_ref, diff_ref, wind_ref, mixing_ref, base_ref, ext, sem = refs
    copy = pltpu.make_async_copy(c_ref, ext.at[:, 128 : 128 + CELLS], sem)
    copy.start()
    ext[:, 0:128] = jnp.zeros((K, 128), F32)
    ext[:, 128 + CELLS :] = jnp.zeros((K, 128), F32)
    mix = mixing_block(mixing_ref[...])
    diffusivity, wind = diff_ref[...], wind_ref[...]
    copy.wait()

    def step(t, total):
        start = pl.multiple_of(t * TILE, TILE)
        window = ext[:, pl.ds(start, TILE + 256)]
        base_ref[:, pl.ds(start, TILE)] = substep_tile(window, mix, diffusivity, wind)
        if not with_mean:
            return total
        hits = column_hits(col_ref[:, pl.ds(start, TILE)])
        high, low = split(window[:, 128 : 128 + TILE])
        rows = jnp.concatenate([high, low, jnp.ones((16, TILE), BF16)], axis=0)
        return total + lax.dot_general(
            rows, hits, (((1,), (1,)), ((), ())), preferred_element_type=F32
        )

    if with_mean:
        total = lax.fori_loop(0, CELLS // TILE, step, jnp.zeros((2 * K + 16, 128), F32), unroll=CELLS // TILE)
        counts = total[2 * K : 2 * K + 8]
        inv = jnp.where(counts > 0.0, 1.0 / jnp.maximum(counts, 1.0), 0.0)
        inv_ref[...] = inv
        mean_ref[...] = (total[:K] + total[K : 2 * K]) * inv[0:1]
    else:
        lax.fori_loop(0, CELLS // TILE, step, 0, unroll=CELLS // TILE)


VMEM_SPEC = pl.BlockSpec(memory_space=pltpu.VMEM)
ANY_SPEC = pl.BlockSpec(memory_space=pl.ANY)


def inner(clouds, col, diffusivity, wind, mixing, with_mean):
    args = [clouds] + ([col] if with_mean else []) + [diffusivity, wind, mixing]
    shapes = [jax.ShapeDtypeStruct((K, CELLS), F32)]
    if with_mean:
        shapes += [jax.ShapeDtypeStruct((K, 128), F32), jax.ShapeDtypeStruct((8, 128), F32)]
    out = pl.pallas_call(
        lambda *refs: inner_kernel(with_mean, *refs),
        in_specs=[ANY_SPEC] + [VMEM_SPEC] * (len(args) - 1),
        out_specs=[VMEM_SPEC] * len(shapes),
        out_shape=shapes,
        scratch_shapes=[pltpu.VMEM((K, CELLS + 256), F32), pltpu.SemaphoreType.DMA],
        cost_estimate=pl.CostEstimate(flops=1 << 30, bytes_accessed=12 << 20, transcendentals=0),
        compiler_params=pltpu.CompilerParams(vmem_limit_bytes=16 << 20),
        name="inner",
    )(*args)
    return out if with_mean else out[0]


def outer_kernel(
    seg_ref, base_ref, first_ref, last_ref, prof_ref, halo_ref, perm_ref, back_ref, mean_ref, inv_ref,
    col_ref, diff_ref, wind_ref, mixing_ref, out_ref, end_ref, send_ref, ext1, ext2, force, cols, sem,
):
    copy = pltpu.make_async_copy(base_ref, ext1.at[:, 256 : 256 + CELLS], sem)
    copy.start()
    seg = seg_ref[0]
    lane = lanes_of((K, 128))
    zeros = jnp.zeros((K, 128), F32)
    mix = mixing_block(mixing_ref[...])
    diffusivity, wind = diff_ref[...], wind_ref[...]

    from_left = halo_ref[lax.rem(seg + SEGS - 1, SEGS), 16:24, :]
    from_right = halo_ref[lax.rem(seg + 1, SEGS), 16:24, :]
    edges = jnp.concatenate([from_left, from_right, jnp.zeros((112, 128), F32)], axis=0).T[:K]
    left_tile = jnp.where(lane >= 125, pltpu.roll(edges, 122, 1), 0.0)
    right_tile = jnp.where(lane < 3, pltpu.roll(edges, 120, 1), 0.0)
    mean = mean_ref[...]
    mean_all = jnp.where(
        lane < COLS,
        mean,
        jnp.where(
            lane == COLS,
            pltpu.roll(edges, COLS - 14, 1),
            jnp.where(lane == COLS + 1, pltpu.roll(edges, COLS + 1 - 7, 1), 0.0),
        ),
    )
    profile = jnp.dot(
        perm_ref[...],
        prof_ref[...].reshape(SEGS * 16, 128),
        precision=HIGHEST,
        preferred_element_type=F32,
    )
    pulled = jnp.where(lane < COLS + 2, RELAXATION * (profile - mean_all), 0.0)
    pulled = jnp.concatenate(split(pulled), axis=1)

    cols[:, 0:256] = jnp.full((1, 256), COLS + 1, jnp.int32)
    cols[:, 256 + CELLS :] = jnp.full((1, 256), COLS, jnp.int32)
    cols[:, 256 : 256 + CELLS] = col_ref[...]
    ext1[:, 0:128] = zeros
    ext1[:, EXT - 128 :] = zeros
    copy.wait()
    left_window = jnp.concatenate([zeros, left_tile, first_ref[...]], axis=1)
    ext1[:, 128:384] = substep_tile(left_window, mix, diffusivity, wind)
    right_window = jnp.concatenate([last_ref[...], right_tile, zeros], axis=1)
    ext1[:, EXT - 384 : EXT - 128] = substep_tile(right_window, mix, diffusivity, wind)

    def force_step(t, _):
        start = pl.multiple_of(128 + t * TILE, 128)
        hits = column_hits(cols[:, pl.ds(start, TILE)])
        forced = jnp.dot(
            pulled, jnp.concatenate([hits, hits], axis=0), preferred_element_type=F32
        )
        force[:, pl.ds(start, TILE)] = forced
        ext1[:, pl.ds(start, TILE)] += forced
        return 0

    lax.fori_loop(0, CELLS // TILE + 1, force_step, 0, unroll=CELLS // TILE + 1)

    def second_step(t, _):
        start = pl.multiple_of(t * TILE, TILE)
        here = pl.multiple_of(start + 128, 128)
        window = ext1[:, pl.ds(start, TILE + 256)]
        ext2[:, pl.ds(here, TILE)] = (
            substep_tile(window, mix, diffusivity, wind) + force[:, pl.ds(here, TILE)]
        )
        return 0

    lax.fori_loop(0, CELLS // TILE + 1, second_step, 0, unroll=CELLS // TILE + 1)

    def third_step(t, total):
        start = pl.multiple_of(t * TILE, TILE)
        here = pl.multiple_of(start + 256, 128)
        window = ext2[:, pl.ds(pl.multiple_of(start + 128, 128), TILE + 256)]
        value = substep_tile(window, mix, diffusivity, wind) + force[:, pl.ds(here, TILE)]
        out_ref[:, pl.ds(start, TILE)] = value
        hits = column_hits(cols[:, pl.ds(here, TILE)])
        rows = jnp.concatenate(split(value), axis=0)
        return total + lax.dot_general(
            rows, hits, (((1,), (1,)), ((), ())), preferred_element_type=F32
        )

    total = lax.fori_loop(0, CELLS // TILE, third_step, jnp.zeros((2 * K, 128), F32), unroll=CELLS // TILE)
    end = (total[:K] + total[K:]) * inv_ref[0:1]
    end_ref[...] = end
    tendency = jnp.where(lane < COLS, end - mean, 0.0)
    sent = jnp.dot(back_ref[...], tendency, precision=HIGHEST, preferred_element_type=F32)
    edge = edge_rows(
        out_ref[:, 0:128], out_ref[:, CELLS - 128 :], end[:, 0:1], end[:, COLS - 1 : COLS]
    )
    for s in range(SEGS):
        send_ref[s, 0:16, :] = sent[16 * s : 16 * s + 16]
        send_ref[s, 16:24, :] = edge


def outer(seg, halo_block, base, clouds, profile, halo, perm, back, mean, inv, col, diffusivity, wind, mixing):
    ends = CELLS // 256 - 1
    full = lambda shape: pl.BlockSpec(shape, lambda i, seg: (0,) * len(shape))
    return pl.pallas_call(
        outer_kernel,
        grid_spec=pltpu.PrefetchScalarGridSpec(
            num_scalar_prefetch=1,
            grid=(1,),
            in_specs=[
                ANY_SPEC,
                pl.BlockSpec((K, 256), lambda i, seg: (0, 0)),
                pl.BlockSpec((K, 256), lambda i, seg: (0, ends)),
                full((SEGS, 16, 128)),
                pl.BlockSpec((SEGS, 24, 128), lambda i, seg: (seg[1] * halo_block, 0, 0)),
                full((K, SEGS * 16)),
                full((SEGS * 16, K)),
                full((K, 128)),
                full((8, 128)),
                full((1, CELLS)),
                full((K, 1)),
                full((K, 1)),
                full((K, K)),
            ],
            out_specs=[full((K, CELLS)), full((K, 128)), full((SEGS, 24, 128))],
            scratch_shapes=[
                pltpu.VMEM((K, EXT), F32),
                pltpu.VMEM((K, EXT), F32),
                pltpu.VMEM((K, EXT), F32),
                pltpu.VMEM((1, EXT), jnp.int32),
                pltpu.SemaphoreType.DMA,
            ],
        ),
        out_shape=[
            jax.ShapeDtypeStruct((K, CELLS), F32),
            jax.ShapeDtypeStruct((K, 128), F32),
            jax.ShapeDtypeStruct((SEGS, 24, 128), F32),
        ],
        cost_estimate=pl.CostEstimate(flops=1 << 31, bytes_accessed=24 << 20, transcendentals=0),
        compiler_params=pltpu.CompilerParams(vmem_limit_bytes=26 << 20),
        name="outer",
    )(seg, base, clouds, clouds, profile, halo, perm, back, mean, inv, col, diffusivity, wind, mixing)


def upper(shape):
    return lax.broadcasted_iota(jnp.int32, shape, len(shape) - 2) % 8 < 4


def swap4(x):
    tiles = x.reshape(-1, 8, x.shape[-1])
    return pltpu.roll(tiles, 4, 1).reshape(x.shape)


def dot3(x, table):
    high, low = split(x)
    rows = x.shape[0]
    both = jnp.dot(jnp.concatenate([high, low], axis=0), table[0], preferred_element_type=F32)
    return both[:rows] + both[rows:] + jnp.dot(high, table[1], preferred_element_type=F32)


def dot3_left(table, x):
    high, low = split(x)
    cols = x.shape[1]
    both = jnp.dot(table[0], jnp.concatenate([high, low], axis=1), preferred_element_type=F32)
    return both[:, :cols] + both[:, cols:] + jnp.dot(table[1], high, preferred_element_type=F32)


def received_rows(chunks, table):
    rows = jnp.concatenate(
        [jnp.concatenate([c[s] for s in range(SEGS)], axis=1) for c in chunks], axis=0
    )
    coeffs = dot3(rows, table)
    out = []
    first = upper((8, M))
    for a in range(len(chunks)):
        c = [coeffs[16 * a + 8 * i : 16 * a + 8 * i + 8, :M] for i in range(2)]
        s = [coeffs[16 * a + 8 * i : 16 * a + 8 * i + 8, M:] for i in range(2)]
        out.append(
            [
                jnp.where(first, c[0], swap4(s[0])),
                jnp.where(first, swap4(c[0]), s[0]),
                jnp.where(first, c[1], swap4(s[1])),
            ]
        )
    return out


def weigh(total, factors, rows):
    vort, mix, turn = factors[:, :M], factors[:, M : 2 * M], factors[:, 2 * M :]
    return [
        total[0] + vort * rows[0],
        total[1] + (mix * rows[1] + turn * rows[2]),
        total[2] + (mix * rows[2] - turn * rows[1]),
    ]


def call(kernel, name, args, shapes, scratch=(), prefetch=None, limit=12, specs=None, flops=1 << 28):
    specs = specs or [VMEM_SPEC] * len(args)
    common = dict(
        out_shape=shapes,
        name=name,
        cost_estimate=pl.CostEstimate(flops=flops, bytes_accessed=6 << 20, transcendentals=0),
        compiler_params=pltpu.CompilerParams(vmem_limit_bytes=limit << 20),
    )
    outs = [VMEM_SPEC] * len(shapes)
    if prefetch is None:
        return pl.pallas_call(
            kernel, in_specs=specs, out_specs=outs, scratch_shapes=list(scratch), **common
        )(*args)
    return pl.pallas_call(
        kernel,
        grid_spec=pltpu.PrefetchScalarGridSpec(
            num_scalar_prefetch=1, grid=(), in_specs=specs, out_specs=outs,
            scratch_shapes=list(scratch),
        ),
        **common,
    )(prefetch, *args)


def rows_kernel(grid_ref, table, rows_ref, lines):
    for v in range(3):
        for j in range(LAT_DEV):
            for l in range(4):
                at = v * 48 + 4 * j + l
                lines[at : at + 1, :] = grid_ref[j, 3 * l + v : 3 * l + v + 1, :]
    coeffs = dot3(lines[...], table)
    cos, sin = coeffs[:, :M], coeffs[:, M:]
    first = upper((144, M))
    even = jnp.where(first, cos, swap4(sin))
    odd = jnp.where(first, swap4(cos), sin)
    for v in range(3):
        for i in range(6):
            at = v * 48 + 8 * i
            rows_ref[v, 2 * i] = even[at : at + 8]
            rows_ref[v, 2 * i + 1] = odd[at : at + 8]
        for j in range(LAT_DEV, 16):
            rows_ref[v, j] = jnp.zeros((8, M), F32)


def base_kernel(factors, rows_ref, mine_ref, others_ref):
    def channel(c, _):
        for half, out in ((0, mine_ref), (16, others_ref)):
            total = [jnp.zeros((8, M), F32)] * 3
            for j in range(LAT_DEV):
                total = weigh(
                    total, factors[c + half, j : j + 1, :], [rows_ref[v, j] for v in range(3)]
                )
            for v in range(3):
                out[c, 8 * v : 8 * v + 8, :] = total[v]
        return 0

    lax.fori_loop(0, 16, channel, 0)


def parts_kernel(got_ref, table, base_ref, more_ref, factors, parts_ref, pair_ref):
    pair = received_rows([got_ref[b, :, 0:16, :] for b in range(2)], table)
    for b in range(2):
        for v in range(3):
            pair_ref[b, v] = pair[b][v]
    for c in range(16):
        total = [
            base_ref[c, 8 * v : 8 * v + 8, :] + more_ref[c, 8 * v : 8 * v + 8, :] for v in range(3)
        ]
        for b in range(2):
            total = weigh(total, factors[c, b : b + 1, :], pair[b])
        for v in range(3):
            parts_ref[c, 8 * v : 8 * v + 8, :] = total[v]


def profile_kernel(parts_ref, table, out_ref):
    total = parts_ref[0]
    for c in range(1, 16):
        total = total + parts_ref[c]
    a, b, c = total[0:8], total[8:16], total[16:24]
    first = upper((8, M))
    cos = jnp.concatenate([jnp.where(first, a, swap4(b)), c], axis=0)
    sin = jnp.concatenate([jnp.where(first, swap4(a), b), swap4(c)], axis=0)
    lines = dot3(jnp.concatenate([cos, sin], axis=1), table)
    for s in range(SEGS):
        out_ref[s] = lines[:, 128 * s : 128 * s + 128]


def spread_kernel(info, rows_ref, pair_ref, send_ref, held):
    for h in range(2):
        held[h] = rows_ref[:, :, :, 128 * h : 128 * h + 128].reshape(384, 128)
        for v in range(3):
            at = pl.ds(pl.multiple_of((v * 16 + info[2]) * 8, 8), 8)
            held[h, at, :] += pair_ref[info[1], v, :, 128 * h : 128 * h + 128]
    for u in range(8):
        for h in range(2):
            send_ref[2 * u + h] = held[h, pl.ds(u, 48, stride=8), :]


def settle_kernel(info, mine_ref, others_ref, to_spec, from_spec, twice, out_ref):
    core, half = info[1], info[3]

    def columns(ref):
        return jnp.concatenate(
            [ref[:, 16 * v : 16 * v + 16, :].reshape(256, 128) for v in range(3)], axis=1
        )

    spec = dot3_left([to_spec[0, core], to_spec[1, core]], columns(mine_ref)) + dot3_left(
        [to_spec[0, 1 - core], to_spec[1, 1 - core]], columns(others_ref)
    )
    vort, div, geo = spec[:, :128], spec[:, 128:256], spec[:, 256:]
    f0, f1, f2 = twice[half, 0], twice[half, 1], twice[half, 2]
    spec = jnp.concatenate([f0 * vort, f1 * div + f2 * geo, f1 * geo - f2 * div], axis=1)
    back = dot3_left([from_spec[0, core], from_spec[1, core]], spec)
    for v in range(3):
        out_ref[:, 16 * v : 16 * v + 16, :] = back[:, 128 * v : 128 * v + 128].reshape(16, 16, 128)


def last_kernel(got_ref, table, out_ref):
    rows = received_rows([got_ref[:, 0:16, :]], table)[0]
    line = jnp.concatenate(rows, axis=0)
    for c in range(16):
        out_ref[c] = line


def add_channels(factors, half, from_ref, held):
    def row_pair(i, _):
        for h in range(2):
            j = 2 * i + h
            total = [held[v, j] for v in range(3)]
            for c in range(16):
                total = weigh(
                    total,
                    factors[c + half, pl.ds(j, 1), :],
                    [from_ref[c, 8 * v : 8 * v + 8, :] for v in range(3)],
                )
            for v in range(3):
                held[v, j] = total[v]
        return 0

    lax.fori_loop(0, LAT_DEV // 2, row_pair, 0)


def gather_kernel(got_ref, factors, from_ref, held, flat):
    for u in range(8):
        for h in range(2):
            flat[h, pl.ds(u, 48, stride=8), :] = got_ref[2 * u + h]
    for h in range(2):
        held[:, :, :, 128 * h : 128 * h + 128] = flat[h].reshape(3, 16, 8, 128)
    add_channels(factors, 0, from_ref, held)


def finish_kernel(part_ref, factors, from_ref, table, out_ref, held):
    held[...] = part_ref[...]
    add_channels(factors, 16, from_ref, held)
    first = upper((8, M))
    cos, sin = [], []
    for v in range(3):
        for i in range(6):
            even, odd = held[v, 2 * i], held[v, 2 * i + 1]
            cos.append(jnp.where(first, even, swap4(odd)))
            sin.append(jnp.where(first, swap4(even), odd))
    rows = jnp.concatenate(
        [jnp.concatenate(cos, axis=0), jnp.concatenate(sin, axis=0)], axis=1
    )
    lines = dot3(rows, table)
    for v in range(3):
        for j in range(LAT_DEV):
            for l in range(4):
                at = v * 48 + 4 * j + l
                out_ref[j, 3 * l + v : 3 * l + v + 1, :] = lines[at : at + 1]


def shape(*dims):
    return jax.ShapeDtypeStruct(dims, F32)


def rows_exchange(x):
    return lax.all_to_all(x, "lat", 0, 0, axis_index_groups=ROW_GROUPS, tiled=True)


def core_swap(x):
    return lax.ppermute(x, "lat", CORE_SWAP)


def shards(atmosphere, cloud_state, channel_lat, cell_column, channel_wind, diffusivity, mixing):
    tab = {name: jnp.asarray(value) for name, value in tables().items()}
    natural, grouped = permutations()
    lat = lax.axis_index("lat").astype(jnp.int32)
    seg = lax.axis_index("seg").astype(jnp.int32)
    core = lat % 2
    chip = lat // 2
    offset = channel_lat - lat * LAT_DEV
    info = jnp.stack((seg, core, offset[0], chip % 2))
    clouds = cloud_state[0]
    col = cell_column
    wind = channel_wind.reshape(K, 1)
    diff = diffusivity.reshape(K, 1)

    first_send = prepare(offset, atmosphere, clouds, col)
    first_got = lax.all_to_all(first_send, "seg", 0, 0, tiled=True)
    channel_lat, grid, first_send = lax.optimization_barrier((channel_lat, atmosphere, first_send))

    own_position = jnp.broadcast_to(channel_lat.astype(F32)[None, :], (1, 128))
    partner_position = core_swap(own_position)
    positions = rows_exchange(
        jnp.broadcast_to(
            jnp.concatenate((own_position, partner_position), axis=0)[None], (16, 2, 128)
        )
    )[:, :, 0]
    pair_positions = jnp.stack((own_position[0, 0], partner_position[0, 0]))
    pair_positions = jnp.where(core == 0, pair_positions, pair_positions[::-1])
    wanted = jnp.concatenate((positions[:, 0], positions[:, 1], pair_positions))
    picks = (wanted.astype(jnp.int32)[:, None] == jnp.arange(NLAT, dtype=jnp.int32)[None, :])
    basis = jnp.dot(picks.astype(F32), tab["basis"], precision=HIGHEST)
    here = lax.dynamic_slice_in_dim(tab["basis"], lat * LAT_DEV, LAT_DEV, axis=0)
    here = jnp.pad(here, ((0, 4), (0, 0)))
    pair = jnp.pad(basis[32:], ((0, 6), (0, 0)))
    products = (basis[:32, None] * here[None]).reshape(32 * 16, NT)
    factors = jnp.dot(products, tab["row_weights"], precision=HIGH).reshape(32, 16, 3 * M)
    products = (basis[:16, None] * pair[None]).reshape(16 * 8, NT)
    pair_factors = jnp.dot(products, tab["row_weights"], precision=HIGH).reshape(16, 8, 3 * M)

    base, mean, inv = inner(clouds, col, diff, wind, mixing, True)

    rows = call(
        rows_kernel, "rows", (grid, tab["forward"]), [shape(3, 16, 8, M)],
        scratch=[pltpu.VMEM((144, NLON), F32)],
    )[0]
    base_mine, base_others = call(
        base_kernel, "base", (factors, rows), [shape(16, 24, M), shape(16, 24, M)]
    )
    base_more = core_swap(base_others)

    clouds, mean_1, send = outer(
        info, 0, base, clouds, first_got, first_got, jnp.asarray(natural), jnp.asarray(grouped.T.copy()),
        mean, inv, col, diff, wind, mixing,
    )
    got = lax.all_to_all(
        jnp.concatenate((send, send), axis=0), ("lat", "seg"), 0, 0,
        axis_index_groups=CHIP_GROUPS, tiled=True,
    )
    base = inner(clouds, col, diff, wind, mixing, False)
    parts, pair_rows = call(
        parts_kernel, "parts",
        (got.reshape(2, SEGS, 24, 128), tab["forward_seg"], base_mine, base_more, pair_factors),
        [shape(16, 24, M), shape(2, 3, 8, M)],
    )
    parts = rows_exchange(parts)
    profile = call(
        profile_kernel, "profile", (parts, tab["inverse_seg"]), [shape(SEGS, 16, 128)]
    )[0]
    profile = lax.all_to_all(profile, "seg", 0, 0, tiled=True)

    spread = call(
        spread_kernel, "spread", (rows, pair_rows), [shape(16, 48, 128)],
        scratch=[pltpu.VMEM((2, 384, 128), F32)], prefetch=info,
    )[0]
    spec_mine = rows_exchange(spread)
    spec_others = core_swap(spec_mine)
    settled = call(
        settle_kernel, "settle",
        (spec_mine, spec_others, tab["to_spec"], tab["from_spec"], tab["twice"]),
        [shape(16, 48, 128)], prefetch=info,
    )[0]
    settled = rows_exchange(settled)

    clouds, _, send = outer(
        info, 1, base, clouds, profile, got, jnp.asarray(grouped), jnp.asarray(grouped.T.copy()),
        mean_1, inv, col, diff, wind, mixing,
    )
    got = lax.all_to_all(send, "seg", 0, 0, tiled=True)
    from_mine = rows_exchange(
        call(last_kernel, "last", (got, tab["forward_seg"]), [shape(16, 24, M)])[0]
    )
    from_others = core_swap(from_mine)
    part = call(
        gather_kernel, "gather", (settled, factors, from_mine), [shape(3, 16, 8, M)],
        scratch=[pltpu.VMEM((2, 384, 128), F32)],
    )[0]
    grid = call(
        finish_kernel, "finish", (part, factors, from_others, tab["inverse"]),
        [shape(LAT_DEV, KD, NLON)], scratch=[pltpu.VMEM((3, 16, 8, M), F32)],
    )[0]
    return grid, clouds[None]


def solution(mesh):
    placed = (
        P("lat", "seg", None),
        P("lat", None, "seg"),
        P("lat"),
        P("lat", "seg"),
        P("lat", None),
        P(),
        P(),
    )
    return jax.shard_map(
        shards,
        mesh=mesh,
        in_specs=placed,
        out_specs=(P("lat", "seg", None), P("lat", None, "seg")),
        check_vma=False,
    )
```

```python
import ml_dtypes
import numpy as np

import jax
import jax.numpy as jnp
from jax import lax
from jax.experimental import pallas as pl
from jax.experimental.pallas import tpu as pltpu
from jax.sharding import PartitionSpec as P

NLON = 768
M = 256
NT = 256
NLAT = 384
LAT_DEV = 12
K = 96
KD = 12
COLS = 96
CELLS = 6144
LATS = 32
SEGS = 8
TILE = 256
EXT = CELLS + 512
RELAXATION = 0.5
MIXING_RATE = 0.3
DAMPING = 0.2
COUPLING = 2.0
F32 = jnp.float32
BF16 = jnp.bfloat16
HIGHEST = lax.Precision.HIGHEST
HIGH = lax.Precision.HIGH

ROW_GROUPS = [[2 * q + b for q in range(16)] for b in range(2)]
CORE_SWAP = [(i, i ^ 1) for i in range(LATS)]


def tables():
    m = np.arange(M)
    x = np.arange(NLON)
    angles = 2.0 * np.pi * ((m[:, None] * x[None, :]) % NLON) / NLON
    waves = np.stack([np.cos(angles), np.sin(angles)])
    sigma = np.where(m == 0, 1.0, 2.0)
    inverse = (waves * sigma[None, :, None]).reshape(2 * M, NLON)
    forward = (waves / NLON).reshape(2 * M, NLON).T
    forward_seg = np.zeros((SEGS, 128, 2 * M))
    forward_seg[:, :COLS] = forward.reshape(SEGS, COLS, 2 * M)
    inverse_seg = np.zeros((2 * M, SEGS, 128))
    for s in range(SEGS):
        inverse_seg[:, s, : COLS + 1] = inverse[:, (COLS * s + np.arange(COLS + 1)) % NLON]
        inverse_seg[:, s, COLS + 1] = inverse[:, (COLS * s - 1) % NLON]
    n = np.arange(NT)
    j = np.arange(NLAT)
    basis = np.cos(np.pi * ((n[:, None] * (2 * j[None, :] + 1)) % (4 * NLAT)) / (2 * NLAT))
    weights = np.where(n == 0, 1.0, 2.0) / NLAT
    size = (m[None, :] ** 2 + n[:, None] ** 2) / (NT * NT)
    damping = 1.0 + size * size
    coupling = COUPLING * size
    det = damping**2 + coupling**2
    keep = (m[None, :] + n[:, None] < NT).astype(np.float64)
    update = np.stack([keep / damping, keep * damping / det, keep * coupling / det])
    twice = np.stack(
        [
            keep / damping**2,
            keep * (damping**2 - coupling**2) / det**2,
            keep * 2.0 * damping * coupling / det**2,
        ]
    )
    row_weights = np.transpose(update * weights[None, :, None], (1, 0, 2)).reshape(NT, 3 * M)
    parity = basis.reshape(NT, 16, 2, LAT_DEV)
    spread = np.zeros((2, NT, 16, 16))
    spread[:, :, :, :LAT_DEV] = np.transpose(parity, (2, 0, 1, 3))
    spread = spread.reshape(2, NT, 256)
    f = np.float32
    return dict(
        forward=pair_of(forward),
        inverse=pair_of(inverse),
        forward_seg=pair_of(forward_seg.reshape(SEGS * 128, 2 * M)),
        inverse_seg=pair_of(inverse_seg.reshape(2 * M, SEGS * 128)),
        to_spec=pair_of(spread * weights[None, :, None]),
        from_spec=pair_of(np.transpose(spread, (0, 2, 1))),
        basis=np.ascontiguousarray(basis.T).astype(f),
        once=np.ascontiguousarray(np.transpose(update.reshape(3, NT, 2, 128), (2, 0, 1, 3))).astype(f),
        twice=np.ascontiguousarray(np.transpose(twice.reshape(3, NT, 2, 128), (2, 0, 1, 3))).astype(f),
        row_weights=row_weights.astype(f),
    )


def pair_of(x):
    x = x.astype(np.float32)
    high = x.astype(ml_dtypes.bfloat16)
    low = (x - high.astype(np.float32)).astype(ml_dtypes.bfloat16)
    return np.stack((high, low))


def permutations():
    natural = np.zeros((K, SEGS * 16), np.float32)
    grouped = np.zeros((K, SEGS * 16), np.float32)
    for s in range(SEGS):
        for i in range(KD):
            natural[KD * s + i, 16 * s + i] = 1.0
            grouped[KD * s + i, 16 * s + (i % 3) * 4 + i // 3] = 1.0
    return natural, grouped


def lanes_of(shape):
    return lax.broadcasted_iota(jnp.int32, shape, len(shape) - 1)


def split(x):
    high = x.astype(BF16)
    low = (x - high.astype(F32)).astype(BF16)
    return high, low


def mixing_block(mixing):
    high, low = split(MIXING_RATE * mixing)
    return jnp.concatenate(
        [jnp.concatenate([high, high], axis=1), jnp.concatenate([low, low], axis=1)], axis=0
    )


def substep_tile(window, mix, diffusivity, wind):
    width = window.shape[1]
    center = window[:, 128 : width - 128]
    right = pltpu.roll(window, width - 1, 1)[:, 128 : width - 128]
    left = pltpu.roll(window, 1, 1)[:, 128 : width - 128]
    high, low = split(center)
    mixed = jnp.dot(mix, jnp.concatenate([high, low], axis=0), preferred_element_type=F32)
    return (
        center
        + diffusivity * (right - 2.0 * center + left)
        - 0.5 * wind * (right - left)
        + (mixed[:K] + mixed[K:])
        - DAMPING * jnp.tanh(center)
    )


def column_hits(col):
    ids = lax.broadcasted_iota(jnp.int32, (128, col.shape[1]), 0)
    return jnp.where(ids == col, 1.0, 0.0).astype(BF16)


def edge_rows(first, last, mean_first, mean_last):
    lane = lanes_of((K, 128))
    edge = jnp.where(
        lane < 3,
        first,
        jnp.where(
            lane < 6, pltpu.roll(last, 6, 1), jnp.where(lane == 6, mean_first, mean_last)
        ),
    )
    padded = jnp.concatenate([edge, jnp.zeros((32, 128), F32)], axis=0)
    return padded.T[:8]


def prepare_kernel(off_ref, row_ref, first_ref, last_ref, colf_ref, coll_ref, send_ref):
    del off_ref
    row = row_ref[0]
    lane = lanes_of((KD, 128))
    hit_first = jnp.where(colf_ref[...] == 0, 1.0, 0.0)
    hit_last = jnp.where(coll_ref[...] == COLS - 1, 1.0, 0.0)
    first, last = first_ref[...], last_ref[...]
    mean_first = jnp.sum(first * hit_first, axis=1, keepdims=True) / jnp.sum(
        hit_first, axis=1, keepdims=True
    )
    mean_last = jnp.sum(last * hit_last, axis=1, keepdims=True) / jnp.sum(
        hit_last, axis=1, keepdims=True
    )
    edge = edge_rows(first, last, mean_first, mean_last)
    for s in range(SEGS):
        own = pltpu.roll(row, (NLON - COLS * s) % NLON, 1)[:, :128]
        before = pltpu.roll(row, (COLS + 1 - (COLS * s - 1)) % NLON, 1)[:, :128]
        chunk = jnp.where(lane <= COLS, own, jnp.where(lane == COLS + 1, before, 0.0))
        send_ref[s, 0:KD, :] = chunk
        send_ref[s, KD:16, :] = jnp.zeros((16 - KD, 128), F32)
        send_ref[s, 16:24, :] = edge


def prepare(offset, atmosphere, clouds, col):
    last = CELLS // 128 - 1
    return pl.pallas_call(
        prepare_kernel,
        grid_spec=pltpu.PrefetchScalarGridSpec(
            num_scalar_prefetch=1,
            grid=(1,),
            in_specs=[
                pl.BlockSpec((1, KD, NLON), lambda i, off: (off[0], 0, 0)),
                pl.BlockSpec((K, 128), lambda i, off: (0, 0)),
                pl.BlockSpec((K, 128), lambda i, off: (0, last)),
                pl.BlockSpec((1, 128), lambda i, off: (0, 0)),
                pl.BlockSpec((1, 128), lambda i, off: (0, last)),
            ],
            out_specs=pl.BlockSpec((SEGS, 24, 128), lambda i, off: (0, 0, 0)),
        ),
        out_shape=jax.ShapeDtypeStruct((SEGS, 24, 128), F32),
        name="prepare",
    )(offset, atmosphere, clouds, clouds, col, col)


def column_of(row):
    size = row.shape[1]
    diagonal = lax.broadcasted_iota(jnp.int32, (size, size), 0) == lanes_of((size, size))
    return jnp.sum(jnp.where(diagonal, row, 0.0), axis=1, keepdims=True)


def inner_kernel(with_mean, *refs):
    if with_mean:
        c_ref, col_ref, diff_ref, wind_ref, mixing_ref, base_ref, ends_ref, mean_ref, inv_ref = refs
    else:
        c_ref, diff_ref, wind_ref, mixing_ref, base_ref, ends_ref = refs
    zeros = jnp.zeros((K, 128), F32)
    mix = mixing_block(mixing_ref[...])
    diffusivity, wind = column_of(diff_ref[...]), column_of(wind_ref[...])
    ends_ref[:, 0:256] = c_ref[:, 0:256]
    ends_ref[:, 256:512] = c_ref[:, CELLS - 256 :]
    total = jnp.zeros((2 * K + 16, 128), F32)
    for start in range(0, CELLS, TILE):
        window = c_ref[:, max(start - 128, 0) : min(start + TILE + 128, CELLS)]
        if start == 0:
            window = jnp.concatenate([zeros, window], axis=1)
        if start + TILE == CELLS:
            window = jnp.concatenate([window, zeros], axis=1)
        base_ref[:, start : start + TILE] = substep_tile(window, mix, diffusivity, wind)
        if with_mean:
            hits = column_hits(col_ref[:, start : start + TILE])
            high, low = split(window[:, 128 : 128 + TILE])
            rows = jnp.concatenate([high, low, jnp.ones((16, TILE), BF16)], axis=0)
            total = total + lax.dot_general(
                rows, hits, (((1,), (1,)), ((), ())), preferred_element_type=F32
            )
    if with_mean:
        counts = total[2 * K : 2 * K + 8]
        inv = jnp.where(counts > 0.0, 1.0 / jnp.maximum(counts, 1.0), 0.0)
        inv_ref[...] = inv
        mean_ref[...] = (total[:K] + total[K : 2 * K]) * inv[0:1]


VMEM_SPEC = pl.BlockSpec(memory_space=pltpu.VMEM)


def inner(clouds, col, diffusivity, wind, mixing, with_mean):
    args = [clouds] + ([col] if with_mean else []) + [diffusivity, wind, mixing]
    shapes = [jax.ShapeDtypeStruct((K, CELLS), F32), jax.ShapeDtypeStruct((K, 512), F32)]
    if with_mean:
        shapes += [jax.ShapeDtypeStruct((K, 128), F32), jax.ShapeDtypeStruct((8, 128), F32)]
    return pl.pallas_call(
        lambda *refs: inner_kernel(with_mean, *refs),
        in_specs=[VMEM_SPEC] * len(args),
        out_specs=[VMEM_SPEC] * len(shapes),
        out_shape=shapes,
        cost_estimate=pl.CostEstimate(flops=1 << 10, bytes_accessed=1 << 10, transcendentals=0),
        compiler_params=pltpu.CompilerParams(vmem_limit_bytes=6 << 20),
        name="inner",
    )(*args)


def outer_kernel(
    info, base_ref, ends_ref, prof_ref, halo_ref, perm_ref, back_ref, mean_ref, inv_ref,
    col_ref, diff_ref, wind_ref, mixing_ref, out_ref, end_ref, send_ref, ext1, ext2, force,
):
    seg = info[0]
    lane = lanes_of((K, 128))
    zeros = jnp.zeros((K, 128), F32)
    mix = mixing_block(mixing_ref[...])
    diffusivity, wind = column_of(diff_ref[...]), column_of(wind_ref[...])

    from_left = halo_ref[lax.rem(seg + SEGS - 1, SEGS), 16:24, :]
    from_right = halo_ref[lax.rem(seg + 1, SEGS), 16:24, :]
    edges = jnp.concatenate([from_left, from_right, jnp.zeros((112, 128), F32)], axis=0).T[:K]
    left_tile = jnp.where(lane >= 125, pltpu.roll(edges, 122, 1), 0.0)
    right_tile = jnp.where(lane < 3, pltpu.roll(edges, 120, 1), 0.0)
    mean = mean_ref[...]
    mean_all = jnp.where(
        lane < COLS,
        mean,
        jnp.where(
            lane == COLS,
            pltpu.roll(edges, COLS - 14, 1),
            jnp.where(lane == COLS + 1, pltpu.roll(edges, COLS + 1 - 7, 1), 0.0),
        ),
    )
    profile = jnp.dot(
        perm_ref[...],
        prof_ref[:, 0:16, :].reshape(SEGS * 16, 128),
        precision=HIGHEST,
        preferred_element_type=F32,
    )
    pulled = jnp.where(lane < COLS + 2, RELAXATION * (profile - mean_all), 0.0)
    pulled = jnp.concatenate(split(pulled), axis=1)

    ext1[:, 0:128] = zeros
    ext1[:, EXT - 128 :] = zeros
    left_col = jnp.full((1, 128), COLS + 1, jnp.int32)
    right_col = jnp.full((1, 128), COLS, jnp.int32)
    for at in range(128, EXT - 128, TILE):
        cell = at - 256
        if cell < 0:
            window = jnp.concatenate([zeros, left_tile, ends_ref[:, 0:256]], axis=1)
            value = substep_tile(window, mix, diffusivity, wind)
            col = jnp.concatenate([left_col, col_ref[:, 0:128]], axis=1)
        elif cell + TILE > CELLS:
            window = jnp.concatenate([ends_ref[:, 256:512], right_tile, zeros], axis=1)
            value = substep_tile(window, mix, diffusivity, wind)
            col = jnp.concatenate([col_ref[:, CELLS - 128 :], right_col], axis=1)
        else:
            value = base_ref[:, cell : cell + TILE]
            col = col_ref[:, cell : cell + TILE]
        hits = column_hits(col)
        forced = jnp.dot(
            pulled, jnp.concatenate([hits, hits], axis=0), preferred_element_type=F32
        )
        force[:, at : at + TILE] = forced
        ext1[:, at : at + TILE] = value + forced

    for at in range(128, EXT - 128, TILE):
        window = ext1[:, at - 128 : at + TILE + 128]
        ext2[:, at : at + TILE] = (
            substep_tile(window, mix, diffusivity, wind) + force[:, at : at + TILE]
        )

    total = jnp.zeros((2 * K, 128), F32)
    for cell in range(0, CELLS, TILE):
        at = cell + 256
        window = ext2[:, at - 128 : at + TILE + 128]
        value = substep_tile(window, mix, diffusivity, wind) + force[:, at : at + TILE]
        out_ref[:, cell : cell + TILE] = value
        hits = column_hits(col_ref[:, cell : cell + TILE])
        rows = jnp.concatenate(split(value), axis=0)
        total = total + lax.dot_general(
            rows, hits, (((1,), (1,)), ((), ())), preferred_element_type=F32
        )
    end = (total[:K] + total[K:]) * inv_ref[0:1]
    end_ref[...] = end
    tendency = jnp.where(lane < COLS, end - mean, 0.0)
    sent = jnp.dot(back_ref[...], tendency, precision=HIGHEST, preferred_element_type=F32)
    edge = edge_rows(
        out_ref[:, 0:128], out_ref[:, CELLS - 128 :], end[:, 0:1], end[:, COLS - 1 : COLS]
    )
    for s in range(send_ref.shape[0]):
        send_ref[s, 0:16, :] = sent[16 * (s % SEGS) : 16 * (s % SEGS) + 16]
        send_ref[s, 16:24, :] = edge


def outer(info, *args):
    return call(
        outer_kernel, "outer", args, [shape(K, CELLS), shape(K, 128), shape(SEGS, 24, 128)],
        scratch=[pltpu.VMEM((K, EXT), F32)] * 3, prefetch=info, limit=14,
    )


def upper(shape):
    return lax.broadcasted_iota(jnp.int32, shape, len(shape) - 2) % 8 < 4


def swap4(x):
    tiles = x.reshape(-1, 8, x.shape[-1])
    return pltpu.roll(tiles, 4, 1).reshape(x.shape)


def dot3(x, table):
    high, low = split(x)
    rows = x.shape[0]
    both = jnp.dot(jnp.concatenate([high, low], axis=0), table[0], preferred_element_type=F32)
    return both[:rows] + both[rows:] + jnp.dot(high, table[1], preferred_element_type=F32)


def dot3_left(table, x):
    high, low = split(x)
    cols = x.shape[1]
    both = jnp.dot(table[0], jnp.concatenate([high, low], axis=1), preferred_element_type=F32)
    return both[:, :cols] + both[:, cols:] + jnp.dot(table[1], high, preferred_element_type=F32)


def received_rows(chunks, table):
    rows = jnp.concatenate(
        [jnp.concatenate([c[s] for s in range(SEGS)], axis=1) for c in chunks], axis=0
    )
    coeffs = dot3(rows, table)
    out = []
    first = upper((8, M))
    for a in range(len(chunks)):
        c = [coeffs[16 * a + 8 * i : 16 * a + 8 * i + 8, :M] for i in range(2)]
        s = [coeffs[16 * a + 8 * i : 16 * a + 8 * i + 8, M:] for i in range(2)]
        out.append(
            [
                jnp.where(first, c[0], swap4(s[0])),
                jnp.where(first, swap4(c[0]), s[0]),
                jnp.where(first, c[1], swap4(s[1])),
            ]
        )
    return out


def weigh(total, factors, rows):
    vort, mix, turn = factors[:, :M], factors[:, M : 2 * M], factors[:, 2 * M :]
    return [
        total[0] + vort * rows[0],
        total[1] + (mix * rows[1] + turn * rows[2]),
        total[2] + (mix * rows[2] - turn * rows[1]),
    ]


def call(kernel, name, args, shapes, scratch=(), prefetch=None, limit=8, specs=None):
    specs = specs or [VMEM_SPEC] * len(args)
    common = dict(
        out_shape=shapes,
        name=name,
        cost_estimate=pl.CostEstimate(flops=1 << 10, bytes_accessed=1 << 10, transcendentals=0),
        compiler_params=pltpu.CompilerParams(vmem_limit_bytes=limit << 20),
    )
    outs = [VMEM_SPEC] * len(shapes)
    if prefetch is None:
        return pl.pallas_call(
            kernel, in_specs=specs, out_specs=outs, scratch_shapes=list(scratch), **common
        )(*args)
    return pl.pallas_call(
        kernel,
        grid_spec=pltpu.PrefetchScalarGridSpec(
            num_scalar_prefetch=1, grid=(), in_specs=specs, out_specs=outs,
            scratch_shapes=list(scratch),
        ),
        **common,
    )(prefetch, *args)


def rows_kernel(grid_ref, table, rows_ref, lines):
    for v in range(3):
        for j in range(LAT_DEV):
            for l in range(4):
                at = v * 48 + 4 * j + l
                lines[at : at + 1, :] = grid_ref[j, 3 * l + v : 3 * l + v + 1, :]
    coeffs = dot3(lines[...], table)
    cos, sin = coeffs[:, :M], coeffs[:, M:]
    first = upper((144, M))
    even = jnp.where(first, cos, swap4(sin))
    odd = jnp.where(first, swap4(cos), sin)
    for v in range(3):
        for i in range(6):
            at = v * 48 + 8 * i
            rows_ref[v, 2 * i] = even[at : at + 8]
            rows_ref[v, 2 * i + 1] = odd[at : at + 8]
        for j in range(LAT_DEV, 16):
            rows_ref[v, j] = jnp.zeros((8, M), F32)


def spread_kernel(info, got_ref, table, rows_ref, send_ref, held):
    forced = received_rows([got_ref[:, 0:16, :]], table)[0]
    for h in range(2):
        held[h] = rows_ref[:, :, :, 128 * h : 128 * h + 128].reshape(384, 128)
        for v in range(3):
            at = pl.ds(pl.multiple_of((v * 16 + info[2]) * 8, 8), 8)
            held[h, at, :] += forced[v][:, 128 * h : 128 * h + 128]
        held[h, LAT_DEV * 8 : LAT_DEV * 8 + 8, :] = jnp.full((8, 128), info[2], jnp.int32).astype(F32)
    for u in range(8):
        for h in range(2):
            send_ref[2 * u + h] = held[h, pl.ds(u, 48, stride=8), :]


def settle_kernel(info, mine_ref, others_ref, to_spec, from_spec, once, twice, out_ref):
    core, half = info[1], info[3]

    def columns(ref):
        return jnp.concatenate(
            [ref[:, 16 * v : 16 * v + 16, :].reshape(256, 128) for v in range(3)], axis=1
        )

    def update(factors, spec):
        vort, div, geo = spec[:, :128], spec[:, 128:256], spec[:, 256:]
        f0, f1, f2 = factors[half, 0], factors[half, 1], factors[half, 2]
        return jnp.concatenate([f0 * vort, f1 * div + f2 * geo, f1 * geo - f2 * div], axis=1)

    spec = dot3_left([to_spec[0, core], to_spec[1, core]], columns(mine_ref)) + dot3_left(
        [to_spec[0, 1 - core], to_spec[1, 1 - core]], columns(others_ref)
    )
    table = [from_spec[0, core], from_spec[1, core]]
    back = dot3_left(table, update(twice, spec))
    offsets = mine_ref[:, LAT_DEV, :][:, 0:1].astype(jnp.int32)
    wanted = 16 * lax.broadcasted_iota(jnp.int32, (16, 256), 0) + offsets
    picks = jnp.where(lanes_of((16, 256)) == wanted, 1.0, 0.0).astype(BF16)
    picked = [jnp.dot(picks, t, preferred_element_type=F32).astype(BF16) for t in table]
    channels = dot3_left(picked, update(once, spec))
    for v in range(3):
        out_ref[:, 16 * v : 16 * v + 16, :] = back[:, 128 * v : 128 * v + 128].reshape(16, 16, 128)
        for q in range(16):
            out_ref[q, 16 * v + LAT_DEV : 16 * v + LAT_DEV + 1, :] = channels[
                q : q + 1, 128 * v : 128 * v + 128
            ]


def profile_kernel(got_ref, table, out_ref, total):
    for v in range(3):
        for u in range(8):
            for h in range(2):
                at = 16 * v + LAT_DEV
                total[8 * v + u : 8 * v + u + 1, 128 * h : 128 * h + 128] = got_ref[
                    2 * u + h, at : at + 1, :
                ]
    a, b, c = total[0:8], total[8:16], total[16:24]
    first = upper((8, M))
    cos = jnp.concatenate([jnp.where(first, a, swap4(b)), c], axis=0)
    sin = jnp.concatenate([jnp.where(first, swap4(a), b), swap4(c)], axis=0)
    lines = dot3(jnp.concatenate([cos, sin], axis=1), table)
    for s in range(SEGS):
        out_ref[s] = lines[:, 128 * s : 128 * s + 128]


def last_kernel(got_ref, table, out_ref):
    rows = received_rows([got_ref[:, 0:16, :]], table)[0]
    line = jnp.concatenate(rows, axis=0)
    for c in range(16):
        out_ref[c] = line


def add_channels(factors, half, from_ref, held):
    def row_pair(i, _):
        for h in range(2):
            j = 2 * i + h
            total = [held[v, j] for v in range(3)]
            for c in range(16):
                total = weigh(
                    total,
                    factors[c + half, pl.ds(j, 1), :],
                    [from_ref[c, 8 * v : 8 * v + 8, :] for v in range(3)],
                )
            for v in range(3):
                held[v, j] = total[v]
        return 0

    lax.fori_loop(0, LAT_DEV // 2, row_pair, 0)


def gather_kernel(got_ref, factors, from_ref, held, flat):
    for u in range(8):
        for h in range(2):
            flat[h, pl.ds(u, 48, stride=8), :] = got_ref[2 * u + h]
    for h in range(2):
        held[:, :, :, 128 * h : 128 * h + 128] = flat[h].reshape(3, 16, 8, 128)
    add_channels(factors, 0, from_ref, held)


def finish_kernel(part_ref, factors, from_ref, table, out_ref, held):
    held[...] = part_ref[...]
    add_channels(factors, 16, from_ref, held)
    first = upper((8, M))
    cos, sin = [], []
    for v in range(3):
        for i in range(6):
            even, odd = held[v, 2 * i], held[v, 2 * i + 1]
            cos.append(jnp.where(first, even, swap4(odd)))
            sin.append(jnp.where(first, swap4(even), odd))
    rows = jnp.concatenate(
        [jnp.concatenate(cos, axis=0), jnp.concatenate(sin, axis=0)], axis=1
    )
    lines = dot3(rows, table)
    for v in range(3):
        for j in range(LAT_DEV):
            for l in range(4):
                at = v * 48 + 4 * j + l
                out_ref[j, 3 * l + v : 3 * l + v + 1, :] = lines[at : at + 1]


def shape(*dims):
    return jax.ShapeDtypeStruct(dims, F32)


def rows_exchange(x):
    return lax.all_to_all(x, "lat", 0, 0, axis_index_groups=ROW_GROUPS, tiled=True)


def core_swap(x):
    return lax.ppermute(x, "lat", CORE_SWAP)


def shards(atmosphere, cloud_state, channel_lat, cell_column, channel_wind, diffusivity, mixing):
    tab = {name: jnp.asarray(value) for name, value in tables().items()}
    natural, grouped = permutations()
    lat = lax.axis_index("lat").astype(jnp.int32)
    seg = lax.axis_index("seg").astype(jnp.int32)
    core = lat % 2
    chip = lat // 2
    offset = channel_lat - lat * LAT_DEV
    info = jnp.stack((seg, core, offset[0], chip % 2))
    clouds = cloud_state[0]
    col = cell_column
    wind = channel_wind
    diff = diffusivity.reshape(1, K)
    spread_table = tab["forward_seg"]
    gather_rows = jnp.asarray(grouped)
    scatter_rows = jnp.asarray(grouped.T.copy())

    send = prepare(offset, atmosphere, clouds, col)
    got = lax.all_to_all(send, "seg", 0, 0, tiled=True)
    grid, state, send = lax.optimization_barrier((atmosphere, clouds, send))
    base, ends, mean, inv = inner(state, col, diff, wind, mixing, True)
    rows = call(
        rows_kernel, "rows", (grid, tab["forward"]), [shape(3, 16, 8, M)],
        scratch=[pltpu.VMEM((144, NLON), F32)],
    )[0]
    clouds, mean_1, send = outer(
        info, base, ends, got, got, jnp.asarray(natural), scatter_rows,
        mean, inv, col, diff, wind, mixing,
    )
    halo = lax.all_to_all(send, "seg", 0, 0, tiled=True)
    base, ends = inner(clouds, col, diff, wind, mixing, False)
    base, ends, halo = lax.optimization_barrier((base, ends, halo))

    spread = call(
        spread_kernel, "spread", (halo, spread_table, rows), [shape(16, 48, 128)],
        scratch=[pltpu.VMEM((2, 384, 128), F32)], prefetch=info,
    )[0]
    spec_mine = rows_exchange(spread)
    spec_others = core_swap(spec_mine)
    settled = call(
        settle_kernel, "settle",
        (spec_mine, spec_others, tab["to_spec"], tab["from_spec"], tab["once"], tab["twice"]),
        [shape(16, 48, 128)], prefetch=info,
    )[0]
    settled = rows_exchange(settled)
    profile = call(
        profile_kernel, "profile", (settled, tab["inverse_seg"]), [shape(SEGS, 16, 128)],
        scratch=[pltpu.VMEM((24, M), F32)],
    )[0]
    profile = lax.all_to_all(profile, "seg", 0, 0, tiled=True)

    numbers = jnp.arange(16, dtype=jnp.int32)
    near = (2 * numbers + core) * LAT_DEV + spec_mine[:, LAT_DEV, 0].astype(jnp.int32)
    far = (2 * numbers + 1 - core) * LAT_DEV + spec_others[:, LAT_DEV, 0].astype(jnp.int32)
    wanted = jnp.concatenate((near, far))
    picks = (wanted[:, None] == jnp.arange(NLAT, dtype=jnp.int32)[None, :]).astype(F32)
    basis = jnp.dot(picks, tab["basis"], precision=HIGHEST)
    here = lax.dynamic_slice_in_dim(tab["basis"], lat * LAT_DEV, LAT_DEV, axis=0)
    here = jnp.pad(here, ((0, 4), (0, 0)))
    products = (basis[:, None] * here[None]).reshape(32 * 16, NT)
    factors = jnp.dot(products, tab["row_weights"], precision=HIGH).reshape(32, 16, 3 * M)

    factors, profile = lax.optimization_barrier((factors, profile))

    clouds, _, send = outer(
        info, base, ends, profile, halo, gather_rows, scatter_rows,
        mean_1, inv, col, diff, wind, mixing,
    )
    got = lax.all_to_all(send, "seg", 0, 0, tiled=True)
    from_mine = rows_exchange(
        call(last_kernel, "last", (got, spread_table), [shape(16, 24, M)])[0]
    )
    from_others = core_swap(from_mine)
    part = call(
        gather_kernel, "gather", (settled, factors, from_mine), [shape(3, 16, 8, M)],
        scratch=[pltpu.VMEM((2, 384, 128), F32)],
    )[0]
    grid = call(
        finish_kernel, "finish", (part, factors, from_others, tab["inverse"]),
        [shape(LAT_DEV, KD, NLON)], scratch=[pltpu.VMEM((3, 16, 8, M), F32)],
    )[0]
    return grid, clouds[None]


def solution(mesh):
    placed = (
        P("lat", "seg", None),
        P("lat", None, "seg"),
        P("lat"),
        P("lat", "seg"),
        P("lat", None),
        P(),
        P(),
    )
    return jax.shard_map(
        shards,
        mesh=mesh,
        in_specs=placed,
        out_specs=(P("lat", "seg", None), P("lat", None, "seg")),
        check_vma=False,
    )
```

```python
import ml_dtypes
import numpy as np

import jax
import jax.numpy as jnp
from jax import lax
from jax.experimental import pallas as pl
from jax.experimental.pallas import tpu as pltpu
from jax.sharding import PartitionSpec as P

NLON = 768
M = 256
NT = 256
NLAT = 384
LAT_DEV = 12
K = 96
KD = 12
COLS = 96
CELLS = 6144
LATS = 32
SEGS = 8
TILE = 256
EXT = CELLS + 512
CHUNK = 1024
PIECES = CELLS // CHUNK
RELAXATION = 0.5
MIXING_RATE = 0.3
DAMPING = 0.2
COUPLING = 2.0
F32 = jnp.float32
BF16 = jnp.bfloat16
HIGHEST = lax.Precision.HIGHEST
HIGH = lax.Precision.HIGH

ROW_GROUPS = [[2 * q + b for q in range(16)] for b in range(2)]
CORE_SWAP = [(i, i ^ 1) for i in range(LATS)]


def tables():
    m = np.arange(M)
    x = np.arange(NLON)
    angles = 2.0 * np.pi * ((m[:, None] * x[None, :]) % NLON) / NLON
    waves = np.stack([np.cos(angles), np.sin(angles)])
    sigma = np.where(m == 0, 1.0, 2.0)
    inverse = (waves * sigma[None, :, None]).reshape(2 * M, NLON)
    forward = (waves / NLON).reshape(2 * M, NLON).T
    forward_seg = np.zeros((SEGS, 128, 2 * M))
    forward_seg[:, :COLS] = forward.reshape(SEGS, COLS, 2 * M)
    inverse_seg = np.zeros((2 * M, SEGS, 128))
    for s in range(SEGS):
        inverse_seg[:, s, : COLS + 1] = inverse[:, (COLS * s + np.arange(COLS + 1)) % NLON]
        inverse_seg[:, s, COLS + 1] = inverse[:, (COLS * s - 1) % NLON]
    n = np.arange(NT)
    j = np.arange(NLAT)
    basis = np.cos(np.pi * ((n[:, None] * (2 * j[None, :] + 1)) % (4 * NLAT)) / (2 * NLAT))
    weights = np.where(n == 0, 1.0, 2.0) / NLAT
    size = (m[None, :] ** 2 + n[:, None] ** 2) / (NT * NT)
    damping = 1.0 + size * size
    coupling = COUPLING * size
    det = damping**2 + coupling**2
    keep = (m[None, :] + n[:, None] < NT).astype(np.float64)
    update = np.stack([keep / damping, keep * damping / det, keep * coupling / det])
    twice = np.stack(
        [
            keep / damping**2,
            keep * (damping**2 - coupling**2) / det**2,
            keep * 2.0 * damping * coupling / det**2,
        ]
    )
    row_weights = np.transpose(update * weights[None, :, None], (1, 0, 2)).reshape(NT, 3 * M)
    parity = basis.reshape(NT, 16, 2, LAT_DEV)
    spread = np.zeros((2, NT, 16, 16))
    spread[:, :, :, :LAT_DEV] = np.transpose(parity, (2, 0, 1, 3))
    spread = spread.reshape(2, NT, 256)
    f = np.float32
    return dict(
        forward=pair_of(forward),
        inverse=pair_of(inverse),
        forward_seg=pair_of(forward_seg.reshape(SEGS * 128, 2 * M)),
        inverse_seg=pair_of(inverse_seg.reshape(2 * M, SEGS * 128)),
        to_spec=pair_of(spread * weights[None, :, None]),
        from_spec=pair_of(np.transpose(spread, (0, 2, 1))),
        once=np.ascontiguousarray(np.transpose(update.reshape(3, NT, 2, 128), (2, 0, 1, 3))).astype(f),
        twice=np.ascontiguousarray(np.transpose(twice.reshape(3, NT, 2, 128), (2, 0, 1, 3))).astype(f),
        row_weights=pair_of(row_weights),
    )


def pair_of(x):
    x = x.astype(np.float32)
    high = x.astype(ml_dtypes.bfloat16)
    low = (x - high.astype(np.float32)).astype(ml_dtypes.bfloat16)
    return np.stack((high, low))


def permutations():
    natural = np.zeros((K, SEGS * 16), np.float32)
    grouped = np.zeros((K, SEGS * 16), np.float32)
    for s in range(SEGS):
        for i in range(KD):
            natural[KD * s + i, 16 * s + i] = 1.0
            grouped[KD * s + i, 16 * s + (i % 3) * 4 + i // 3] = 1.0
    return natural, grouped


def lanes_of(shape):
    return lax.broadcasted_iota(jnp.int32, shape, len(shape) - 1)


def split(x):
    high = x.astype(BF16)
    low = (x - high.astype(F32)).astype(BF16)
    return high, low


def mixing_block(mixing):
    high, low = split(MIXING_RATE * mixing)
    return jnp.concatenate(
        [jnp.concatenate([high, high], axis=1), jnp.concatenate([low, low], axis=1)], axis=0
    )


def substep_tile(window, mix, diffusivity, wind):
    width = window.shape[1]
    center = window[:, 128 : width - 128]
    right = pltpu.roll(window, width - 1, 1)[:, 128 : width - 128]
    left = pltpu.roll(window, 1, 1)[:, 128 : width - 128]
    high, low = split(center)
    mixed = jnp.dot(mix, jnp.concatenate([high, low], axis=0), preferred_element_type=F32)
    return (
        center
        + diffusivity * (right - 2.0 * center + left)
        - 0.5 * wind * (right - left)
        + (mixed[:K] + mixed[K:])
        - DAMPING * jnp.tanh(center)
    )


def column_hits(col):
    ids = lax.broadcasted_iota(jnp.int32, (128, col.shape[1]), 0)
    return jnp.where(ids == col, 1.0, 0.0).astype(BF16)


def edge_rows(first, last, mean_first, mean_last):
    lane = lanes_of((K, 128))
    edge = jnp.where(
        lane < 3,
        first,
        jnp.where(
            lane < 6, pltpu.roll(last, 6, 1), jnp.where(lane == 6, mean_first, mean_last)
        ),
    )
    padded = jnp.concatenate([edge, jnp.zeros((32, 128), F32)], axis=0)
    return padded.T[:8]


def place(info):
    lat = info[1]
    return lax.rem(lat, 2), lax.div(lat, 2), info[2] - lat * LAT_DEV


def prepare_kernel(info, row_ref, first_ref, last_ref, colf_ref, coll_ref, send_ref):
    del info
    row = row_ref[0]
    lane = lanes_of((KD, 128))
    hit_first = jnp.where(colf_ref[...] == 0, 1.0, 0.0)
    hit_last = jnp.where(coll_ref[...] == COLS - 1, 1.0, 0.0)
    first, last = first_ref[...], last_ref[...]
    mean_first = jnp.sum(first * hit_first, axis=1, keepdims=True) / jnp.sum(
        hit_first, axis=1, keepdims=True
    )
    mean_last = jnp.sum(last * hit_last, axis=1, keepdims=True) / jnp.sum(
        hit_last, axis=1, keepdims=True
    )
    edge = edge_rows(first, last, mean_first, mean_last)
    for s in range(SEGS):
        own = pltpu.roll(row, (NLON - COLS * s) % NLON, 1)[:, :128]
        before = pltpu.roll(row, (COLS + 1 - (COLS * s - 1)) % NLON, 1)[:, :128]
        chunk = jnp.where(lane <= COLS, own, jnp.where(lane == COLS + 1, before, 0.0))
        send_ref[s, 0:KD, :] = chunk
        send_ref[s, KD:16, :] = jnp.zeros((16 - KD, 128), F32)
        send_ref[s, 16:24, :] = edge


def prepare(info, atmosphere, clouds, col):
    last = CELLS // 128 - 1
    return pl.pallas_call(
        prepare_kernel,
        grid_spec=pltpu.PrefetchScalarGridSpec(
            num_scalar_prefetch=1,
            grid=(1,),
            in_specs=[
                pl.BlockSpec((1, KD, NLON), lambda i, info: (place(info)[2], 0, 0)),
                pl.BlockSpec((K, 128), lambda i, off: (0, 0)),
                pl.BlockSpec((K, 128), lambda i, off: (0, last)),
                pl.BlockSpec((1, 128), lambda i, off: (0, 0)),
                pl.BlockSpec((1, 128), lambda i, off: (0, last)),
            ],
            out_specs=pl.BlockSpec((SEGS, 24, 128), lambda i, off: (0, 0, 0)),
        ),
        out_shape=jax.ShapeDtypeStruct((SEGS, 24, 128), F32),
        name="prepare",
    )(info, atmosphere, clouds, clouds, col, col)


def column_of(row):
    size = row.shape[1]
    diagonal = lax.broadcasted_iota(jnp.int32, (size, size), 0) == lanes_of((size, size))
    return jnp.sum(jnp.where(diagonal, row, 0.0), axis=1, keepdims=True)


def pieces(source, target, sems, shift=0):
    return [
        pltpu.make_async_copy(
            source.at[:, i * CHUNK : (i + 1) * CHUNK],
            target.at[:, shift + i * CHUNK : shift + (i + 1) * CHUNK],
            sems.at[i],
        )
        for i in range(PIECES)
    ]


def inner_kernel(with_mean, *refs):
    if with_mean:
        c_hbm, col_ref, diff_ref, wind_ref, mixing_ref, base_hbm, mean_ref, inv_ref = refs[:8]
    else:
        c_hbm, diff_ref, wind_ref, mixing_ref, base_hbm = refs[:5]
    c_ref, base_ref, in_sems, out_sems = refs[-4:]
    reads = pieces(c_hbm, c_ref, in_sems)
    writes = pieces(base_ref, base_hbm, out_sems)
    for copy in reads:
        copy.start()
    zeros = jnp.zeros((K, 128), F32)
    mix = mixing_block(mixing_ref[...])
    diffusivity, wind = column_of(diff_ref[...]), column_of(wind_ref[...])
    total = jnp.zeros((2 * K + 16, 128), F32)
    reads[0].wait()
    for start in range(0, CELLS, TILE):
        if start % CHUNK == 0 and start // CHUNK + 1 < PIECES:
            reads[start // CHUNK + 1].wait()
        window = c_ref[:, max(start - 128, 0) : min(start + TILE + 128, CELLS)]
        if start == 0:
            window = jnp.concatenate([zeros, window], axis=1)
        if start + TILE == CELLS:
            window = jnp.concatenate([window, zeros], axis=1)
        base_ref[:, start : start + TILE] = substep_tile(window, mix, diffusivity, wind)
        if (start + TILE) % CHUNK == 0:
            writes[start // CHUNK].start()
        if with_mean:
            hits = column_hits(col_ref[:, start : start + TILE])
            high, low = split(window[:, 128 : 128 + TILE])
            rows = jnp.concatenate([high, low, jnp.ones((16, TILE), BF16)], axis=0)
            total = total + lax.dot_general(
                rows, hits, (((1,), (1,)), ((), ())), preferred_element_type=F32
            )
    if with_mean:
        counts = total[2 * K : 2 * K + 8]
        inv = jnp.where(counts > 0.0, 1.0 / jnp.maximum(counts, 1.0), 0.0)
        inv_ref[...] = inv
        mean_ref[...] = (total[:K] + total[K : 2 * K]) * inv[0:1]
    for copy in writes:
        copy.wait()


VMEM_SPEC = pl.BlockSpec(memory_space=pltpu.VMEM)
HBM_SPEC = pl.BlockSpec(memory_space=pltpu.HBM)


def in_hbm(x):
    return pltpu.with_memory_space_constraint(x, pltpu.HBM)


STATE_SCRATCH = [
    pltpu.VMEM((K, CELLS), F32),
    pltpu.VMEM((K, CELLS), F32),
    pltpu.SemaphoreType.DMA((PIECES,)),
    pltpu.SemaphoreType.DMA((PIECES,)),
]


def inner(clouds, col, diffusivity, wind, mixing, with_mean):
    args = [in_hbm(clouds)] + ([col] if with_mean else []) + [diffusivity, wind, mixing]
    shapes = [pltpu.HBM((K, CELLS), F32)]
    if with_mean:
        shapes += [jax.ShapeDtypeStruct((K, 128), F32), jax.ShapeDtypeStruct((8, 128), F32)]
    return pl.pallas_call(
        lambda *refs: inner_kernel(with_mean, *refs),
        in_specs=[HBM_SPEC] + [VMEM_SPEC] * (len(args) - 1),
        out_specs=[HBM_SPEC] + [VMEM_SPEC] * (len(shapes) - 1),
        out_shape=shapes,
        scratch_shapes=STATE_SCRATCH,
        cost_estimate=pl.CostEstimate(flops=1 << 10, bytes_accessed=1 << 10, transcendentals=0),
        compiler_params=pltpu.CompilerParams(vmem_limit_bytes=10 << 20),
        name="inner",
    )(*args)


def outer_kernel(
    info, base_hbm, c_hbm, prof_ref, halo_ref, perm_ref, back_ref, mean_ref, inv_ref,
    col_ref, diff_ref, wind_ref, mixing_ref, out_hbm, end_ref, send_ref, ext1, ext2, force, ends_ref, end_sems, out_ref,
    in_sems, out_sems,
):
    seg = info[0]
    reads = pieces(base_hbm, ext1, in_sems, 256)
    ends = [
        pltpu.make_async_copy(
            c_hbm.at[:, at : at + 256], ends_ref.at[:, 256 * i : 256 * i + 256], end_sems.at[i]
        )
        for i, at in enumerate((0, CELLS - 256))
    ]
    for copy in ends:
        copy.start()
    writes = pieces(out_ref, out_hbm, out_sems)
    for copy in reads:
        copy.start()
    lane = lanes_of((K, 128))
    zeros = jnp.zeros((K, 128), F32)
    mix = mixing_block(mixing_ref[...])
    diffusivity, wind = column_of(diff_ref[...]), column_of(wind_ref[...])

    from_left = halo_ref[lax.rem(seg + SEGS - 1, SEGS), 16:24, :]
    from_right = halo_ref[lax.rem(seg + 1, SEGS), 16:24, :]
    edges = jnp.concatenate([from_left, from_right, jnp.zeros((112, 128), F32)], axis=0).T[:K]
    left_tile = jnp.where(lane >= 125, pltpu.roll(edges, 122, 1), 0.0)
    right_tile = jnp.where(lane < 3, pltpu.roll(edges, 120, 1), 0.0)
    mean = mean_ref[...]
    mean_all = jnp.where(
        lane < COLS,
        mean,
        jnp.where(
            lane == COLS,
            pltpu.roll(edges, COLS - 14, 1),
            jnp.where(lane == COLS + 1, pltpu.roll(edges, COLS + 1 - 7, 1), 0.0),
        ),
    )
    profile = jnp.dot(
        perm_ref[...],
        prof_ref[:, 0:16, :].reshape(SEGS * 16, 128),
        precision=HIGHEST,
        preferred_element_type=F32,
    )
    pulled = jnp.where(lane < COLS + 2, RELAXATION * (profile - mean_all), 0.0)
    pulled = jnp.concatenate(split(pulled), axis=1)

    ext1[:, 0:128] = zeros
    ext1[:, EXT - 128 :] = zeros
    left_col = jnp.full((1, 128), COLS + 1, jnp.int32)
    right_col = jnp.full((1, 128), COLS, jnp.int32)
    for at in range(128, EXT - 128, TILE):
        cell = at - 256
        if (cell + 128) % CHUNK == 0 and (cell + 128) // CHUNK < PIECES:
            reads[(cell + 128) // CHUNK].wait()
        if cell < 0:
            ends[0].wait()
            window = jnp.concatenate([zeros, left_tile, ends_ref[:, 0:256]], axis=1)
            value = substep_tile(window, mix, diffusivity, wind)
            col = jnp.concatenate([left_col, col_ref[:, 0:128]], axis=1)
        elif cell + TILE > CELLS:
            ends[1].wait()
            window = jnp.concatenate([ends_ref[:, 256:512], right_tile, zeros], axis=1)
            value = substep_tile(window, mix, diffusivity, wind)
            col = jnp.concatenate([col_ref[:, CELLS - 128 :], right_col], axis=1)
        else:
            value = ext1[:, at : at + TILE]
            col = col_ref[:, cell : cell + TILE]
        hits = column_hits(col)
        forced = jnp.dot(
            pulled, jnp.concatenate([hits, hits], axis=0), preferred_element_type=F32
        )
        force[:, at : at + TILE] = forced
        ext1[:, at : at + TILE] = value + forced

    for at in range(128, EXT - 128, TILE):
        window = ext1[:, at - 128 : at + TILE + 128]
        ext2[:, at : at + TILE] = (
            substep_tile(window, mix, diffusivity, wind) + force[:, at : at + TILE]
        )

    total = jnp.zeros((2 * K, 128), F32)
    for cell in range(0, CELLS, TILE):
        at = cell + 256
        window = ext2[:, at - 128 : at + TILE + 128]
        value = substep_tile(window, mix, diffusivity, wind) + force[:, at : at + TILE]
        out_ref[:, cell : cell + TILE] = value
        if (cell + TILE) % CHUNK == 0:
            writes[cell // CHUNK].start()
        hits = column_hits(col_ref[:, cell : cell + TILE])
        rows = jnp.concatenate(split(value), axis=0)
        total = total + lax.dot_general(
            rows, hits, (((1,), (1,)), ((), ())), preferred_element_type=F32
        )
    end = (total[:K] + total[K:]) * inv_ref[0:1]
    end_ref[...] = end
    tendency = jnp.where(lane < COLS, end - mean, 0.0)
    sent = jnp.dot(back_ref[...], tendency, precision=HIGHEST, preferred_element_type=F32)
    edge = edge_rows(
        out_ref[:, 0:128], out_ref[:, CELLS - 128 :], end[:, 0:1], end[:, COLS - 1 : COLS]
    )
    for s in range(send_ref.shape[0]):
        send_ref[s, 0:16, :] = sent[16 * (s % SEGS) : 16 * (s % SEGS) + 16]
        send_ref[s, 16:24, :] = edge
    for copy in writes:
        copy.wait()


def outer(info, base, clouds, *args):
    return call(
        outer_kernel, "outer", (in_hbm(base), in_hbm(clouds), *args), [pltpu.HBM((K, CELLS), F32), shape(K, 128), shape(SEGS, 24, 128)],
        scratch=[pltpu.VMEM((K, EXT), F32)] * 3
        + [pltpu.VMEM((K, 512), F32), pltpu.SemaphoreType.DMA((2,))]
        + STATE_SCRATCH[1:],
        prefetch=info, limit=16, hbm=True,
    )


def upper(shape):
    return lax.broadcasted_iota(jnp.int32, shape, len(shape) - 2) % 8 < 4


def swap4(x):
    tiles = x.reshape(-1, 8, x.shape[-1])
    return pltpu.roll(tiles, 4, 1).reshape(x.shape)


def dot3(x, table):
    high, low = split(x)
    rows = x.shape[0]
    both = jnp.dot(jnp.concatenate([high, low], axis=0), table[0], preferred_element_type=F32)
    return both[:rows] + both[rows:] + jnp.dot(high, table[1], preferred_element_type=F32)


def dot3_left(table, x):
    high, low = split(x)
    cols = x.shape[1]
    both = jnp.dot(table[0], jnp.concatenate([high, low], axis=1), preferred_element_type=F32)
    return both[:, :cols] + both[:, cols:] + jnp.dot(table[1], high, preferred_element_type=F32)


def received_rows(chunks, table):
    rows = jnp.concatenate(
        [jnp.concatenate([c[s] for s in range(SEGS)], axis=1) for c in chunks], axis=0
    )
    coeffs = dot3(rows, table)
    out = []
    first = upper((8, M))
    for a in range(len(chunks)):
        c = [coeffs[16 * a + 8 * i : 16 * a + 8 * i + 8, :M] for i in range(2)]
        s = [coeffs[16 * a + 8 * i : 16 * a + 8 * i + 8, M:] for i in range(2)]
        out.append(
            [
                jnp.where(first, c[0], swap4(s[0])),
                jnp.where(first, swap4(c[0]), s[0]),
                jnp.where(first, c[1], swap4(s[1])),
            ]
        )
    return out


def weigh(total, factors, rows):
    vort, mix, turn = factors[:, :M], factors[:, M : 2 * M], factors[:, 2 * M :]
    return [
        total[0] + vort * rows[0],
        total[1] + (mix * rows[1] + turn * rows[2]),
        total[2] + (mix * rows[2] - turn * rows[1]),
    ]


def call(kernel, name, args, shapes, scratch=(), prefetch=None, limit=8, hbm=False):
    specs = [VMEM_SPEC] * len(args)
    common = dict(
        out_shape=shapes,
        name=name,
        cost_estimate=pl.CostEstimate(flops=1 << 10, bytes_accessed=1 << 10, transcendentals=0),
        compiler_params=pltpu.CompilerParams(vmem_limit_bytes=limit << 20),
    )
    outs = [VMEM_SPEC] * len(shapes)
    if hbm:
        specs[0] = specs[1] = outs[0] = HBM_SPEC
    if prefetch is None:
        return pl.pallas_call(
            kernel, in_specs=specs, out_specs=outs, scratch_shapes=list(scratch), **common
        )(*args)
    return pl.pallas_call(
        kernel,
        grid_spec=pltpu.PrefetchScalarGridSpec(
            num_scalar_prefetch=1, grid=(), in_specs=specs, out_specs=outs,
            scratch_shapes=list(scratch),
        ),
        **common,
    )(prefetch, *args)


def rows_kernel(grid_ref, table, rows_ref, lines):
    for v in range(3):
        for j in range(LAT_DEV):
            for l in range(4):
                at = v * 48 + 4 * j + l
                lines[at : at + 1, :] = grid_ref[j, 3 * l + v : 3 * l + v + 1, :]
    coeffs = dot3(lines[...], table)
    cos, sin = coeffs[:, :M], coeffs[:, M:]
    first = upper((144, M))
    even = jnp.where(first, cos, swap4(sin))
    odd = jnp.where(first, swap4(cos), sin)
    for v in range(3):
        for i in range(6):
            at = v * 48 + 8 * i
            rows_ref[v, 2 * i] = even[at : at + 8]
            rows_ref[v, 2 * i + 1] = odd[at : at + 8]
        for j in range(LAT_DEV, 16):
            rows_ref[v, j] = jnp.zeros((8, M), F32)


def spread_kernel(info, got_ref, table, rows_ref, send_ref, held):
    offset = place(info)[2]
    forced = received_rows([got_ref[:, 0:16, :]], table)[0]
    for h in range(2):
        held[h] = rows_ref[:, :, :, 128 * h : 128 * h + 128].reshape(384, 128)
        for v in range(3):
            at = pl.ds(pl.multiple_of((v * 16 + offset) * 8, 8), 8)
            held[h, at, :] += forced[v][:, 128 * h : 128 * h + 128]
        held[h, LAT_DEV * 8 : LAT_DEV * 8 + 8, :] = jnp.full((8, 128), offset, jnp.int32).astype(F32)
    for u in range(8):
        for h in range(2):
            send_ref[2 * u + h] = held[h, pl.ds(u, 48, stride=8), :]


def channel_basis(spec_ref, table):
    offsets = spec_ref[:, LAT_DEV, :][:, 0:1].astype(jnp.int32)
    wanted = 16 * lax.broadcasted_iota(jnp.int32, (16, 256), 0) + offsets
    picks = jnp.where(lanes_of((16, 256)) == wanted, 1.0, 0.0).astype(BF16)
    return [jnp.dot(picks, t, preferred_element_type=F32) for t in table]


def weights_kernel(info, mine_ref, others_ref, from_spec, row_weights, out_ref):
    core, chip, _ = place(info)
    own = pl.ds(pl.multiple_of(chip * 16, 16), 16)
    here = from_spec[0, core, own, :].astype(F32) + from_spec[1, core, own, :].astype(F32)
    for half, ref, side in ((0, mine_ref, core), (16, others_ref, 1 - core)):
        high, low = channel_basis(ref, [from_spec[0, side], from_spec[1, side]])
        basis = high + low
        products = jnp.concatenate([basis[c : c + 1] * here for c in range(16)], axis=0)
        out_ref[half : half + 16] = dot3(products, row_weights).reshape(16, 16, 3 * M)


def settle_kernel(info, mine_ref, others_ref, to_spec, from_spec, once, twice, out_ref):
    core, chip, _ = place(info)
    half = lax.rem(chip, 2)

    def columns(ref):
        return jnp.concatenate(
            [ref[:, 16 * v : 16 * v + 16, :].reshape(256, 128) for v in range(3)], axis=1
        )

    def update(factors, spec):
        vort, div, geo = spec[:, :128], spec[:, 128:256], spec[:, 256:]
        f0, f1, f2 = factors[half, 0], factors[half, 1], factors[half, 2]
        return jnp.concatenate([f0 * vort, f1 * div + f2 * geo, f1 * geo - f2 * div], axis=1)

    spec = dot3_left([to_spec[0, core], to_spec[1, core]], columns(mine_ref)) + dot3_left(
        [to_spec[0, 1 - core], to_spec[1, 1 - core]], columns(others_ref)
    )
    table = [from_spec[0, core], from_spec[1, core]]
    back = dot3_left(table, update(twice, spec))
    channels = dot3_left(
        [t.astype(BF16) for t in channel_basis(mine_ref, table)], update(once, spec)
    )
    for v in range(3):
        out_ref[:, 16 * v : 16 * v + 16, :] = back[:, 128 * v : 128 * v + 128].reshape(16, 16, 128)
        for q in range(16):
            out_ref[q, 16 * v + LAT_DEV : 16 * v + LAT_DEV + 1, :] = channels[
                q : q + 1, 128 * v : 128 * v + 128
            ]


def profile_kernel(got_ref, table, out_ref, total):
    for v in range(3):
        for u in range(8):
            for h in range(2):
                at = 16 * v + LAT_DEV
                total[8 * v + u : 8 * v + u + 1, 128 * h : 128 * h + 128] = got_ref[
                    2 * u + h, at : at + 1, :
                ]
    a, b, c = total[0:8], total[8:16], total[16:24]
    first = upper((8, M))
    cos = jnp.concatenate([jnp.where(first, a, swap4(b)), c], axis=0)
    sin = jnp.concatenate([jnp.where(first, swap4(a), b), swap4(c)], axis=0)
    lines = dot3(jnp.concatenate([cos, sin], axis=1), table)
    for s in range(SEGS):
        out_ref[s] = lines[:, 128 * s : 128 * s + 128]


def last_kernel(got_ref, table, out_ref):
    rows = received_rows([got_ref[:, 0:16, :]], table)[0]
    line = jnp.concatenate(rows, axis=0)
    for c in range(16):
        out_ref[c] = line


def add_channels(factors, half, from_ref, held):
    def row_pair(i, _):
        for h in range(2):
            j = 2 * i + h
            total = [held[v, j] for v in range(3)]
            for c in range(16):
                total = weigh(
                    total,
                    factors[c + half, pl.ds(j, 1), :],
                    [from_ref[c, 8 * v : 8 * v + 8, :] for v in range(3)],
                )
            for v in range(3):
                held[v, j] = total[v]
        return 0

    lax.fori_loop(0, LAT_DEV // 2, row_pair, 0)


def gather_kernel(got_ref, factors, from_ref, held, flat):
    for u in range(8):
        for h in range(2):
            flat[h, pl.ds(u, 48, stride=8), :] = got_ref[2 * u + h]
    for h in range(2):
        held[:, :, :, 128 * h : 128 * h + 128] = flat[h].reshape(3, 16, 8, 128)
    add_channels(factors, 0, from_ref, held)


def finish_kernel(part_ref, factors, from_ref, table, out_ref, held):
    held[...] = part_ref[...]
    add_channels(factors, 16, from_ref, held)
    first = upper((8, M))
    cos, sin = [], []
    for v in range(3):
        for i in range(6):
            even, odd = held[v, 2 * i], held[v, 2 * i + 1]
            cos.append(jnp.where(first, even, swap4(odd)))
            sin.append(jnp.where(first, swap4(even), odd))
    rows = jnp.concatenate(
        [jnp.concatenate(cos, axis=0), jnp.concatenate(sin, axis=0)], axis=1
    )
    lines = dot3(rows, table)
    for v in range(3):
        for j in range(LAT_DEV):
            for l in range(4):
                at = v * 48 + 4 * j + l
                out_ref[j, 3 * l + v : 3 * l + v + 1, :] = lines[at : at + 1]


def shape(*dims):
    return jax.ShapeDtypeStruct(dims, F32)


def rows_exchange(x):
    return lax.all_to_all(x, "lat", 0, 0, axis_index_groups=ROW_GROUPS, tiled=True)


def core_swap(x):
    return lax.ppermute(x, "lat", CORE_SWAP)


def shards(atmosphere, cloud_state, channel_lat, cell_column, channel_wind, diffusivity, mixing):
    tab = {name: jnp.asarray(value) for name, value in tables().items()}
    natural, grouped = permutations()
    lat = lax.axis_index("lat").astype(jnp.int32)
    seg = lax.axis_index("seg").astype(jnp.int32)
    info = jnp.stack((seg, lat, channel_lat[0]))
    clouds = cloud_state[0]
    col = cell_column
    wind = channel_wind
    diff = diffusivity.reshape(1, K)
    spread_table = tab["forward_seg"]
    gather_rows = jnp.asarray(grouped)
    scatter_rows = jnp.asarray(grouped.T.copy())

    send = prepare(info, atmosphere, clouds, col)
    got = lax.all_to_all(send, "seg", 0, 0, tiled=True)
    grid, state, send = lax.optimization_barrier((atmosphere, clouds, send))
    base, mean, inv = inner(state, col, diff, wind, mixing, True)
    rows = call(
        rows_kernel, "rows", (grid, tab["forward"]), [shape(3, 16, 8, M)],
        scratch=[pltpu.VMEM((144, NLON), F32)],
    )[0]
    rows, got = lax.optimization_barrier((rows, got))
    clouds, mean_1, send = outer(
        info, base, state, got, got, jnp.asarray(natural), scatter_rows,
        mean, inv, col, diff, wind, mixing,
    )
    halo = lax.all_to_all(send, "seg", 0, 0, tiled=True)
    base = inner(clouds, col, diff, wind, mixing, False)[0]
    base, halo = lax.optimization_barrier((base, halo))

    spread = call(
        spread_kernel, "spread", (halo, spread_table, rows), [shape(16, 48, 128)],
        scratch=[pltpu.VMEM((2, 384, 128), F32)], prefetch=info,
    )[0]
    spec_mine = rows_exchange(spread)
    spec_others = core_swap(spec_mine)
    settled = call(
        settle_kernel, "settle",
        (spec_mine, spec_others, tab["to_spec"], tab["from_spec"], tab["once"], tab["twice"]),
        [shape(16, 48, 128)], prefetch=info,
    )[0]
    settled = rows_exchange(settled)
    profile = call(
        profile_kernel, "profile", (settled, tab["inverse_seg"]), [shape(SEGS, 16, 128)],
        scratch=[pltpu.VMEM((24, M), F32)],
    )[0]
    profile, spec_mine, spec_others = lax.optimization_barrier((profile, spec_mine, spec_others))
    factors = call(
        weights_kernel, "weights", (spec_mine, spec_others, tab["from_spec"], tab["row_weights"]),
        [shape(32, 16, 3 * M)], prefetch=info,
    )[0]
    profile = lax.all_to_all(profile, "seg", 0, 0, tiled=True)

    factors, profile = lax.optimization_barrier((factors, profile))

    clouds, _, send = outer(
        info, base, clouds, profile, halo, gather_rows, scatter_rows,
        mean_1, inv, col, diff, wind, mixing,
    )
    got = lax.all_to_all(send, "seg", 0, 0, tiled=True)
    from_mine = rows_exchange(
        call(last_kernel, "last", (got, spread_table), [shape(16, 24, M)])[0]
    )
    from_others = core_swap(from_mine)
    part = call(
        gather_kernel, "gather", (settled, factors, from_mine), [shape(3, 16, 8, M)],
        scratch=[pltpu.VMEM((2, 384, 128), F32)],
    )[0]
    grid = call(
        finish_kernel, "finish", (part, factors, from_others, tab["inverse"]),
        [shape(LAT_DEV, KD, NLON)], scratch=[pltpu.VMEM((3, 16, 8, M), F32)],
    )[0]
    return grid, clouds[None]


def solution(mesh):
    placed = (
        P("lat", "seg", None),
        P("lat", None, "seg"),
        P("lat"),
        P("lat", "seg"),
        P("lat", None),
        P(),
        P(),
    )
    return jax.shard_map(
        shards,
        mesh=mesh,
        in_specs=placed,
        out_specs=(P("lat", "seg", None), P("lat", None, "seg")),
        check_vma=False,
    )
```

```python
import ml_dtypes
import numpy as np

import jax
import jax.numpy as jnp
from jax import lax
from jax.experimental import pallas as pl
from jax.experimental.pallas import tpu as pltpu
from jax.sharding import PartitionSpec as P

NLON = 768
M = 256
NT = 256
NLAT = 384
LAT_DEV = 12
K = 96
KD = 12
COLS = 96
CELLS = 6144
LATS = 32
SEGS = 8
TILE = 256
T2 = 1280
T3 = 1536
TI = 1536
EXT = CELLS + 512
CHUNK = 1536
PIECES = CELLS // CHUNK
RELAXATION = 0.5
MIXING_RATE = 0.3
DAMPING = 0.2
COUPLING = 2.0
F32 = jnp.float32
BF16 = jnp.bfloat16

ROW_GROUPS = [[2 * q + b for q in range(16)] for b in range(2)]
CORE_SWAP = [(i, i ^ 1) for i in range(LATS)]


def tables():
    m = np.arange(M)
    x = np.arange(NLON)
    angles = 2.0 * np.pi * ((m[:, None] * x[None, :]) % NLON) / NLON
    waves = np.stack([np.cos(angles), np.sin(angles)])
    sigma = np.where(m == 0, 1.0, 2.0)
    inverse = (waves * sigma[None, :, None]).reshape(2 * M, NLON)
    forward = (waves / NLON).reshape(2 * M, NLON).T
    forward_seg = np.zeros((SEGS, 128, 2 * M))
    forward_seg[:, :COLS] = forward.reshape(SEGS, COLS, 2 * M)
    inverse_seg = np.zeros((2 * M, SEGS, 128))
    for s in range(SEGS):
        inverse_seg[:, s, : COLS + 1] = inverse[:, (COLS * s + np.arange(COLS + 1)) % NLON]
        inverse_seg[:, s, COLS + 1] = inverse[:, (COLS * s - 1) % NLON]
    n = np.arange(NT)
    j = np.arange(NLAT)
    basis = np.cos(np.pi * ((n[:, None] * (2 * j[None, :] + 1)) % (4 * NLAT)) / (2 * NLAT))
    weights = np.where(n == 0, 1.0, 2.0) / NLAT
    size = (m[None, :] ** 2 + n[:, None] ** 2) / (NT * NT)
    damping = 1.0 + size * size
    coupling = COUPLING * size
    det = damping**2 + coupling**2
    keep = (m[None, :] + n[:, None] < NT).astype(np.float64)
    update = np.stack([keep / damping, keep * damping / det, keep * coupling / det])
    twice = np.stack(
        [
            keep / damping**2,
            keep * (damping**2 - coupling**2) / det**2,
            keep * 2.0 * damping * coupling / det**2,
        ]
    )
    row_weights = np.transpose(update * weights[None, :, None], (1, 0, 2)).reshape(NT, 3 * M)
    parity = basis.reshape(NT, 16, 2, LAT_DEV)
    spread = np.zeros((2, NT, 16, 16))
    spread[:, :, :, :LAT_DEV] = np.transpose(parity, (2, 0, 1, 3))
    spread = spread.reshape(2, NT, 256)
    f = np.float32
    return dict(
        forward=pair_of(forward),
        inverse=pair_of(inverse),
        forward_seg=pair_of(forward_seg.reshape(SEGS * 128, 2 * M)),
        inverse_seg=pair_of(inverse_seg.reshape(2 * M, SEGS * 128)),
        to_spec=pair_of(spread * weights[None, :, None]),
        from_spec=pair_of(np.transpose(spread, (0, 2, 1))),
        once=np.ascontiguousarray(np.transpose(update.reshape(3, NT, 2, 128), (2, 0, 1, 3))).astype(f),
        twice=np.ascontiguousarray(np.transpose(twice.reshape(3, NT, 2, 128), (2, 0, 1, 3))).astype(f),
        row_weights=pair_of(row_weights),
    )


def pair_of(x):
    x = x.astype(np.float32)
    high = x.astype(ml_dtypes.bfloat16)
    low = (x - high.astype(np.float32)).astype(ml_dtypes.bfloat16)
    return np.stack((high, low))


def lanes_of(shape):
    return lax.broadcasted_iota(jnp.int32, shape, len(shape) - 1)


def split(x):
    high = x.astype(BF16)
    low = (x - high.astype(F32)).astype(BF16)
    return high, low


def mixing_block(mixing):
    high, low = split(MIXING_RATE * mixing)
    return jnp.concatenate(
        [jnp.concatenate([high, high], axis=1), jnp.concatenate([low, low], axis=1)], axis=0
    )


def substep_tile(window, mix, diffusivity, wind):
    width = window.shape[1]
    center = window[:, 128 : width - 128]
    right = pltpu.roll(window, width - 1, 1)[:, 128 : width - 128]
    left = pltpu.roll(window, 1, 1)[:, 128 : width - 128]
    high, low = split(center)
    mixed = jnp.dot(mix, jnp.concatenate([high, low], axis=0), preferred_element_type=F32)
    return (
        center
        + diffusivity * (right - 2.0 * center + left)
        - 0.5 * wind * (right - left)
        + (mixed[:K] + mixed[K:])
        - DAMPING * jnp.tanh(center)
    )


def column_hits(col):
    ids = lax.broadcasted_iota(jnp.int32, (128, col.shape[1]), 0)
    return jnp.where(ids == col, 1.0, 0.0).astype(BF16)


def row_order(grouped, transposed):
    size = (SEGS * 16, K) if transposed else (K, SEGS * 16)
    pair = lax.broadcasted_iota(jnp.int32, size, 1 if transposed else 0)
    row = lax.broadcasted_iota(jnp.int32, size, 0 if transposed else 1)
    owner = (pair * 43691) >> 19
    within = pair - KD * owner
    level = (within * 11) >> 5
    place_in = (within - 3 * level) * 4 + level if grouped else within
    return jnp.where(row == 16 * owner + place_in, 1.0, 0.0).astype(BF16)


def reorder(matrix, x):
    high, low = split(x)
    rest = (x - high.astype(F32) - low.astype(F32)).astype(BF16)
    width = x.shape[1]
    out = jnp.dot(matrix, jnp.concatenate([high, low, rest], axis=1), preferred_element_type=F32)
    return out[:, :width] + out[:, width : 2 * width] + out[:, 2 * width :]


def edge_rows(first, last, mean_first, mean_last):
    lane = lanes_of((K, 128))
    edge = jnp.where(
        lane < 3,
        first,
        jnp.where(
            lane < 6, pltpu.roll(last, 6, 1), jnp.where(lane == 6, mean_first, mean_last)
        ),
    )
    padded = jnp.concatenate([edge, jnp.zeros((32, 128), F32)], axis=0)
    return padded.T[:8]


def place(info):
    lat = info[1]
    return lax.rem(lat, 2), lax.div(lat, 2), info[2] - lat * LAT_DEV


def prepare_kernel(info, row_ref, first_ref, last_ref, colf_ref, coll_ref, send_ref):
    del info
    row = row_ref[0]
    lane = lanes_of((KD, 128))
    hit_first = jnp.where(colf_ref[...] == 0, 1.0, 0.0)
    hit_last = jnp.where(coll_ref[...] == COLS - 1, 1.0, 0.0)
    first, last = first_ref[...], last_ref[...]
    mean_first = jnp.sum(first * hit_first, axis=1, keepdims=True) / jnp.sum(
        hit_first, axis=1, keepdims=True
    )
    mean_last = jnp.sum(last * hit_last, axis=1, keepdims=True) / jnp.sum(
        hit_last, axis=1, keepdims=True
    )
    edge = edge_rows(first, last, mean_first, mean_last)
    for s in range(SEGS):
        own = pltpu.roll(row, (NLON - COLS * s) % NLON, 1)[:, :128]
        before = pltpu.roll(row, (COLS + 1 - (COLS * s - 1)) % NLON, 1)[:, :128]
        chunk = jnp.where(lane <= COLS, own, jnp.where(lane == COLS + 1, before, 0.0))
        send_ref[s, 0:KD, :] = chunk
        send_ref[s, KD:16, :] = jnp.zeros((16 - KD, 128), F32)
        send_ref[s, 16:24, :] = edge


def prepare(info, atmosphere, clouds, col):
    last = CELLS // 128 - 1
    return pl.pallas_call(
        prepare_kernel,
        grid_spec=pltpu.PrefetchScalarGridSpec(
            num_scalar_prefetch=1,
            grid=(1,),
            in_specs=[
                pl.BlockSpec((1, KD, NLON), lambda i, info: (place(info)[2], 0, 0)),
                pl.BlockSpec((K, 128), lambda i, off: (0, 0)),
                pl.BlockSpec((K, 128), lambda i, off: (0, last)),
                pl.BlockSpec((1, 128), lambda i, off: (0, 0)),
                pl.BlockSpec((1, 128), lambda i, off: (0, last)),
            ],
            out_specs=pl.BlockSpec((SEGS, 24, 128), lambda i, off: (0, 0, 0)),
        ),
        out_shape=jax.ShapeDtypeStruct((SEGS, 24, 128), F32),
        name="prepare",
    )(info, atmosphere, clouds, clouds, col, col)


def column_of(row):
    size = row.shape[1]
    diagonal = lax.broadcasted_iota(jnp.int32, (size, size), 0) == lanes_of((size, size))
    return jnp.sum(jnp.where(diagonal, row, 0.0), axis=1, keepdims=True)


def pieces(source, target, sems, shift=0):
    return [
        pltpu.make_async_copy(
            source.at[:, i * CHUNK : (i + 1) * CHUNK],
            target.at[:, shift + i * CHUNK : shift + (i + 1) * CHUNK],
            sems.at[i],
        )
        for i in range(PIECES)
    ]


def inner_kernel(with_mean, *refs):
    if with_mean:
        c_hbm, col_ref, diff_ref, wind_ref, mixing_ref, base_hbm, mean_hbm, inv_ref = refs[:8]
        mean_ref, mean_sem = refs[8:10]
    else:
        c_hbm, diff_ref, wind_ref, mixing_ref, base_hbm = refs[:5]
    c_ref, base_ref, in_sems, out_sems = refs[-4:]
    reads = pieces(c_hbm, c_ref, in_sems)
    writes = pieces(base_ref, base_hbm, out_sems)
    for copy in reads:
        copy.start()
    zeros = jnp.zeros((K, 128), F32)
    mix = mixing_block(mixing_ref[...])
    diffusivity, wind = column_of(diff_ref[...]), column_of(wind_ref[...])
    total = jnp.zeros((2 * K + 16, 128), F32)
    reads[0].wait()
    for start in range(0, CELLS, TI):
        if start % CHUNK == 0 and start // CHUNK + 1 < PIECES:
            reads[start // CHUNK + 1].wait()
        window = c_ref[:, max(start - 128, 0) : min(start + TI + 128, CELLS)]
        if start == 0:
            window = jnp.concatenate([zeros, window], axis=1)
        if start + TI == CELLS:
            window = jnp.concatenate([window, zeros], axis=1)
        base_ref[:, start : start + TI] = substep_tile(window, mix, diffusivity, wind)
        if (start + TI) % CHUNK == 0:
            writes[start // CHUNK].start()
        if with_mean:
            hits = column_hits(col_ref[:, start : start + TI])
            high, low = split(window[:, 128 : 128 + TI])
            rows = jnp.concatenate([high, low, jnp.ones((16, TI), BF16)], axis=0)
            total = total + lax.dot_general(
                rows, hits, (((1,), (1,)), ((), ())), preferred_element_type=F32
            )
    if with_mean:
        counts = total[2 * K : 2 * K + 8]
        inv = jnp.where(counts > 0.0, 1.0 / jnp.maximum(counts, 1.0), 0.0)
        inv_ref[...] = inv
        mean_ref[...] = (total[:K] + total[K : 2 * K]) * inv[0:1]
        mean_write = pltpu.make_async_copy(mean_ref, mean_hbm, mean_sem)
        mean_write.start()
        mean_write.wait()
    for copy in writes:
        copy.wait()


VMEM_SPEC = pl.BlockSpec(memory_space=pltpu.VMEM)
HBM_SPEC = pl.BlockSpec(memory_space=pltpu.HBM)
MEAN_SCRATCH = [pltpu.VMEM((K, 128), F32), pltpu.SemaphoreType.DMA]


def in_hbm(x):
    return pltpu.with_memory_space_constraint(x, pltpu.HBM)


STATE_SCRATCH = [
    pltpu.VMEM((K, CELLS), F32),
    pltpu.VMEM((K, CELLS), F32),
    pltpu.SemaphoreType.DMA((PIECES,)),
    pltpu.SemaphoreType.DMA((PIECES,)),
]


def inner(clouds, col, diffusivity, wind, mixing, with_mean):
    args = [in_hbm(clouds)] + ([col] if with_mean else []) + [diffusivity, wind, mixing]
    shapes = [pltpu.HBM((K, CELLS), F32)]
    if with_mean:
        shapes += [pltpu.HBM((K, 128), F32), jax.ShapeDtypeStruct((8, 128), F32)]
    return pl.pallas_call(
        lambda *refs: inner_kernel(with_mean, *refs),
        in_specs=[HBM_SPEC] + [VMEM_SPEC] * (len(args) - 1),
        out_specs=([HBM_SPEC, HBM_SPEC, VMEM_SPEC] if with_mean else [HBM_SPEC]),
        out_shape=shapes,
        scratch_shapes=MEAN_SCRATCH * with_mean + STATE_SCRATCH,
        cost_estimate=pl.CostEstimate(flops=1 << 10, bytes_accessed=1 << 10, transcendentals=0),
        compiler_params=pltpu.CompilerParams(vmem_limit_bytes=10 << 20),
        name="inner",
    )(*args)


def outer_kernel(
    grouped, info, base_hbm, c_hbm, mean_hbm, prof_ref, halo_ref, inv_ref, col_ref, diff_ref, wind_ref,
    mixing_ref, out_hbm, end_hbm, send_ref, ext1, ext2, force, ends_ref, mean_ref, end_ref, small_sems,
    out_ref, in_sems, out_sems,
):
    seg = info[0]
    reads = pieces(base_hbm, ext1, in_sems, 256)
    ends = [
        pltpu.make_async_copy(
            c_hbm.at[:, at : at + 256], ends_ref.at[:, 256 * i : 256 * i + 256], small_sems.at[i]
        )
        for i, at in enumerate((0, CELLS - 256))
    ]
    mean_read = pltpu.make_async_copy(mean_hbm, mean_ref, small_sems.at[2])
    mean_read.start()
    end_write = pltpu.make_async_copy(end_ref, end_hbm, small_sems.at[3])
    for copy in ends:
        copy.start()
    writes = pieces(out_ref, out_hbm, out_sems)
    for copy in reads:
        copy.start()
    lane = lanes_of((K, 128))
    zeros = jnp.zeros((K, 128), F32)
    mix = mixing_block(mixing_ref[...])
    diffusivity, wind = column_of(diff_ref[...]), column_of(wind_ref[...])

    from_left = halo_ref[lax.rem(seg + SEGS - 1, SEGS), 16:24, :]
    from_right = halo_ref[lax.rem(seg + 1, SEGS), 16:24, :]
    edges = jnp.concatenate([from_left, from_right, jnp.zeros((112, 128), F32)], axis=0).T[:K]
    left_tile = jnp.where(lane >= 125, pltpu.roll(edges, 122, 1), 0.0)
    right_tile = jnp.where(lane < 3, pltpu.roll(edges, 120, 1), 0.0)
    mean_read.wait()
    mean = mean_ref[...]
    mean_all = jnp.where(
        lane < COLS,
        mean,
        jnp.where(
            lane == COLS,
            pltpu.roll(edges, COLS - 14, 1),
            jnp.where(lane == COLS + 1, pltpu.roll(edges, COLS + 1 - 7, 1), 0.0),
        ),
    )
    profile = reorder(
        row_order(grouped, False), prof_ref[:, 0:16, :].reshape(SEGS * 16, 128)
    )
    pulled = jnp.where(lane < COLS + 2, RELAXATION * (profile - mean_all), 0.0)
    pulled = jnp.concatenate(split(pulled), axis=1)

    ext1[:, 0:128] = zeros
    ext1[:, EXT - 128 :] = zeros
    left_col = jnp.full((1, 128), COLS + 1, jnp.int32)
    right_col = jnp.full((1, 128), COLS, jnp.int32)
    for at in range(128, EXT - 128, TILE):
        cell = at - 256
        if cell < 0:
            col = jnp.concatenate([left_col, col_ref[:, 0:128]], axis=1)
        elif cell + TILE > CELLS:
            col = jnp.concatenate([col_ref[:, CELLS - 128 :], right_col], axis=1)
        else:
            col = col_ref[:, cell : cell + TILE]
        hits = column_hits(col)
        force[:, at : at + TILE] = jnp.dot(
            pulled, jnp.concatenate([hits, hits], axis=0), preferred_element_type=F32
        )

    for at in range(128, EXT - 128, TILE):
        cell = at - 256
        if (cell + 128) % CHUNK == 0 and (cell + 128) // CHUNK < PIECES:
            reads[(cell + 128) // CHUNK].wait()
        if cell < 0:
            ends[0].wait()
            window = jnp.concatenate([zeros, left_tile, ends_ref[:, 0:256]], axis=1)
            value = substep_tile(window, mix, diffusivity, wind)
        elif cell + TILE > CELLS:
            ends[1].wait()
            window = jnp.concatenate([ends_ref[:, 256:512], right_tile, zeros], axis=1)
            value = substep_tile(window, mix, diffusivity, wind)
        else:
            value = ext1[:, at : at + TILE]
        ext1[:, at : at + TILE] = value + force[:, at : at + TILE]

    for at in range(128, EXT - 128, T2):
        window = ext1[:, at - 128 : at + T2 + 128]
        ext2[:, at : at + T2] = (
            substep_tile(window, mix, diffusivity, wind) + force[:, at : at + T2]
        )

    total = jnp.zeros((2 * K, 128), F32)
    for cell in range(0, CELLS, T3):
        at = cell + 256
        window = ext2[:, at - 128 : at + T3 + 128]
        value = substep_tile(window, mix, diffusivity, wind) + force[:, at : at + T3]
        out_ref[:, cell : cell + T3] = value
        if (cell + T3) % CHUNK == 0:
            writes[cell // CHUNK].start()
        hits = column_hits(col_ref[:, cell : cell + T3])
        rows = jnp.concatenate(split(value), axis=0)
        total = total + lax.dot_general(
            rows, hits, (((1,), (1,)), ((), ())), preferred_element_type=F32
        )
    end = (total[:K] + total[K:]) * inv_ref[0:1]
    end_ref[...] = end
    end_write.start()
    tendency = jnp.where(lane < COLS, end - mean, 0.0)
    sent = reorder(row_order(True, True), tendency)
    edge = edge_rows(
        out_ref[:, 0:128], out_ref[:, CELLS - 128 :], end[:, 0:1], end[:, COLS - 1 : COLS]
    )
    for s in range(send_ref.shape[0]):
        send_ref[s, 0:16, :] = sent[16 * (s % SEGS) : 16 * (s % SEGS) + 16]
        send_ref[s, 16:24, :] = edge
    end_write.wait()
    for copy in writes:
        copy.wait()


def outer(grouped, info, base, clouds, mean, *args):
    return call(
        lambda *refs: outer_kernel(grouped, *refs), "outer",
        (in_hbm(base), in_hbm(clouds), in_hbm(mean), *args),
        [pltpu.HBM((K, CELLS), F32), pltpu.HBM((K, 128), F32), shape(SEGS, 24, 128)],
        scratch=[pltpu.VMEM((K, EXT), F32)] * 3
        + [pltpu.VMEM((K, 512), F32), pltpu.VMEM((K, 128), F32), pltpu.VMEM((K, 128), F32)]
        + [pltpu.SemaphoreType.DMA((4,))]
        + STATE_SCRATCH[1:],
        prefetch=info, limit=16, hbm=(3, 2),
    )


def upper(shape):
    return lax.broadcasted_iota(jnp.int32, shape, len(shape) - 2) % 8 < 4


def swap4(x):
    tiles = x.reshape(-1, 8, x.shape[-1])
    return pltpu.roll(tiles, 4, 1).reshape(x.shape)


def dot3(x, table):
    high, low = split(x)
    rows = x.shape[0]
    both = jnp.dot(jnp.concatenate([high, low], axis=0), table[0], preferred_element_type=F32)
    return both[:rows] + both[rows:] + jnp.dot(high, table[1], preferred_element_type=F32)


def dot3_left(table, x):
    high, low = split(x)
    cols = x.shape[1]
    both = jnp.dot(table[0], jnp.concatenate([high, low], axis=1), preferred_element_type=F32)
    return both[:, :cols] + both[:, cols:] + jnp.dot(table[1], high, preferred_element_type=F32)


def received_rows(chunks, table):
    rows = jnp.concatenate(
        [jnp.concatenate([c[s] for s in range(SEGS)], axis=1) for c in chunks], axis=0
    )
    coeffs = dot3(rows, table)
    out = []
    first = upper((8, M))
    for a in range(len(chunks)):
        c = [coeffs[16 * a + 8 * i : 16 * a + 8 * i + 8, :M] for i in range(2)]
        s = [coeffs[16 * a + 8 * i : 16 * a + 8 * i + 8, M:] for i in range(2)]
        out.append(
            [
                jnp.where(first, c[0], swap4(s[0])),
                jnp.where(first, swap4(c[0]), s[0]),
                jnp.where(first, c[1], swap4(s[1])),
            ]
        )
    return out


def weigh(total, factors, rows):
    vort, mix, turn = factors[:, :M], factors[:, M : 2 * M], factors[:, 2 * M :]
    return [
        total[0] + vort * rows[0],
        total[1] + (mix * rows[1] + turn * rows[2]),
        total[2] + (mix * rows[2] - turn * rows[1]),
    ]


def call(kernel, name, args, shapes, scratch=(), prefetch=None, limit=8, hbm=(0, 0)):
    specs = [VMEM_SPEC] * len(args)
    common = dict(
        out_shape=shapes,
        name=name,
        cost_estimate=pl.CostEstimate(flops=1 << 10, bytes_accessed=1 << 10, transcendentals=0),
        compiler_params=pltpu.CompilerParams(vmem_limit_bytes=limit << 20),
    )
    outs = [VMEM_SPEC] * len(shapes)
    specs[: hbm[0]] = [HBM_SPEC] * hbm[0]
    outs[: hbm[1]] = [HBM_SPEC] * hbm[1]
    if prefetch is None:
        return pl.pallas_call(
            kernel, in_specs=specs, out_specs=outs, scratch_shapes=list(scratch), **common
        )(*args)
    return pl.pallas_call(
        kernel,
        grid_spec=pltpu.PrefetchScalarGridSpec(
            num_scalar_prefetch=1, grid=(), in_specs=specs, out_specs=outs,
            scratch_shapes=list(scratch),
        ),
        **common,
    )(prefetch, *args)


def rows_kernel(grid_ref, table, rows_ref, lines):
    for v in range(3):
        for j in range(LAT_DEV):
            for l in range(4):
                at = v * 48 + 4 * j + l
                lines[at : at + 1, :] = grid_ref[j, 3 * l + v : 3 * l + v + 1, :]
    coeffs = dot3(lines[...], table)
    cos, sin = coeffs[:, :M], coeffs[:, M:]
    first = upper((144, M))
    even = jnp.where(first, cos, swap4(sin))
    odd = jnp.where(first, swap4(cos), sin)
    for v in range(3):
        for i in range(6):
            at = v * 48 + 8 * i
            rows_ref[v, 2 * i] = even[at : at + 8]
            rows_ref[v, 2 * i + 1] = odd[at : at + 8]
        for j in range(LAT_DEV, 16):
            rows_ref[v, j] = jnp.zeros((8, M), F32)


def spread_kernel(info, got_ref, table, rows_ref, send_ref, held):
    offset = place(info)[2]
    forced = received_rows([got_ref[:, 0:16, :]], table)[0]
    for h in range(2):
        held[h] = rows_ref[:, :, :, 128 * h : 128 * h + 128].reshape(384, 128)
        for v in range(3):
            at = pl.ds(pl.multiple_of((v * 16 + offset) * 8, 8), 8)
            held[h, at, :] += forced[v][:, 128 * h : 128 * h + 128]
        held[h, LAT_DEV * 8 : LAT_DEV * 8 + 8, :] = jnp.full((8, 128), offset, jnp.int32).astype(F32)
    for u in range(8):
        for h in range(2):
            send_ref[2 * u + h] = held[h, pl.ds(u, 48, stride=8), :]


def channel_basis(spec_ref, table):
    offsets = spec_ref[:, LAT_DEV, :][:, 0:1].astype(jnp.int32)
    wanted = 16 * lax.broadcasted_iota(jnp.int32, (16, 256), 0) + offsets
    picks = jnp.where(lanes_of((16, 256)) == wanted, 1.0, 0.0).astype(BF16)
    return [jnp.dot(picks, t, preferred_element_type=F32) for t in table]


def weights_kernel(info, mine_ref, others_ref, from_spec, row_weights, out_ref):
    core, chip, _ = place(info)
    own = pl.ds(pl.multiple_of(chip * 16, 16), 16)
    here = from_spec[0, core, own, :].astype(F32) + from_spec[1, core, own, :].astype(F32)
    for half, ref, side in ((0, mine_ref, core), (16, others_ref, 1 - core)):
        high, low = channel_basis(ref, [from_spec[0, side], from_spec[1, side]])
        basis = high + low
        products = jnp.concatenate([basis[c : c + 1] * here for c in range(16)], axis=0)
        out_ref[half : half + 16] = dot3(products, row_weights).reshape(16, 16, 3 * M)


def settle_kernel(info, mine_ref, others_ref, to_spec, from_spec, once, twice, out_ref):
    core, chip, _ = place(info)
    half = lax.rem(chip, 2)

    def columns(ref):
        return jnp.concatenate(
            [ref[:, 16 * v : 16 * v + 16, :].reshape(256, 128) for v in range(3)], axis=1
        )

    def update(factors, spec):
        vort, div, geo = spec[:, :128], spec[:, 128:256], spec[:, 256:]
        f0, f1, f2 = factors[half, 0], factors[half, 1], factors[half, 2]
        return jnp.concatenate([f0 * vort, f1 * div + f2 * geo, f1 * geo - f2 * div], axis=1)

    spec = dot3_left([to_spec[0, core], to_spec[1, core]], columns(mine_ref)) + dot3_left(
        [to_spec[0, 1 - core], to_spec[1, 1 - core]], columns(others_ref)
    )
    table = [from_spec[0, core], from_spec[1, core]]
    back = dot3_left(table, update(twice, spec))
    channels = dot3_left(
        [t.astype(BF16) for t in channel_basis(mine_ref, table)], update(once, spec)
    )
    for v in range(3):
        out_ref[:, 16 * v : 16 * v + 16, :] = back[:, 128 * v : 128 * v + 128].reshape(16, 16, 128)
        for q in range(16):
            out_ref[q, 16 * v + LAT_DEV : 16 * v + LAT_DEV + 1, :] = channels[
                q : q + 1, 128 * v : 128 * v + 128
            ]


def profile_kernel(got_ref, table, out_ref, total):
    for v in range(3):
        for u in range(8):
            for h in range(2):
                at = 16 * v + LAT_DEV
                total[8 * v + u : 8 * v + u + 1, 128 * h : 128 * h + 128] = got_ref[
                    2 * u + h, at : at + 1, :
                ]
    a, b, c = total[0:8], total[8:16], total[16:24]
    first = upper((8, M))
    cos = jnp.concatenate([jnp.where(first, a, swap4(b)), c], axis=0)
    sin = jnp.concatenate([jnp.where(first, swap4(a), b), swap4(c)], axis=0)
    lines = dot3(jnp.concatenate([cos, sin], axis=1), table)
    for s in range(SEGS):
        out_ref[s] = lines[:, 128 * s : 128 * s + 128]


def last_kernel(got_ref, table, out_ref):
    rows = received_rows([got_ref[:, 0:16, :]], table)[0]
    line = jnp.concatenate(rows, axis=0)
    for c in range(16):
        out_ref[c] = line


def add_channels(factors, half, from_ref, held):
    def row_pair(i, _):
        for h in range(2):
            j = 2 * i + h
            total = [held[v, j] for v in range(3)]
            for c in range(16):
                total = weigh(
                    total,
                    factors[c + half, pl.ds(j, 1), :],
                    [from_ref[c, 8 * v : 8 * v + 8, :] for v in range(3)],
                )
            for v in range(3):
                held[v, j] = total[v]
        return 0

    lax.fori_loop(0, LAT_DEV // 2, row_pair, 0)


def gather_kernel(got_ref, factors, from_ref, held, flat):
    for u in range(8):
        for h in range(2):
            flat[h, pl.ds(u, 48, stride=8), :] = got_ref[2 * u + h]
    for h in range(2):
        held[:, :, :, 128 * h : 128 * h + 128] = flat[h].reshape(3, 16, 8, 128)
    add_channels(factors, 0, from_ref, held)


def finish_kernel(part_ref, factors, from_ref, table, out_ref, held):
    held[...] = part_ref[...]
    add_channels(factors, 16, from_ref, held)
    first = upper((8, M))
    cos, sin = [], []
    for v in range(3):
        for i in range(6):
            even, odd = held[v, 2 * i], held[v, 2 * i + 1]
            cos.append(jnp.where(first, even, swap4(odd)))
            sin.append(jnp.where(first, swap4(even), odd))
    rows = jnp.concatenate(
        [jnp.concatenate(cos, axis=0), jnp.concatenate(sin, axis=0)], axis=1
    )
    lines = dot3(rows, table)
    for v in range(3):
        for j in range(LAT_DEV):
            for l in range(4):
                at = v * 48 + 4 * j + l
                out_ref[j, 3 * l + v : 3 * l + v + 1, :] = lines[at : at + 1]


def shape(*dims):
    return jax.ShapeDtypeStruct(dims, F32)


def rows_exchange(x):
    return lax.all_to_all(x, "lat", 0, 0, axis_index_groups=ROW_GROUPS, tiled=True)


def core_swap(x):
    return lax.ppermute(x, "lat", CORE_SWAP)


def shards(atmosphere, cloud_state, channel_lat, cell_column, channel_wind, diffusivity, mixing):
    tab = {name: jnp.asarray(value) for name, value in tables().items()}
    lat = lax.axis_index("lat").astype(jnp.int32)
    seg = lax.axis_index("seg").astype(jnp.int32)
    info = jnp.stack((seg, lat, channel_lat[0]))
    clouds = cloud_state[0]
    col = cell_column
    wind = channel_wind
    diff = diffusivity.reshape(1, K)
    spread_table = tab["forward_seg"]

    send = prepare(info, atmosphere, clouds, col)
    got = lax.all_to_all(send, "seg", 0, 0, tiled=True)
    grid, state, send = lax.optimization_barrier((atmosphere, clouds, send))
    base, mean, inv = inner(state, col, diff, wind, mixing, True)
    rows = call(
        rows_kernel, "rows", (grid, tab["forward"]), [shape(3, 16, 8, M)],
        scratch=[pltpu.VMEM((144, NLON), F32)],
    )[0]
    rows, got = lax.optimization_barrier((rows, got))
    clouds, mean_1, send = outer(
        False, info, base, state, mean, got, got, inv, col, diff, wind, mixing,
    )
    halo = lax.all_to_all(send, "seg", 0, 0, tiled=True)
    base = inner(clouds, col, diff, wind, mixing, False)[0]
    base, halo = lax.optimization_barrier((base, halo))

    spread = call(
        spread_kernel, "spread", (halo, spread_table, rows), [shape(16, 48, 128)],
        scratch=[pltpu.VMEM((2, 384, 128), F32)], prefetch=info,
    )[0]
    spec_mine = rows_exchange(spread)
    spec_others = core_swap(spec_mine)
    settled = call(
        settle_kernel, "settle",
        (spec_mine, spec_others, tab["to_spec"], tab["from_spec"], tab["once"], tab["twice"]),
        [shape(16, 48, 128)], prefetch=info,
    )[0]
    settled = rows_exchange(settled)
    profile = call(
        profile_kernel, "profile", (settled, tab["inverse_seg"]), [shape(SEGS, 16, 128)],
        scratch=[pltpu.VMEM((24, M), F32)],
    )[0]
    profile, spec_mine, spec_others = lax.optimization_barrier((profile, spec_mine, spec_others))
    factors = call(
        weights_kernel, "weights", (spec_mine, spec_others, tab["from_spec"], tab["row_weights"]),
        [shape(32, 16, 3 * M)], prefetch=info,
    )[0]
    profile = lax.all_to_all(profile, "seg", 0, 0, tiled=True)

    factors, profile = lax.optimization_barrier((factors, profile))

    clouds, _, send = outer(
        True, info, base, clouds, mean_1, profile, halo, inv, col, diff, wind, mixing,
    )
    got = lax.all_to_all(send, "seg", 0, 0, tiled=True)
    from_mine = rows_exchange(
        call(last_kernel, "last", (got, spread_table), [shape(16, 24, M)])[0]
    )
    from_others = core_swap(from_mine)
    part = call(
        gather_kernel, "gather", (settled, factors, from_mine), [shape(3, 16, 8, M)],
        scratch=[pltpu.VMEM((2, 384, 128), F32)],
    )[0]
    grid = call(
        finish_kernel, "finish", (part, factors, from_others, tab["inverse"]),
        [shape(LAT_DEV, KD, NLON)], scratch=[pltpu.VMEM((3, 16, 8, M), F32)],
    )[0]
    return grid, clouds[None]


def solution(mesh):
    placed = (
        P("lat", "seg", None),
        P("lat", None, "seg"),
        P("lat"),
        P("lat", "seg"),
        P("lat", None),
        P(),
        P(),
    )
    return jax.shard_map(
        shards,
        mesh=mesh,
        in_specs=placed,
        out_specs=(P("lat", "seg", None), P("lat", None, "seg")),
        check_vma=False,
    )
```

```python
import ml_dtypes
import numpy as np

import jax
import jax.numpy as jnp
from jax import lax
from jax.experimental import pallas as pl
from jax.experimental.pallas import tpu as pltpu
from jax.sharding import PartitionSpec as P

NLON = 768
M = 256
NT = 256
NLAT = 384
LAT_DEV = 12
K = 96
KD = 12
COLS = 96
CELLS = 6144
LATS = 32
SEGS = 8
TILE = 256
T2 = 1280
T3 = 1536
TI = 1536
EXT = CELLS + 512
CHUNK = 1536
PIECES = CELLS // CHUNK
RELAXATION = 0.5
MIXING_RATE = 0.3
DAMPING = 0.2
COUPLING = 2.0
F32 = jnp.float32
BF16 = jnp.bfloat16

ROW_GROUPS = [[2 * q + b for q in range(16)] for b in range(2)]
CORE_SWAP = [(i, i ^ 1) for i in range(LATS)]


def tables():
    m = np.arange(M)
    x = np.arange(NLON)
    angles = 2.0 * np.pi * ((m[:, None] * x[None, :]) % NLON) / NLON
    waves = np.stack([np.cos(angles), np.sin(angles)])
    sigma = np.where(m == 0, 1.0, 2.0)
    inverse = (waves * sigma[None, :, None]).reshape(2 * M, NLON)
    forward = (waves / NLON).reshape(2 * M, NLON).T
    forward_seg = np.zeros((SEGS, 128, 2 * M))
    forward_seg[:, :COLS] = forward.reshape(SEGS, COLS, 2 * M)
    inverse_seg = np.zeros((2 * M, SEGS, 128))
    for s in range(SEGS):
        inverse_seg[:, s, : COLS + 1] = inverse[:, (COLS * s + np.arange(COLS + 1)) % NLON]
        inverse_seg[:, s, COLS + 1] = inverse[:, (COLS * s - 1) % NLON]
    n = np.arange(NT)
    j = np.arange(NLAT)
    basis = np.cos(np.pi * ((n[:, None] * (2 * j[None, :] + 1)) % (4 * NLAT)) / (2 * NLAT))
    weights = np.where(n == 0, 1.0, 2.0) / NLAT
    size = (m[None, :] ** 2 + n[:, None] ** 2) / (NT * NT)
    damping = 1.0 + size * size
    coupling = COUPLING * size
    det = damping**2 + coupling**2
    keep = (m[None, :] + n[:, None] < NT).astype(np.float64)
    update = np.stack([keep / damping, keep * damping / det, keep * coupling / det])
    twice = np.stack(
        [
            keep / damping**2,
            keep * (damping**2 - coupling**2) / det**2,
            keep * 2.0 * damping * coupling / det**2,
        ]
    )
    row_weights = np.transpose(update * weights[None, :, None], (1, 0, 2)).reshape(NT, 3 * M)
    parity = basis.reshape(NT, 16, 2, LAT_DEV)
    spread = np.zeros((2, NT, 16, 16))
    spread[:, :, :, :LAT_DEV] = np.transpose(parity, (2, 0, 1, 3))
    spread = spread.reshape(2, NT, 256)
    f = np.float32
    return dict(
        forward=pair_of(forward),
        inverse=pair_of(inverse),
        forward_seg=pair_of(forward_seg.reshape(SEGS * 128, 2 * M)),
        inverse_seg=pair_of(inverse_seg.reshape(2 * M, SEGS * 128)),
        to_spec=pair_of(spread * weights[None, :, None]),
        from_spec=pair_of(np.transpose(spread, (0, 2, 1))),
        once=np.ascontiguousarray(np.transpose(update.reshape(3, NT, 2, 128), (2, 0, 1, 3))).astype(f),
        twice=np.ascontiguousarray(np.transpose(twice.reshape(3, NT, 2, 128), (2, 0, 1, 3))).astype(f),
        row_weights=pair_of(row_weights),
    )


def pair_of(x):
    x = x.astype(np.float32)
    high = x.astype(ml_dtypes.bfloat16)
    low = (x - high.astype(np.float32)).astype(ml_dtypes.bfloat16)
    return np.stack((high, low))


def lanes_of(shape):
    return lax.broadcasted_iota(jnp.int32, shape, len(shape) - 1)


def split(x):
    high = x.astype(BF16)
    low = (x - high.astype(F32)).astype(BF16)
    return high, low


def mixing_block(mixing):
    high, low = split(MIXING_RATE * mixing)
    return jnp.concatenate(
        [jnp.concatenate([high, high], axis=1), jnp.concatenate([low, low], axis=1)], axis=0
    )


def substep_tile(window, mix, diffusivity, wind):
    width = window.shape[1]
    center = window[:, 128 : width - 128]
    right = pltpu.roll(window, width - 1, 1)[:, 128 : width - 128]
    left = pltpu.roll(window, 1, 1)[:, 128 : width - 128]
    high, low = split(center)
    mixed = jnp.dot(mix, jnp.concatenate([high, low], axis=0), preferred_element_type=F32)
    return (
        center
        + diffusivity * (right - 2.0 * center + left)
        - 0.5 * wind * (right - left)
        + (mixed[:K] + mixed[K:])
        - DAMPING * jnp.tanh(center)
    )


def column_hits(col):
    ids = lax.broadcasted_iota(jnp.int32, (128, col.shape[1]), 0)
    return jnp.where(ids == col, 1.0, 0.0).astype(BF16)


def row_order(grouped, transposed):
    size = (SEGS * 16, K) if transposed else (K, SEGS * 16)
    pair = lax.broadcasted_iota(jnp.int32, size, 1 if transposed else 0)
    row = lax.broadcasted_iota(jnp.int32, size, 0 if transposed else 1)
    owner = (pair * 43691) >> 19
    within = pair - KD * owner
    level = (within * 11) >> 5
    place_in = (within - 3 * level) * 4 + level if grouped else within
    return jnp.where(row == 16 * owner + place_in, 1.0, 0.0).astype(BF16)


def reorder(matrix, x):
    high, low = split(x)
    rest = (x - high.astype(F32) - low.astype(F32)).astype(BF16)
    width = x.shape[1]
    out = jnp.dot(matrix, jnp.concatenate([high, low, rest], axis=1), preferred_element_type=F32)
    return out[:, :width] + out[:, width : 2 * width] + out[:, 2 * width :]


def edge_rows(first, last, mean_first, mean_last):
    lane = lanes_of((K, 128))
    edge = jnp.where(
        lane < 3,
        first,
        jnp.where(
            lane < 6, pltpu.roll(last, 6, 1), jnp.where(lane == 6, mean_first, mean_last)
        ),
    )
    padded = jnp.concatenate([edge, jnp.zeros((32, 128), F32)], axis=0)
    return padded.T[:8]


def place(info):
    lat = lax.axis_index("lat")
    return lax.rem(lat, 2), lax.div(lat, 2), info[0]


def prepare_kernel(info, row_ref, first_ref, last_ref, colf_ref, coll_ref, send_ref):
    del info
    row = row_ref[0]
    lane = lanes_of((KD, 128))
    hit_first = jnp.where(colf_ref[...] == 0, 1.0, 0.0)
    hit_last = jnp.where(coll_ref[...] == COLS - 1, 1.0, 0.0)
    first, last = first_ref[...], last_ref[...]
    mean_first = jnp.sum(first * hit_first, axis=1, keepdims=True) / jnp.sum(
        hit_first, axis=1, keepdims=True
    )
    mean_last = jnp.sum(last * hit_last, axis=1, keepdims=True) / jnp.sum(
        hit_last, axis=1, keepdims=True
    )
    edge = edge_rows(first, last, mean_first, mean_last)
    for s in range(SEGS):
        own = pltpu.roll(row, (NLON - COLS * s) % NLON, 1)[:, :128]
        before = pltpu.roll(row, (COLS + 1 - (COLS * s - 1)) % NLON, 1)[:, :128]
        chunk = jnp.where(lane <= COLS, own, jnp.where(lane == COLS + 1, before, 0.0))
        send_ref[s, 0:KD, :] = chunk
        send_ref[s, KD:16, :] = jnp.zeros((16 - KD, 128), F32)
        send_ref[s, 16:24, :] = edge


def prepare(info, atmosphere, clouds, col):
    last = CELLS // 128 - 1
    return pl.pallas_call(
        prepare_kernel,
        grid_spec=pltpu.PrefetchScalarGridSpec(
            num_scalar_prefetch=1,
            grid=(1,),
            in_specs=[
                pl.BlockSpec((1, KD, NLON), lambda i, info: (info[0], 0, 0)),
                pl.BlockSpec((K, 128), lambda i, off: (0, 0)),
                pl.BlockSpec((K, 128), lambda i, off: (0, last)),
                pl.BlockSpec((1, 128), lambda i, off: (0, 0)),
                pl.BlockSpec((1, 128), lambda i, off: (0, last)),
            ],
            out_specs=pl.BlockSpec((SEGS, 24, 128), lambda i, off: (0, 0, 0)),
        ),
        out_shape=jax.ShapeDtypeStruct((SEGS, 24, 128), F32),
        name="prepare",
    )(info, atmosphere, clouds, clouds, col, col)


def column_of(row):
    size = row.shape[1]
    diagonal = lax.broadcasted_iota(jnp.int32, (size, size), 0) == lanes_of((size, size))
    return jnp.sum(jnp.where(diagonal, row, 0.0), axis=1, keepdims=True)


def pieces(source, target, sems, shift=0):
    return [
        pltpu.make_async_copy(
            source.at[:, i * CHUNK : (i + 1) * CHUNK],
            target.at[:, shift + i * CHUNK : shift + (i + 1) * CHUNK],
            sems.at[i],
        )
        for i in range(PIECES)
    ]


def inner_kernel(with_mean, *refs):
    if with_mean:
        c_hbm, col_ref, diff_ref, wind_ref, mixing_ref, base_hbm, mean_hbm, inv_ref = refs[:8]
        mean_ref, mean_sem = refs[8:10]
    else:
        c_hbm, diff_ref, wind_ref, mixing_ref, base_hbm = refs[:5]
    c_ref, base_ref, in_sems, out_sems = refs[-4:]
    reads = pieces(c_hbm, c_ref, in_sems)
    writes = pieces(base_ref, base_hbm, out_sems)
    for copy in reads:
        copy.start()
    zeros = jnp.zeros((K, 128), F32)
    mix = mixing_block(mixing_ref[...])
    diffusivity, wind = column_of(diff_ref[...]), column_of(wind_ref[...])
    total = jnp.zeros((2 * K + 16, 128), F32)
    reads[0].wait()
    for start in range(0, CELLS, TI):
        if start % CHUNK == 0 and start // CHUNK + 1 < PIECES:
            reads[start // CHUNK + 1].wait()
        window = c_ref[:, max(start - 128, 0) : min(start + TI + 128, CELLS)]
        if start == 0:
            window = jnp.concatenate([zeros, window], axis=1)
        if start + TI == CELLS:
            window = jnp.concatenate([window, zeros], axis=1)
        base_ref[:, start : start + TI] = substep_tile(window, mix, diffusivity, wind)
        if (start + TI) % CHUNK == 0:
            writes[start // CHUNK].start()
        if with_mean:
            hits = column_hits(col_ref[:, start : start + TI])
            high, low = split(window[:, 128 : 128 + TI])
            rows = jnp.concatenate([high, low, jnp.ones((16, TI), BF16)], axis=0)
            total = total + lax.dot_general(
                rows, hits, (((1,), (1,)), ((), ())), preferred_element_type=F32
            )
    if with_mean:
        counts = total[2 * K : 2 * K + 8]
        inv = jnp.where(counts > 0.0, 1.0 / jnp.maximum(counts, 1.0), 0.0)
        inv_ref[...] = inv
        mean_ref[...] = (total[:K] + total[K : 2 * K]) * inv[0:1]
        mean_write = pltpu.make_async_copy(mean_ref, mean_hbm, mean_sem)
        mean_write.start()
        mean_write.wait()
    for copy in writes:
        copy.wait()


VMEM_SPEC = pl.BlockSpec(memory_space=pltpu.VMEM)
HBM_SPEC = pl.BlockSpec(memory_space=pltpu.HBM)
MEAN_SCRATCH = [pltpu.VMEM((K, 128), F32), pltpu.SemaphoreType.DMA]


def in_hbm(x):
    return pltpu.with_memory_space_constraint(x, pltpu.HBM)


STATE_SCRATCH = [
    pltpu.VMEM((K, CELLS), F32),
    pltpu.VMEM((K, CELLS), F32),
    pltpu.SemaphoreType.DMA((PIECES,)),
    pltpu.SemaphoreType.DMA((PIECES,)),
]


def inner(clouds, col, diffusivity, wind, mixing, with_mean):
    args = [in_hbm(clouds)] + ([col] if with_mean else []) + [diffusivity, wind, mixing]
    shapes = [pltpu.HBM((K, CELLS), F32)]
    if with_mean:
        shapes += [pltpu.HBM((K, 128), F32), jax.ShapeDtypeStruct((8, 128), F32)]
    return pl.pallas_call(
        lambda *refs: inner_kernel(with_mean, *refs),
        in_specs=[HBM_SPEC] + [VMEM_SPEC] * (len(args) - 1),
        out_specs=([HBM_SPEC, HBM_SPEC, VMEM_SPEC] if with_mean else [HBM_SPEC]),
        out_shape=shapes,
        scratch_shapes=MEAN_SCRATCH * with_mean + STATE_SCRATCH,
        cost_estimate=pl.CostEstimate(flops=1 << 10, bytes_accessed=1 << 10, transcendentals=0),
        compiler_params=pltpu.CompilerParams(vmem_limit_bytes=10 << 20),
        name="inner",
    )(*args)


def outer_kernel(
    grouped, info, base_hbm, c_hbm, mean_hbm, prof_ref, halo_ref, inv_ref, col_ref, diff_ref, wind_ref,
    mixing_ref, out_hbm, end_hbm, send_ref, ext1, ext2, force, ends_ref, mean_ref, end_ref, small_sems,
    out_ref, in_sems, out_sems,
):
    seg = lax.axis_index("seg")
    reads = pieces(base_hbm, ext1, in_sems, 256)
    ends = [
        pltpu.make_async_copy(
            c_hbm.at[:, at : at + 256], ends_ref.at[:, 256 * i : 256 * i + 256], small_sems.at[i]
        )
        for i, at in enumerate((0, CELLS - 256))
    ]
    mean_read = pltpu.make_async_copy(mean_hbm, mean_ref, small_sems.at[2])
    mean_read.start()
    end_write = pltpu.make_async_copy(end_ref, end_hbm, small_sems.at[3])
    for copy in ends:
        copy.start()
    writes = pieces(out_ref, out_hbm, out_sems)
    for copy in reads:
        copy.start()
    lane = lanes_of((K, 128))
    zeros = jnp.zeros((K, 128), F32)
    mix = mixing_block(mixing_ref[...])
    diffusivity, wind = column_of(diff_ref[...]), column_of(wind_ref[...])

    from_left = halo_ref[lax.rem(seg + SEGS - 1, SEGS), 16:24, :]
    from_right = halo_ref[lax.rem(seg + 1, SEGS), 16:24, :]
    edges = jnp.concatenate([from_left, from_right, jnp.zeros((112, 128), F32)], axis=0).T[:K]
    left_tile = jnp.where(lane >= 125, pltpu.roll(edges, 122, 1), 0.0)
    right_tile = jnp.where(lane < 3, pltpu.roll(edges, 120, 1), 0.0)
    mean_read.wait()
    mean = mean_ref[...]
    mean_all = jnp.where(
        lane < COLS,
        mean,
        jnp.where(
            lane == COLS,
            pltpu.roll(edges, COLS - 14, 1),
            jnp.where(lane == COLS + 1, pltpu.roll(edges, COLS + 1 - 7, 1), 0.0),
        ),
    )
    profile = reorder(
        row_order(grouped, False), prof_ref[:, 0:16, :].reshape(SEGS * 16, 128)
    )
    pulled = jnp.where(lane < COLS + 2, RELAXATION * (profile - mean_all), 0.0)
    pulled = jnp.concatenate(split(pulled), axis=1)

    ext1[:, 0:128] = zeros
    ext1[:, EXT - 128 :] = zeros
    left_col = jnp.full((1, 128), COLS + 1, jnp.int32)
    right_col = jnp.full((1, 128), COLS, jnp.int32)
    for at in range(128, EXT - 128, TILE):
        cell = at - 256
        if cell < 0:
            col = jnp.concatenate([left_col, col_ref[:, 0:128]], axis=1)
        elif cell + TILE > CELLS:
            col = jnp.concatenate([col_ref[:, CELLS - 128 :], right_col], axis=1)
        else:
            col = col_ref[:, cell : cell + TILE]
        hits = column_hits(col)
        force[:, at : at + TILE] = jnp.dot(
            pulled, jnp.concatenate([hits, hits], axis=0), preferred_element_type=F32
        )

    for at in range(128, EXT - 128, TILE):
        cell = at - 256
        if (cell + 128) % CHUNK == 0 and (cell + 128) // CHUNK < PIECES:
            reads[(cell + 128) // CHUNK].wait()
        if cell < 0:
            ends[0].wait()
            window = jnp.concatenate([zeros, left_tile, ends_ref[:, 0:256]], axis=1)
            value = substep_tile(window, mix, diffusivity, wind)
        elif cell + TILE > CELLS:
            ends[1].wait()
            window = jnp.concatenate([ends_ref[:, 256:512], right_tile, zeros], axis=1)
            value = substep_tile(window, mix, diffusivity, wind)
        else:
            value = ext1[:, at : at + TILE]
        ext1[:, at : at + TILE] = value + force[:, at : at + TILE]

    for at in range(128, EXT - 128, T2):
        window = ext1[:, at - 128 : at + T2 + 128]
        ext2[:, at : at + T2] = (
            substep_tile(window, mix, diffusivity, wind) + force[:, at : at + T2]
        )

    total = jnp.zeros((2 * K, 128), F32)
    for cell in range(0, CELLS, T3):
        at = cell + 256
        window = ext2[:, at - 128 : at + T3 + 128]
        value = substep_tile(window, mix, diffusivity, wind) + force[:, at : at + T3]
        out_ref[:, cell : cell + T3] = value
        if (cell + T3) % CHUNK == 0:
            writes[cell // CHUNK].start()
        hits = column_hits(col_ref[:, cell : cell + T3])
        rows = jnp.concatenate(split(value), axis=0)
        total = total + lax.dot_general(
            rows, hits, (((1,), (1,)), ((), ())), preferred_element_type=F32
        )
    end = (total[:K] + total[K:]) * inv_ref[0:1]
    end_ref[...] = end
    end_write.start()
    tendency = jnp.where(lane < COLS, end - mean, 0.0)
    sent = reorder(row_order(True, True), tendency)
    edge = edge_rows(
        out_ref[:, 0:128], out_ref[:, CELLS - 128 :], end[:, 0:1], end[:, COLS - 1 : COLS]
    )
    for s in range(send_ref.shape[0]):
        send_ref[s, 0:16, :] = sent[16 * (s % SEGS) : 16 * (s % SEGS) + 16]
        send_ref[s, 16:24, :] = edge
    end_write.wait()
    for copy in writes:
        copy.wait()


def outer(grouped, info, base, clouds, mean, *args):
    return call(
        lambda *refs: outer_kernel(grouped, *refs), "outer",
        (in_hbm(base), in_hbm(clouds), in_hbm(mean), *args),
        [pltpu.HBM((K, CELLS), F32), pltpu.HBM((K, 128), F32), shape(SEGS, 24, 128)],
        scratch=[pltpu.VMEM((K, EXT), F32)] * 3
        + [pltpu.VMEM((K, 512), F32), pltpu.VMEM((K, 128), F32), pltpu.VMEM((K, 128), F32)]
        + [pltpu.SemaphoreType.DMA((4,))]
        + STATE_SCRATCH[1:],
        prefetch=info, limit=16, hbm=(3, 2),
    )


def upper(shape):
    return lax.broadcasted_iota(jnp.int32, shape, len(shape) - 2) % 8 < 4


def swap4(x):
    tiles = x.reshape(-1, 8, x.shape[-1])
    return pltpu.roll(tiles, 4, 1).reshape(x.shape)


def dot3(x, table):
    high, low = split(x)
    rows = x.shape[0]
    both = jnp.dot(jnp.concatenate([high, low], axis=0), table[0], preferred_element_type=F32)
    return both[:rows] + both[rows:] + jnp.dot(high, table[1], preferred_element_type=F32)


def dot3_left(table, x):
    high, low = split(x)
    cols = x.shape[1]
    both = jnp.dot(table[0], jnp.concatenate([high, low], axis=1), preferred_element_type=F32)
    return both[:, :cols] + both[:, cols:] + jnp.dot(table[1], high, preferred_element_type=F32)


def received_rows(chunks, table):
    rows = jnp.concatenate(
        [jnp.concatenate([c[s] for s in range(SEGS)], axis=1) for c in chunks], axis=0
    )
    coeffs = dot3(rows, table)
    out = []
    first = upper((8, M))
    for a in range(len(chunks)):
        c = [coeffs[16 * a + 8 * i : 16 * a + 8 * i + 8, :M] for i in range(2)]
        s = [coeffs[16 * a + 8 * i : 16 * a + 8 * i + 8, M:] for i in range(2)]
        out.append(
            [
                jnp.where(first, c[0], swap4(s[0])),
                jnp.where(first, swap4(c[0]), s[0]),
                jnp.where(first, c[1], swap4(s[1])),
            ]
        )
    return out


def weigh(total, factors, rows):
    vort, mix, turn = factors[:, :M], factors[:, M : 2 * M], factors[:, 2 * M :]
    return [
        total[0] + vort * rows[0],
        total[1] + (mix * rows[1] + turn * rows[2]),
        total[2] + (mix * rows[2] - turn * rows[1]),
    ]


def call(kernel, name, args, shapes, scratch=(), prefetch=None, limit=8, hbm=(0, 0)):
    specs = [VMEM_SPEC] * len(args)
    common = dict(
        out_shape=shapes,
        name=name,
        cost_estimate=pl.CostEstimate(flops=1 << 10, bytes_accessed=1 << 10, transcendentals=0),
        compiler_params=pltpu.CompilerParams(vmem_limit_bytes=limit << 20),
    )
    outs = [VMEM_SPEC] * len(shapes)
    specs[: hbm[0]] = [HBM_SPEC] * hbm[0]
    outs[: hbm[1]] = [HBM_SPEC] * hbm[1]
    if prefetch is None:
        return pl.pallas_call(
            kernel, in_specs=specs, out_specs=outs, scratch_shapes=list(scratch), **common
        )(*args)
    return pl.pallas_call(
        kernel,
        grid_spec=pltpu.PrefetchScalarGridSpec(
            num_scalar_prefetch=1, grid=(), in_specs=specs, out_specs=outs,
            scratch_shapes=list(scratch),
        ),
        **common,
    )(prefetch, *args)


def rows_kernel(grid_ref, table, rows_ref, lines):
    for v in range(3):
        for j in range(LAT_DEV):
            for l in range(4):
                at = v * 48 + 4 * j + l
                lines[at : at + 1, :] = grid_ref[j, 3 * l + v : 3 * l + v + 1, :]
    coeffs = dot3(lines[...], table)
    cos, sin = coeffs[:, :M], coeffs[:, M:]
    first = upper((144, M))
    even = jnp.where(first, cos, swap4(sin))
    odd = jnp.where(first, swap4(cos), sin)
    for v in range(3):
        for i in range(6):
            at = v * 48 + 8 * i
            rows_ref[v, 2 * i] = even[at : at + 8]
            rows_ref[v, 2 * i + 1] = odd[at : at + 8]
        for j in range(LAT_DEV, 16):
            rows_ref[v, j] = jnp.zeros((8, M), F32)


def spread_kernel(info, got_ref, table, rows_ref, send_ref, held):
    offset = place(info)[2]
    forced = received_rows([got_ref[:, 0:16, :]], table)[0]
    for h in range(2):
        held[h] = rows_ref[:, :, :, 128 * h : 128 * h + 128].reshape(384, 128)
        for v in range(3):
            at = pl.ds(pl.multiple_of((v * 16 + offset) * 8, 8), 8)
            held[h, at, :] += forced[v][:, 128 * h : 128 * h + 128]
        held[h, LAT_DEV * 8 : LAT_DEV * 8 + 8, :] = jnp.full((8, 128), offset, jnp.int32).astype(F32)
    for u in range(8):
        for h in range(2):
            send_ref[2 * u + h] = held[h, pl.ds(u, 48, stride=8), :]


def channel_basis(spec_ref, table):
    offsets = spec_ref[:, LAT_DEV, :][:, 0:1].astype(jnp.int32)
    wanted = 16 * lax.broadcasted_iota(jnp.int32, (16, 256), 0) + offsets
    picks = jnp.where(lanes_of((16, 256)) == wanted, 1.0, 0.0).astype(BF16)
    return [jnp.dot(picks, t, preferred_element_type=F32) for t in table]


def weights_kernel(info, mine_ref, others_ref, from_spec, row_weights, out_ref):
    core, chip, _ = place(info)
    own = pl.ds(pl.multiple_of(chip * 16, 16), 16)
    here = from_spec[0, core, own, :].astype(F32) + from_spec[1, core, own, :].astype(F32)
    for half, ref, side in ((0, mine_ref, core), (16, others_ref, 1 - core)):
        high, low = channel_basis(ref, [from_spec[0, side], from_spec[1, side]])
        basis = high + low
        products = jnp.concatenate([basis[c : c + 1] * here for c in range(16)], axis=0)
        out_ref[half : half + 16] = dot3(products, row_weights).reshape(16, 16, 3 * M)


def settle_kernel(info, mine_ref, others_ref, to_spec, from_spec, once, twice, out_ref):
    core, chip, _ = place(info)
    half = lax.rem(chip, 2)

    def columns(ref):
        return jnp.concatenate(
            [ref[:, 16 * v : 16 * v + 16, :].reshape(256, 128) for v in range(3)], axis=1
        )

    def update(factors, spec):
        vort, div, geo = spec[:, :128], spec[:, 128:256], spec[:, 256:]
        f0, f1, f2 = factors[half, 0], factors[half, 1], factors[half, 2]
        return jnp.concatenate([f0 * vort, f1 * div + f2 * geo, f1 * geo - f2 * div], axis=1)

    spec = dot3_left([to_spec[0, core], to_spec[1, core]], columns(mine_ref)) + dot3_left(
        [to_spec[0, 1 - core], to_spec[1, 1 - core]], columns(others_ref)
    )
    table = [from_spec[0, core], from_spec[1, core]]
    back = dot3_left(table, update(twice, spec))
    channels = dot3_left(
        [t.astype(BF16) for t in channel_basis(mine_ref, table)], update(once, spec)
    )
    for v in range(3):
        out_ref[:, 16 * v : 16 * v + 16, :] = back[:, 128 * v : 128 * v + 128].reshape(16, 16, 128)
        for q in range(16):
            out_ref[q, 16 * v + LAT_DEV : 16 * v + LAT_DEV + 1, :] = channels[
                q : q + 1, 128 * v : 128 * v + 128
            ]


def profile_kernel(got_ref, table, out_ref, total):
    for v in range(3):
        for u in range(8):
            for h in range(2):
                at = 16 * v + LAT_DEV
                total[8 * v + u : 8 * v + u + 1, 128 * h : 128 * h + 128] = got_ref[
                    2 * u + h, at : at + 1, :
                ]
    a, b, c = total[0:8], total[8:16], total[16:24]
    first = upper((8, M))
    cos = jnp.concatenate([jnp.where(first, a, swap4(b)), c], axis=0)
    sin = jnp.concatenate([jnp.where(first, swap4(a), b), swap4(c)], axis=0)
    lines = dot3(jnp.concatenate([cos, sin], axis=1), table)
    for s in range(SEGS):
        out_ref[s] = lines[:, 128 * s : 128 * s + 128]


def last_kernel(got_ref, table, out_ref):
    rows = received_rows([got_ref[:, 0:16, :]], table)[0]
    line = jnp.concatenate(rows, axis=0)
    for c in range(16):
        out_ref[c] = line


def add_channels(factors, half, from_ref, held):
    def row_pair(i, _):
        for h in range(2):
            j = 2 * i + h
            total = [held[v, j] for v in range(3)]
            for c in range(16):
                total = weigh(
                    total,
                    factors[c + half, pl.ds(j, 1), :],
                    [from_ref[c, 8 * v : 8 * v + 8, :] for v in range(3)],
                )
            for v in range(3):
                held[v, j] = total[v]
        return 0

    lax.fori_loop(0, LAT_DEV // 2, row_pair, 0)


def gather_kernel(got_ref, factors, from_ref, held, flat):
    for u in range(8):
        for h in range(2):
            flat[h, pl.ds(u, 48, stride=8), :] = got_ref[2 * u + h]
    for h in range(2):
        held[:, :, :, 128 * h : 128 * h + 128] = flat[h].reshape(3, 16, 8, 128)
    add_channels(factors, 0, from_ref, held)


def finish_kernel(part_ref, factors, from_ref, table, out_ref, held):
    held[...] = part_ref[...]
    add_channels(factors, 16, from_ref, held)
    first = upper((8, M))
    cos, sin = [], []
    for v in range(3):
        for i in range(6):
            even, odd = held[v, 2 * i], held[v, 2 * i + 1]
            cos.append(jnp.where(first, even, swap4(odd)))
            sin.append(jnp.where(first, swap4(even), odd))
    rows = jnp.concatenate(
        [jnp.concatenate(cos, axis=0), jnp.concatenate(sin, axis=0)], axis=1
    )
    lines = dot3(rows, table)
    for v in range(3):
        for j in range(LAT_DEV):
            for l in range(4):
                at = v * 48 + 4 * j + l
                out_ref[j, 3 * l + v : 3 * l + v + 1, :] = lines[at : at + 1]


def shape(*dims):
    return jax.ShapeDtypeStruct(dims, F32)


def rows_exchange(x):
    return lax.all_to_all(x, "lat", 0, 0, axis_index_groups=ROW_GROUPS, tiled=True)


def core_swap(x):
    return lax.ppermute(x, "lat", CORE_SWAP)


def shards(atmosphere, cloud_state, channel_lat, cell_column, channel_wind, diffusivity, mixing):
    tab = {name: jnp.asarray(value) for name, value in tables().items()}
    lat = lax.axis_index("lat").astype(jnp.int32)
    info = channel_lat - lat * LAT_DEV
    clouds = cloud_state[0]
    col = cell_column
    wind = channel_wind
    diff = diffusivity.reshape(1, K)
    spread_table = tab["forward_seg"]

    send = prepare(info, atmosphere, clouds, col)
    got = lax.all_to_all(send, "seg", 0, 0, tiled=True)
    grid, state, send = lax.optimization_barrier((atmosphere, clouds, send))
    base, mean, inv = inner(state, col, diff, wind, mixing, True)
    rows = call(
        rows_kernel, "rows", (grid, tab["forward"]), [shape(3, 16, 8, M)],
        scratch=[pltpu.VMEM((144, NLON), F32)],
    )[0]
    rows, got = lax.optimization_barrier((rows, got))
    clouds, mean_1, send = outer(
        False, info, base, state, mean, got, got, inv, col, diff, wind, mixing,
    )
    halo = lax.all_to_all(send, "seg", 0, 0, tiled=True)
    base = inner(clouds, col, diff, wind, mixing, False)[0]
    base, halo = lax.optimization_barrier((base, halo))

    spread = call(
        spread_kernel, "spread", (halo, spread_table, rows), [shape(16, 48, 128)],
        scratch=[pltpu.VMEM((2, 384, 128), F32)], prefetch=info,
    )[0]
    spec_mine = rows_exchange(spread)
    spec_others = core_swap(spec_mine)
    settled = call(
        settle_kernel, "settle",
        (spec_mine, spec_others, tab["to_spec"], tab["from_spec"], tab["once"], tab["twice"]),
        [shape(16, 48, 128)], prefetch=info,
    )[0]
    settled = rows_exchange(settled)
    profile = call(
        profile_kernel, "profile", (settled, tab["inverse_seg"]), [shape(SEGS, 16, 128)],
        scratch=[pltpu.VMEM((24, M), F32)],
    )[0]
    profile, spec_mine, spec_others = lax.optimization_barrier((profile, spec_mine, spec_others))
    factors = call(
        weights_kernel, "weights", (spec_mine, spec_others, tab["from_spec"], tab["row_weights"]),
        [shape(32, 16, 3 * M)], prefetch=info,
    )[0]
    profile = lax.all_to_all(profile, "seg", 0, 0, tiled=True)

    factors, profile = lax.optimization_barrier((factors, profile))

    clouds, _, send = outer(
        True, info, base, clouds, mean_1, profile, halo, inv, col, diff, wind, mixing,
    )
    got = lax.all_to_all(send, "seg", 0, 0, tiled=True)
    from_mine = rows_exchange(
        call(last_kernel, "last", (got, spread_table), [shape(16, 24, M)])[0]
    )
    from_others = core_swap(from_mine)
    part = call(
        gather_kernel, "gather", (settled, factors, from_mine), [shape(3, 16, 8, M)],
        scratch=[pltpu.VMEM((2, 384, 128), F32)],
    )[0]
    grid = call(
        finish_kernel, "finish", (part, factors, from_others, tab["inverse"]),
        [shape(LAT_DEV, KD, NLON)], scratch=[pltpu.VMEM((3, 16, 8, M), F32)],
    )[0]
    return grid, clouds[None]


def solution(mesh):
    placed = (
        P("lat", "seg", None),
        P("lat", None, "seg"),
        P("lat"),
        P("lat", "seg"),
        P("lat", None),
        P(),
        P(),
    )
    return jax.shard_map(
        shards,
        mesh=mesh,
        in_specs=placed,
        out_specs=(P("lat", "seg", None), P("lat", None, "seg")),
        check_vma=False,
    )
```

```python
import ml_dtypes
import numpy as np

import jax
import jax.numpy as jnp
from jax import lax
from jax.experimental import pallas as pl
from jax.experimental.pallas import tpu as pltpu
from jax.sharding import PartitionSpec as P

NLON = 768
M = 256
NT = 256
NLAT = 384
LAT_DEV = 12
K = 96
KD = 12
COLS = 96
CELLS = 6144
LATS = 32
SEGS = 8
TILE = 256
T2 = 1280
T3 = 2048
TI = 2048
EXT = CELLS + 512
CHUNK = 2048
PIECES = CELLS // CHUNK
RELAXATION = 0.5
MIXING_RATE = 0.3
DAMPING = 0.2
COUPLING = 2.0
F32 = jnp.float32
BF16 = jnp.bfloat16

ROW_GROUPS = [[2 * q + b for q in range(16)] for b in range(2)]
CORE_SWAP = [(i, i ^ 1) for i in range(LATS)]


def tables():
    m = np.arange(M)
    x = np.arange(NLON)
    angles = 2.0 * np.pi * ((m[:, None] * x[None, :]) % NLON) / NLON
    waves = np.stack([np.cos(angles), np.sin(angles)])
    sigma = np.where(m == 0, 1.0, 2.0)
    inverse = (waves * sigma[None, :, None]).reshape(2 * M, NLON)
    forward = (waves / NLON).reshape(2 * M, NLON).T
    forward_seg = np.zeros((SEGS, 128, 2 * M))
    forward_seg[:, :COLS] = forward.reshape(SEGS, COLS, 2 * M)
    inverse_seg = np.zeros((2 * M, SEGS, 128))
    for s in range(SEGS):
        inverse_seg[:, s, : COLS + 1] = inverse[:, (COLS * s + np.arange(COLS + 1)) % NLON]
        inverse_seg[:, s, COLS + 1] = inverse[:, (COLS * s - 1) % NLON]
    n = np.arange(NT)
    j = np.arange(NLAT)
    basis = np.cos(np.pi * ((n[:, None] * (2 * j[None, :] + 1)) % (4 * NLAT)) / (2 * NLAT))
    weights = np.where(n == 0, 1.0, 2.0) / NLAT
    size = (m[None, :] ** 2 + n[:, None] ** 2) / (NT * NT)
    damping = 1.0 + size * size
    coupling = COUPLING * size
    det = damping**2 + coupling**2
    keep = (m[None, :] + n[:, None] < NT).astype(np.float64)
    update = np.stack([keep / damping, keep * damping / det, keep * coupling / det])
    twice = np.stack(
        [
            keep / damping**2,
            keep * (damping**2 - coupling**2) / det**2,
            keep * 2.0 * damping * coupling / det**2,
        ]
    )
    row_weights = np.transpose(update * weights[None, :, None], (1, 0, 2)).reshape(NT, 3 * M)
    parity = basis.reshape(NT, 16, 2, LAT_DEV)
    spread = np.zeros((2, NT, 16, 16))
    spread[:, :, :, :LAT_DEV] = np.transpose(parity, (2, 0, 1, 3))
    spread = spread.reshape(2, NT, 256)
    f = np.float32
    return dict(
        forward=pair_of(forward),
        inverse=pair_of(inverse),
        forward_seg=pair_of(forward_seg.reshape(SEGS * 128, 2 * M)),
        inverse_seg=pair_of(inverse_seg.reshape(2 * M, SEGS * 128)),
        to_spec=pair_of(spread * weights[None, :, None]),
        from_spec=pair_of(np.transpose(spread, (0, 2, 1))),
        once=np.ascontiguousarray(np.transpose(update.reshape(3, NT, 2, 128), (2, 0, 1, 3))).astype(f),
        twice=np.ascontiguousarray(np.transpose(twice.reshape(3, NT, 2, 128), (2, 0, 1, 3))).astype(f),
        row_weights=pair_of(row_weights),
    )


def pair_of(x):
    x = x.astype(np.float32)
    high = x.astype(ml_dtypes.bfloat16)
    low = (x - high.astype(np.float32)).astype(ml_dtypes.bfloat16)
    return np.stack((high, low))


def lanes_of(shape):
    return lax.broadcasted_iota(jnp.int32, shape, len(shape) - 1)


def split(x):
    high = x.astype(BF16)
    low = (x - high.astype(F32)).astype(BF16)
    return high, low


def mixing_block(mixing):
    high, low = split(MIXING_RATE * mixing)
    return jnp.concatenate(
        [jnp.concatenate([high, high], axis=1), jnp.concatenate([low, low], axis=1)], axis=0
    )


def substep_tile(window, mix, diffusivity, wind):
    width = window.shape[1]
    center = window[:, 128 : width - 128]
    right = pltpu.roll(window, width - 1, 1)[:, 128 : width - 128]
    left = pltpu.roll(window, 1, 1)[:, 128 : width - 128]
    high, low = split(center)
    mixed = jnp.dot(mix, jnp.concatenate([high, low], axis=0), preferred_element_type=F32)
    return (
        center
        + diffusivity * (right - 2.0 * center + left)
        - 0.5 * wind * (right - left)
        + (mixed[:K] + mixed[K:])
        - DAMPING * jnp.tanh(center)
    )


def column_hits(col):
    ids = lax.broadcasted_iota(jnp.int32, (128, col.shape[1]), 0)
    return jnp.where(ids == col, 1.0, 0.0).astype(BF16)


def row_order(grouped, transposed):
    size = (SEGS * 16, K) if transposed else (K, SEGS * 16)
    pair = lax.broadcasted_iota(jnp.int32, size, 1 if transposed else 0)
    row = lax.broadcasted_iota(jnp.int32, size, 0 if transposed else 1)
    owner = (pair * 43691) >> 19
    within = pair - KD * owner
    level = (within * 11) >> 5
    place_in = (within - 3 * level) * 4 + level if grouped else within
    return jnp.where(row == 16 * owner + place_in, 1.0, 0.0).astype(BF16)


def reorder(matrix, x):
    high, low = split(x)
    rest = (x - high.astype(F32) - low.astype(F32)).astype(BF16)
    width = x.shape[1]
    out = jnp.dot(matrix, jnp.concatenate([high, low, rest], axis=1), preferred_element_type=F32)
    return out[:, :width] + out[:, width : 2 * width] + out[:, 2 * width :]


def edge_rows(first, last, mean_first, mean_last):
    lane = lanes_of((K, 128))
    edge = jnp.where(
        lane < 3,
        first,
        jnp.where(
            lane < 6, pltpu.roll(last, 6, 1), jnp.where(lane == 6, mean_first, mean_last)
        ),
    )
    padded = jnp.concatenate([edge, jnp.zeros((32, 128), F32)], axis=0)
    return padded.T[:8]


def place(info):
    lat = lax.axis_index("lat")
    return lax.rem(lat, 2), lax.div(lat, 2), info[0]


def prepare_kernel(info, row_ref, first_ref, last_ref, colf_ref, coll_ref, send_ref):
    del info
    row = row_ref[0]
    lane = lanes_of((KD, 128))
    hit_first = jnp.where(colf_ref[...] == 0, 1.0, 0.0)
    hit_last = jnp.where(coll_ref[...] == COLS - 1, 1.0, 0.0)
    first, last = first_ref[...], last_ref[...]
    mean_first = jnp.sum(first * hit_first, axis=1, keepdims=True) / jnp.sum(
        hit_first, axis=1, keepdims=True
    )
    mean_last = jnp.sum(last * hit_last, axis=1, keepdims=True) / jnp.sum(
        hit_last, axis=1, keepdims=True
    )
    edge = edge_rows(first, last, mean_first, mean_last)
    for s in range(SEGS):
        own = pltpu.roll(row, (NLON - COLS * s) % NLON, 1)[:, :128]
        before = pltpu.roll(row, (COLS + 1 - (COLS * s - 1)) % NLON, 1)[:, :128]
        chunk = jnp.where(lane <= COLS, own, jnp.where(lane == COLS + 1, before, 0.0))
        send_ref[s, 0:KD, :] = chunk
        send_ref[s, KD:16, :] = jnp.zeros((16 - KD, 128), F32)
        send_ref[s, 16:24, :] = edge


def prepare(info, atmosphere, clouds, col):
    last = CELLS // 128 - 1
    return pl.pallas_call(
        prepare_kernel,
        grid_spec=pltpu.PrefetchScalarGridSpec(
            num_scalar_prefetch=1,
            grid=(1,),
            in_specs=[
                pl.BlockSpec((1, KD, NLON), lambda i, info: (info[0], 0, 0)),
                pl.BlockSpec((K, 128), lambda i, off: (0, 0)),
                pl.BlockSpec((K, 128), lambda i, off: (0, last)),
                pl.BlockSpec((1, 128), lambda i, off: (0, 0)),
                pl.BlockSpec((1, 128), lambda i, off: (0, last)),
            ],
            out_specs=pl.BlockSpec((SEGS, 24, 128), lambda i, off: (0, 0, 0)),
        ),
        out_shape=jax.ShapeDtypeStruct((SEGS, 24, 128), F32),
        name="prepare",
    )(info, atmosphere, clouds, clouds, col, col)


def column_of(row):
    size = row.shape[1]
    diagonal = lax.broadcasted_iota(jnp.int32, (size, size), 0) == lanes_of((size, size))
    return jnp.sum(jnp.where(diagonal, row, 0.0), axis=1, keepdims=True)


def pieces(source, target, sems, shift=0):
    return [
        pltpu.make_async_copy(
            source.at[:, i * CHUNK : (i + 1) * CHUNK],
            target.at[:, shift + i * CHUNK : shift + (i + 1) * CHUNK],
            sems.at[i],
        )
        for i in range(PIECES)
    ]


def inner_kernel(with_mean, *refs):
    if with_mean:
        c_hbm, col_ref, diff_ref, wind_ref, mixing_ref, base_hbm, mean_hbm, inv_ref = refs[:8]
        mean_ref, mean_sem = refs[8:10]
    else:
        c_hbm, diff_ref, wind_ref, mixing_ref, base_hbm = refs[:5]
    c_ref, base_ref, in_sems, out_sems = refs[-4:]
    reads = pieces(c_hbm, c_ref, in_sems)
    writes = pieces(base_ref, base_hbm, out_sems)
    for copy in reads:
        copy.start()
    zeros = jnp.zeros((K, 128), F32)
    mix = mixing_block(mixing_ref[...])
    diffusivity, wind = column_of(diff_ref[...]), column_of(wind_ref[...])
    total = jnp.zeros((2 * K + 16, 128), F32)
    reads[0].wait()
    for start in range(0, CELLS, TI):
        if start % CHUNK == 0 and start // CHUNK + 1 < PIECES:
            reads[start // CHUNK + 1].wait()
        window = c_ref[:, max(start - 128, 0) : min(start + TI + 128, CELLS)]
        if start == 0:
            window = jnp.concatenate([zeros, window], axis=1)
        if start + TI == CELLS:
            window = jnp.concatenate([window, zeros], axis=1)
        base_ref[:, start : start + TI] = substep_tile(window, mix, diffusivity, wind)
        if (start + TI) % CHUNK == 0:
            writes[start // CHUNK].start()
        if with_mean:
            hits = column_hits(col_ref[:, start : start + TI])
            high, low = split(window[:, 128 : 128 + TI])
            rows = jnp.concatenate([high, low, jnp.ones((16, TI), BF16)], axis=0)
            total = total + lax.dot_general(
                rows, hits, (((1,), (1,)), ((), ())), preferred_element_type=F32
            )
    if with_mean:
        counts = total[2 * K : 2 * K + 8]
        inv = jnp.where(counts > 0.0, 1.0 / jnp.maximum(counts, 1.0), 0.0)
        inv_ref[...] = inv
        mean_ref[...] = (total[:K] + total[K : 2 * K]) * inv[0:1]
        mean_write = pltpu.make_async_copy(mean_ref, mean_hbm, mean_sem)
        mean_write.start()
        mean_write.wait()
    for copy in writes:
        copy.wait()


VMEM_SPEC = pl.BlockSpec(memory_space=pltpu.VMEM)
HBM_SPEC = pl.BlockSpec(memory_space=pltpu.HBM)
MEAN_SCRATCH = [pltpu.VMEM((K, 128), F32), pltpu.SemaphoreType.DMA]


def in_hbm(x):
    return pltpu.with_memory_space_constraint(x, pltpu.HBM)


STATE_SCRATCH = [
    pltpu.VMEM((K, CELLS), F32),
    pltpu.VMEM((K, CELLS), F32),
    pltpu.SemaphoreType.DMA((PIECES,)),
    pltpu.SemaphoreType.DMA((PIECES,)),
]


def inner(clouds, col, diffusivity, wind, mixing, with_mean):
    args = [in_hbm(clouds)] + ([col] if with_mean else []) + [diffusivity, wind, mixing]
    shapes = [pltpu.HBM((K, CELLS), F32)]
    if with_mean:
        shapes += [pltpu.HBM((K, 128), F32), jax.ShapeDtypeStruct((8, 128), F32)]
    return pl.pallas_call(
        lambda *refs: inner_kernel(with_mean, *refs),
        in_specs=[HBM_SPEC] + [VMEM_SPEC] * (len(args) - 1),
        out_specs=([HBM_SPEC, HBM_SPEC, VMEM_SPEC] if with_mean else [HBM_SPEC]),
        out_shape=shapes,
        scratch_shapes=MEAN_SCRATCH * with_mean + STATE_SCRATCH,
        cost_estimate=pl.CostEstimate(flops=1 << 10, bytes_accessed=1 << 10, transcendentals=0),
        compiler_params=pltpu.CompilerParams(vmem_limit_bytes=10 << 20),
        name="inner",
    )(*args)


def outer_kernel(
    grouped, info, base_hbm, c_hbm, mean_hbm, prof_ref, halo_ref, inv_ref, col_ref, diff_ref, wind_ref,
    mixing_ref, out_hbm, end_hbm, send_ref, ext1, ext2, force, ends_ref, mean_ref, end_ref, small_sems,
    out_ref, in_sems, out_sems,
):
    seg = lax.axis_index("seg")
    reads = pieces(base_hbm, ext1, in_sems, 256)
    ends = [
        pltpu.make_async_copy(
            c_hbm.at[:, at : at + 256], ends_ref.at[:, 256 * i : 256 * i + 256], small_sems.at[i]
        )
        for i, at in enumerate((0, CELLS - 256))
    ]
    mean_read = pltpu.make_async_copy(mean_hbm, mean_ref, small_sems.at[2])
    mean_read.start()
    end_write = pltpu.make_async_copy(end_ref, end_hbm, small_sems.at[3])
    for copy in ends:
        copy.start()
    writes = pieces(out_ref, out_hbm, out_sems)
    for copy in reads:
        copy.start()
    lane = lanes_of((K, 128))
    zeros = jnp.zeros((K, 128), F32)
    mix = mixing_block(mixing_ref[...])
    diffusivity, wind = column_of(diff_ref[...]), column_of(wind_ref[...])

    from_left = halo_ref[lax.rem(seg + SEGS - 1, SEGS), 16:24, :]
    from_right = halo_ref[lax.rem(seg + 1, SEGS), 16:24, :]
    edges = jnp.concatenate([from_left, from_right, jnp.zeros((112, 128), F32)], axis=0).T[:K]
    left_tile = jnp.where(lane >= 125, pltpu.roll(edges, 122, 1), 0.0)
    right_tile = jnp.where(lane < 3, pltpu.roll(edges, 120, 1), 0.0)
    mean_read.wait()
    mean = mean_ref[...]
    mean_all = jnp.where(
        lane < COLS,
        mean,
        jnp.where(
            lane == COLS,
            pltpu.roll(edges, COLS - 14, 1),
            jnp.where(lane == COLS + 1, pltpu.roll(edges, COLS + 1 - 7, 1), 0.0),
        ),
    )
    profile = reorder(
        row_order(grouped, False), prof_ref[:, 0:16, :].reshape(SEGS * 16, 128)
    )
    pulled = jnp.where(lane < COLS + 2, RELAXATION * (profile - mean_all), 0.0)
    pulled = jnp.concatenate(split(pulled), axis=1)

    ext1[:, 0:128] = zeros
    ext1[:, EXT - 128 :] = zeros
    left_col = jnp.full((1, 128), COLS + 1, jnp.int32)
    right_col = jnp.full((1, 128), COLS, jnp.int32)
    for at in range(128, EXT - 128, TILE):
        cell = at - 256
        if cell < 0:
            col = jnp.concatenate([left_col, col_ref[:, 0:128]], axis=1)
        elif cell + TILE > CELLS:
            col = jnp.concatenate([col_ref[:, CELLS - 128 :], right_col], axis=1)
        else:
            col = col_ref[:, cell : cell + TILE]
        hits = column_hits(col)
        force[:, at : at + TILE] = jnp.dot(
            pulled, jnp.concatenate([hits, hits], axis=0), preferred_element_type=F32
        )

    for at in range(128, EXT - 128, TILE):
        cell = at - 256
        if (cell + 128) % CHUNK == 0 and (cell + 128) // CHUNK < PIECES:
            reads[(cell + 128) // CHUNK].wait()
        if cell < 0:
            ends[0].wait()
            window = jnp.concatenate([zeros, left_tile, ends_ref[:, 0:256]], axis=1)
            value = substep_tile(window, mix, diffusivity, wind)
        elif cell + TILE > CELLS:
            ends[1].wait()
            window = jnp.concatenate([ends_ref[:, 256:512], right_tile, zeros], axis=1)
            value = substep_tile(window, mix, diffusivity, wind)
        else:
            value = ext1[:, at : at + TILE]
        ext1[:, at : at + TILE] = value + force[:, at : at + TILE]

    for at in range(128, EXT - 128, T2):
        window = ext1[:, at - 128 : at + T2 + 128]
        ext2[:, at : at + T2] = (
            substep_tile(window, mix, diffusivity, wind) + force[:, at : at + T2]
        )

    total = jnp.zeros((2 * K, 128), F32)
    for cell in range(0, CELLS, T3):
        at = cell + 256
        window = ext2[:, at - 128 : at + T3 + 128]
        value = substep_tile(window, mix, diffusivity, wind) + force[:, at : at + T3]
        out_ref[:, cell : cell + T3] = value
        if (cell + T3) % CHUNK == 0:
            writes[cell // CHUNK].start()
        hits = column_hits(col_ref[:, cell : cell + T3])
        rows = jnp.concatenate(split(value), axis=0)
        total = total + lax.dot_general(
            rows, hits, (((1,), (1,)), ((), ())), preferred_element_type=F32
        )
    end = (total[:K] + total[K:]) * inv_ref[0:1]
    end_ref[...] = end
    end_write.start()
    tendency = jnp.where(lane < COLS, end - mean, 0.0)
    sent = reorder(row_order(True, True), tendency)
    edge = edge_rows(
        out_ref[:, 0:128], out_ref[:, CELLS - 128 :], end[:, 0:1], end[:, COLS - 1 : COLS]
    )
    for s in range(send_ref.shape[0]):
        send_ref[s, 0:16, :] = sent[16 * (s % SEGS) : 16 * (s % SEGS) + 16]
        send_ref[s, 16:24, :] = edge
    end_write.wait()
    for copy in writes:
        copy.wait()


def outer(grouped, info, base, clouds, mean, *args):
    return call(
        lambda *refs: outer_kernel(grouped, *refs), "outer",
        (in_hbm(base), in_hbm(clouds), in_hbm(mean), *args),
        [pltpu.HBM((K, CELLS), F32), pltpu.HBM((K, 128), F32), shape(SEGS, 24, 128)],
        scratch=[pltpu.VMEM((K, EXT), F32)] * 3
        + [pltpu.VMEM((K, 512), F32), pltpu.VMEM((K, 128), F32), pltpu.VMEM((K, 128), F32)]
        + [pltpu.SemaphoreType.DMA((4,))]
        + STATE_SCRATCH[1:],
        prefetch=info, limit=16, hbm=(3, 2),
    )


def upper(shape):
    return lax.broadcasted_iota(jnp.int32, shape, len(shape) - 2) % 8 < 4


def swap4(x):
    tiles = x.reshape(-1, 8, x.shape[-1])
    return pltpu.roll(tiles, 4, 1).reshape(x.shape)


def dot3(x, table):
    high, low = split(x)
    rows = x.shape[0]
    both = jnp.dot(jnp.concatenate([high, low], axis=0), table[0], preferred_element_type=F32)
    return both[:rows] + both[rows:] + jnp.dot(high, table[1], preferred_element_type=F32)


def dot3_left(table, x):
    high, low = split(x)
    cols = x.shape[1]
    both = jnp.dot(table[0], jnp.concatenate([high, low], axis=1), preferred_element_type=F32)
    return both[:, :cols] + both[:, cols:] + jnp.dot(table[1], high, preferred_element_type=F32)


def received_rows(chunks, table):
    rows = jnp.concatenate(
        [jnp.concatenate([c[s] for s in range(SEGS)], axis=1) for c in chunks], axis=0
    )
    coeffs = dot3(rows, table)
    out = []
    first = upper((8, M))
    for a in range(len(chunks)):
        c = [coeffs[16 * a + 8 * i : 16 * a + 8 * i + 8, :M] for i in range(2)]
        s = [coeffs[16 * a + 8 * i : 16 * a + 8 * i + 8, M:] for i in range(2)]
        out.append(
            [
                jnp.where(first, c[0], swap4(s[0])),
                jnp.where(first, swap4(c[0]), s[0]),
                jnp.where(first, c[1], swap4(s[1])),
            ]
        )
    return out


def weigh(total, factors, rows):
    vort, mix, turn = factors[:, :M], factors[:, M : 2 * M], factors[:, 2 * M :]
    return [
        total[0] + vort * rows[0],
        total[1] + (mix * rows[1] + turn * rows[2]),
        total[2] + (mix * rows[2] - turn * rows[1]),
    ]


def call(kernel, name, args, shapes, scratch=(), prefetch=None, limit=8, hbm=(0, 0)):
    specs = [VMEM_SPEC] * len(args)
    common = dict(
        out_shape=shapes,
        name=name,
        cost_estimate=pl.CostEstimate(flops=1 << 10, bytes_accessed=1 << 10, transcendentals=0),
        compiler_params=pltpu.CompilerParams(vmem_limit_bytes=limit << 20),
    )
    outs = [VMEM_SPEC] * len(shapes)
    specs[: hbm[0]] = [HBM_SPEC] * hbm[0]
    outs[: hbm[1]] = [HBM_SPEC] * hbm[1]
    if prefetch is None:
        return pl.pallas_call(
            kernel, in_specs=specs, out_specs=outs, scratch_shapes=list(scratch), **common
        )(*args)
    return pl.pallas_call(
        kernel,
        grid_spec=pltpu.PrefetchScalarGridSpec(
            num_scalar_prefetch=1, grid=(), in_specs=specs, out_specs=outs,
            scratch_shapes=list(scratch),
        ),
        **common,
    )(prefetch, *args)


def rows_kernel(grid_ref, table, rows_ref, lines):
    for v in range(3):
        for j in range(LAT_DEV):
            for l in range(4):
                at = v * 48 + 4 * j + l
                lines[at : at + 1, :] = grid_ref[j, 3 * l + v : 3 * l + v + 1, :]
    coeffs = dot3(lines[...], table)
    cos, sin = coeffs[:, :M], coeffs[:, M:]
    first = upper((144, M))
    even = jnp.where(first, cos, swap4(sin))
    odd = jnp.where(first, swap4(cos), sin)
    for v in range(3):
        for i in range(6):
            at = v * 48 + 8 * i
            rows_ref[v, 2 * i] = even[at : at + 8]
            rows_ref[v, 2 * i + 1] = odd[at : at + 8]
        for j in range(LAT_DEV, 16):
            rows_ref[v, j] = jnp.zeros((8, M), F32)


def spread_kernel(info, got_ref, table, rows_ref, send_ref, held):
    offset = place(info)[2]
    forced = received_rows([got_ref[:, 0:16, :]], table)[0]
    for h in range(2):
        held[h] = rows_ref[:, :, :, 128 * h : 128 * h + 128].reshape(384, 128)
        for v in range(3):
            at = pl.ds(pl.multiple_of((v * 16 + offset) * 8, 8), 8)
            held[h, at, :] += forced[v][:, 128 * h : 128 * h + 128]
        held[h, LAT_DEV * 8 : LAT_DEV * 8 + 8, :] = jnp.full((8, 128), offset, jnp.int32).astype(F32)
    for u in range(8):
        for h in range(2):
            send_ref[2 * u + h] = held[h, pl.ds(u, 48, stride=8), :]


def channel_basis(spec_ref, table):
    offsets = spec_ref[:, LAT_DEV, :][:, 0:1].astype(jnp.int32)
    wanted = 16 * lax.broadcasted_iota(jnp.int32, (16, 256), 0) + offsets
    picks = jnp.where(lanes_of((16, 256)) == wanted, 1.0, 0.0).astype(BF16)
    return [jnp.dot(picks, t, preferred_element_type=F32) for t in table]


def weights_kernel(info, mine_ref, others_ref, from_spec, row_weights, out_ref):
    core, chip, _ = place(info)
    own = pl.ds(pl.multiple_of(chip * 16, 16), 16)
    here = from_spec[0, core, own, :].astype(F32) + from_spec[1, core, own, :].astype(F32)
    for half, ref, side in ((0, mine_ref, core), (16, others_ref, 1 - core)):
        high, low = channel_basis(ref, [from_spec[0, side], from_spec[1, side]])
        basis = high + low
        products = jnp.concatenate([basis[c : c + 1] * here for c in range(16)], axis=0)
        out_ref[half : half + 16] = dot3(products, row_weights).reshape(16, 16, 3 * M)


def settle_kernel(info, mine_ref, others_ref, to_spec, from_spec, once, twice, out_ref):
    core, chip, _ = place(info)
    half = lax.rem(chip, 2)

    def columns(ref):
        return jnp.concatenate(
            [ref[:, 16 * v : 16 * v + 16, :].reshape(256, 128) for v in range(3)], axis=1
        )

    def update(factors, spec):
        vort, div, geo = spec[:, :128], spec[:, 128:256], spec[:, 256:]
        f0, f1, f2 = factors[half, 0], factors[half, 1], factors[half, 2]
        return jnp.concatenate([f0 * vort, f1 * div + f2 * geo, f1 * geo - f2 * div], axis=1)

    spec = dot3_left([to_spec[0, core], to_spec[1, core]], columns(mine_ref)) + dot3_left(
        [to_spec[0, 1 - core], to_spec[1, 1 - core]], columns(others_ref)
    )
    table = [from_spec[0, core], from_spec[1, core]]
    back = dot3_left(table, update(twice, spec))
    channels = dot3_left(
        [t.astype(BF16) for t in channel_basis(mine_ref, table)], update(once, spec)
    )
    for v in range(3):
        out_ref[:, 16 * v : 16 * v + 16, :] = back[:, 128 * v : 128 * v + 128].reshape(16, 16, 128)
        for q in range(16):
            out_ref[q, 16 * v + LAT_DEV : 16 * v + LAT_DEV + 1, :] = channels[
                q : q + 1, 128 * v : 128 * v + 128
            ]


def profile_kernel(got_ref, table, out_ref, total):
    for v in range(3):
        for u in range(8):
            for h in range(2):
                at = 16 * v + LAT_DEV
                total[8 * v + u : 8 * v + u + 1, 128 * h : 128 * h + 128] = got_ref[
                    2 * u + h, at : at + 1, :
                ]
    a, b, c = total[0:8], total[8:16], total[16:24]
    first = upper((8, M))
    cos = jnp.concatenate([jnp.where(first, a, swap4(b)), c], axis=0)
    sin = jnp.concatenate([jnp.where(first, swap4(a), b), swap4(c)], axis=0)
    lines = dot3(jnp.concatenate([cos, sin], axis=1), table)
    for s in range(SEGS):
        out_ref[s] = lines[:, 128 * s : 128 * s + 128]


def last_kernel(got_ref, table, out_ref):
    rows = received_rows([got_ref[:, 0:16, :]], table)[0]
    line = jnp.concatenate(rows, axis=0)
    for c in range(16):
        out_ref[c] = line


def add_channels(factors, half, from_ref, held):
    def row_pair(i, _):
        for h in range(2):
            j = 2 * i + h
            total = [held[v, j] for v in range(3)]
            for c in range(16):
                total = weigh(
                    total,
                    factors[c + half, pl.ds(j, 1), :],
                    [from_ref[c, 8 * v : 8 * v + 8, :] for v in range(3)],
                )
            for v in range(3):
                held[v, j] = total[v]
        return 0

    lax.fori_loop(0, LAT_DEV // 2, row_pair, 0)


def gather_kernel(got_ref, factors, from_ref, held, flat):
    for u in range(8):
        for h in range(2):
            flat[h, pl.ds(u, 48, stride=8), :] = got_ref[2 * u + h]
    for h in range(2):
        held[:, :, :, 128 * h : 128 * h + 128] = flat[h].reshape(3, 16, 8, 128)
    add_channels(factors, 0, from_ref, held)


def finish_kernel(part_ref, factors, from_ref, table, out_ref, held):
    held[...] = part_ref[...]
    add_channels(factors, 16, from_ref, held)
    first = upper((8, M))
    cos, sin = [], []
    for v in range(3):
        for i in range(6):
            even, odd = held[v, 2 * i], held[v, 2 * i + 1]
            cos.append(jnp.where(first, even, swap4(odd)))
            sin.append(jnp.where(first, swap4(even), odd))
    rows = jnp.concatenate(
        [jnp.concatenate(cos, axis=0), jnp.concatenate(sin, axis=0)], axis=1
    )
    lines = dot3(rows, table)
    for v in range(3):
        for j in range(LAT_DEV):
            for l in range(4):
                at = v * 48 + 4 * j + l
                out_ref[j, 3 * l + v : 3 * l + v + 1, :] = lines[at : at + 1]


def shape(*dims):
    return jax.ShapeDtypeStruct(dims, F32)


def rows_exchange(x):
    return lax.all_to_all(x, "lat", 0, 0, axis_index_groups=ROW_GROUPS, tiled=True)


def core_swap(x):
    return lax.ppermute(x, "lat", CORE_SWAP)


def shards(atmosphere, cloud_state, channel_lat, cell_column, channel_wind, diffusivity, mixing):
    tab = {name: jnp.asarray(value) for name, value in tables().items()}
    lat = lax.axis_index("lat").astype(jnp.int32)
    info = channel_lat - lat * LAT_DEV
    clouds = cloud_state[0]
    col = cell_column
    wind = channel_wind
    diff = diffusivity.reshape(1, K)
    spread_table = tab["forward_seg"]

    send = prepare(info, atmosphere, clouds, col)
    got = lax.all_to_all(send, "seg", 0, 0, tiled=True)
    grid, state, send = lax.optimization_barrier((atmosphere, clouds, send))
    base, mean, inv = inner(state, col, diff, wind, mixing, True)
    rows = call(
        rows_kernel, "rows", (grid, tab["forward"]), [shape(3, 16, 8, M)],
        scratch=[pltpu.VMEM((144, NLON), F32)],
    )[0]
    rows, got = lax.optimization_barrier((rows, got))
    clouds, mean_1, send = outer(
        False, info, base, state, mean, got, got, inv, col, diff, wind, mixing,
    )
    halo = lax.all_to_all(send, "seg", 0, 0, tiled=True)
    base = inner(clouds, col, diff, wind, mixing, False)[0]
    base, halo = lax.optimization_barrier((base, halo))

    spread = call(
        spread_kernel, "spread", (halo, spread_table, rows), [shape(16, 48, 128)],
        scratch=[pltpu.VMEM((2, 384, 128), F32)], prefetch=info,
    )[0]
    spec_mine = rows_exchange(spread)
    spec_others = core_swap(spec_mine)
    settled = call(
        settle_kernel, "settle",
        (spec_mine, spec_others, tab["to_spec"], tab["from_spec"], tab["once"], tab["twice"]),
        [shape(16, 48, 128)], prefetch=info,
    )[0]
    settled = rows_exchange(settled)
    profile = call(
        profile_kernel, "profile", (settled, tab["inverse_seg"]), [shape(SEGS, 16, 128)],
        scratch=[pltpu.VMEM((24, M), F32)],
    )[0]
    profile, spec_mine, spec_others = lax.optimization_barrier((profile, spec_mine, spec_others))
    factors = call(
        weights_kernel, "weights", (spec_mine, spec_others, tab["from_spec"], tab["row_weights"]),
        [shape(32, 16, 3 * M)], prefetch=info,
    )[0]
    profile = lax.all_to_all(profile, "seg", 0, 0, tiled=True)

    factors, profile = lax.optimization_barrier((factors, profile))

    clouds, _, send = outer(
        True, info, base, clouds, mean_1, profile, halo, inv, col, diff, wind, mixing,
    )
    got = lax.all_to_all(send, "seg", 0, 0, tiled=True)
    from_mine = rows_exchange(
        call(last_kernel, "last", (got, spread_table), [shape(16, 24, M)])[0]
    )
    from_others = core_swap(from_mine)
    part = call(
        gather_kernel, "gather", (settled, factors, from_mine), [shape(3, 16, 8, M)],
        scratch=[pltpu.VMEM((2, 384, 128), F32)],
    )[0]
    grid = call(
        finish_kernel, "finish", (part, factors, from_others, tab["inverse"]),
        [shape(LAT_DEV, KD, NLON)], scratch=[pltpu.VMEM((3, 16, 8, M), F32)],
    )[0]
    return grid, clouds[None]


def solution(mesh):
    placed = (
        P("lat", "seg", None),
        P("lat", None, "seg"),
        P("lat"),
        P("lat", "seg"),
        P("lat", None),
        P(),
        P(),
    )
    return jax.shard_map(
        shards,
        mesh=mesh,
        in_specs=placed,
        out_specs=(P("lat", "seg", None), P("lat", None, "seg")),
        check_vma=False,
    )
```
